32 devices in a mesh: ctx: 4 (over z), tp: 4 (over y, x), dp: 2 (over core).
Axes of the slice: x: 2, y: 2, z: 4, core: 2. Of those that a mesh axis runs over, the one named last changes fastest.
Arguments:
- projected: bfloat16 [3, 2, 1024, 1024], P(None, 'dp', 'ctx', 'tp'), may hold values from -6 to 6
- segment_ids: int32 [2, 1024], P('dp', 'ctx'), may hold values from 0 to 1, never falling along the last dimension, each value on 1 to 768 neighbouring positions
- short_filter: float32 [3, 3, 1024], P(None, None, 'tp'), may hold values from -3.5 to 3.5
- long_filter: float32 [64, 1024], P('tp', 'ctx'), may hold values from -4 to 4
- out_proj: bfloat16 [1024, 1024], P('tp'), may hold values from -0.1875 to 0.1875
- mixed_cotangent: bfloat16 [2, 1024, 1024], P('dp', 'ctx', 'tp'), may hold values from -6 to 6
Outputs:
- mixed: bfloat16 [2, 1024, 1024], P('dp', 'ctx', 'tp')
- grad_projected: bfloat16 [3, 2, 1024, 1024], P(None, 'dp', 'ctx', 'tp')
- grad_short: float32 [3, 3, 1024], P(None, None, 'tp')
- grad_long: float32 [64, 1024], P('tp', 'ctx')
- grad_out_proj: float32 [1024, 1024], P('tp')
The draws below stay inside these ranges and needn't reach their ends.
Inputs may be any that keep to these rules, and one draw needn't show every extreme that they name: `segment_ids`: along each window the id never falls; every id covers 1 to 768 consecutive positions, and one covers exactly 768.
All inputs are finite; a program needn't handle non-finite values.
Results may differ from the reference program's by a relative error of at most 0.0049.
Values may be sent and summed in bfloat16 or wider, within the bound.
No kernel may reach another device: no remote copies, remote signals or barrier semaphores. Data moves between devices by JAX's collectives and lax.ppermute only.
A program may use at most 64 MiB of HBM per device.

```python
import math
import jax
import jax.numpy as jnp
import numpy as np
from jax import lax

CH = 1024
GROUP = 16
SHORT = 3
LEN_DEV = 256
PACKED_SPAN = 1024
SEQS = 2
KERNEL_SETS = 64
DOCS = 2


def draw_long_filter(key, part):
    fraction_seed_handle, jitter_seed_handle, cluster_seed_handle = jax.random.split(jax.random.fold_in(key, 17), 3)
    removal_sites = jnp.arange(PACKED_SPAN, dtype=jnp.float32)[None, :]
    rates = jnp.exp(jax.random.uniform(fraction_seed_handle, (KERNEL_SETS, 1), jnp.float32, math.log(0.5 / PACKED_SPAN), math.log(1.0 / 30.0)))
    noise = jnp.clip(jax.random.normal(jitter_seed_handle, (KERNEL_SETS, PACKED_SPAN), jnp.float32), -4.0, 4.0)
    scaling = jnp.sqrt((1.0 - jnp.exp(-2.0 * rates)) / (1.0 - jnp.exp(-2.0 * rates * PACKED_SPAN)))
    cluster_extents = jax.random.randint(cluster_seed_handle, (3, KERNEL_SETS, 1), 0, PACKED_SPAN).astype(jnp.float32)
    removed_symbols = jnp.prod(jnp.where(removal_sites[None] >= cluster_extents, 0.65, 1.0), axis=0)
    return (scaling * jnp.exp(-rates * removal_sites) * removed_symbols * noise).astype(jnp.float32)


def level_of(key, dims, shards, least, top_value):
    factor_of = 1.0
    for axis_at, shards_of in shards:
        heights = jax.random.uniform(jax.random.fold_in(jax.random.fold_in(key, 6), axis_at), (shards_of,), jnp.float32, least / len(shards), top_value / len(shards))
        factor_of = factor_of * jnp.repeat(jnp.exp(heights), dims[axis_at] // shards_of).reshape((-1,) + (1,) * (len(dims) - 1 - axis_at))
    return factor_of


def split_up(number_of, total, bound, skew):
    loads = [(1 << 20) // math.isqrt(grade ** skew) + 1 for grade in range(2, number_of + 1)]
    spare, counts = total - bound - (number_of - 1), [1] * (number_of - 1)
    while spare > 0:
        candidates = [i for i in range(number_of - 1) if counts[i] < bound]
        pool, remaining = sum([loads[i] for i in candidates]), spare
        for i in candidates:
            addition = min(bound - counts[i], max(1, remaining * loads[i] // pool), spare)
            counts[i] = counts[i] + addition
            spare = spare - addition
    return np.array([bound] + counts)


def ragged_sizes(own_key, number_of, total, bound, lean):
    if number_of == 2:
        one = jax.random.randint(own_key, (), max(1, total - bound), min(bound, total - 1) + 1)
        return jnp.stack([one, total - one])
    tallies = jnp.asarray(split_up(number_of, total, bound, lean), jnp.int32)
    pairs = (number_of - 1) // 2
    donor, sink = tallies[1:1 + 2 * pairs:2], tallies[2:2 + 2 * pairs:2]
    room = jnp.minimum(donor - 1, bound - sink)
    shifted = jax.random.randint(jax.random.fold_in(own_key, 1), (pairs,), 0, 1 << 20) % (room + 1)
    tallies = tallies.at[1:1 + 2 * pairs:2].set(donor - shifted).at[2:2 + 2 * pairs:2].set(sink + shifted)
    return tallies[jax.random.permutation(jax.random.fold_in(own_key, 2), number_of)]


def normal_values(rng, shape, spread, limit, pieces=(), kind=jnp.bfloat16):
    result = spread * jax.random.normal(rng, shape, jnp.float32)
    if pieces:
        result = result * level_of(rng, shape, pieces, -0.22, 0.18)
    return jnp.clip(result, -limit, limit).astype(kind)


def setup_inputs(seed: int = 0) -> dict:
    keys = jax.random.split(jax.random.key(seed), 7)
    return {
        "projected": normal_values(keys[0], (3, SEQS, PACKED_SPAN, CH), 1.0, 6.0, ((1, 2), (2, 4), (3, 4))),
        "segment_ids": jax.vmap(lambda own: jnp.searchsorted(jnp.cumsum(ragged_sizes(own, DOCS, PACKED_SPAN, 3 * LEN_DEV, 0)), jnp.arange(PACKED_SPAN), side="right"))(jax.random.split(keys[1], SEQS)).reshape((SEQS, PACKED_SPAN)).astype(jnp.int32),
        "short_filter": normal_values(keys[2], (3, SHORT, CH), SHORT ** -0.5, 3.5, ((2, 4),), jnp.float32),
        "long_filter": draw_long_filter(jax.random.fold_in(keys[6], 71), 0),
        "out_proj": normal_values(keys[4], (CH, CH), CH ** -0.5, 0.1875, ((0, 4),)),
        "mixed_cotangent": normal_values(keys[5], (SEQS, PACKED_SPAN, CH), 1.0, 6.0, ((0, 2), (1, 4), (2, 4))),
    }


def tap_mask(segments, shift_by):
    length = segments.shape[1]
    removal_sites = jnp.arange(length, dtype=jnp.int32)
    earlier = jnp.roll(segments, shift_by, axis=1)
    return jnp.where((removal_sites >= shift_by)[None, :] & (earlier == segments), 1.0, 0.0).astype(jnp.float32)

def short_forward(inputs, filters, segments):
    running = jnp.zeros_like(inputs)
    for shift_by in range(filters.shape[1]):
        valid_mask = tap_mask(segments, shift_by)
        running = running + filters[:, shift_by][:, None, None, :] * valid_mask[None, :, :, None] * jnp.roll(inputs, shift_by, axis=2)
    return running

def short_backward(inputs, filters, segments, cotangent):
    pulled = jnp.zeros_like(cotangent)
    tap_rows = []
    for shift_by in range(filters.shape[1]):
        masked = cotangent * tap_mask(segments, shift_by)[None, :, :, None]
        pulled = pulled + filters[:, shift_by][:, None, None, :] * jnp.roll(masked, -shift_by, axis=2)
        tap_rows.append(lax.optimization_barrier(jnp.sum(masked * jnp.roll(inputs, shift_by, axis=2), axis=(1, 2))))
    return (pulled, jnp.stack(tap_rows, axis=1))

def reference(projected, segment_ids, short_filter, long_filter, out_proj, mixed_cotangent):
    grad_scale = 1.0 / math.sqrt(SEQS * PACKED_SPAN)
    inputs = projected.astype(jnp.float32)
    short_out = short_forward(inputs, short_filter, segment_ids)
    gated_rows = short_out[1] * short_out[2]
    fft_length = 2 * PACKED_SPAN
    mid_spec = jnp.fft.rfft(gated_rows, n=fft_length, axis=1)
    filt_spec = jnp.fft.rfft(jnp.repeat(long_filter.T, GROUP, axis=1), n=fft_length, axis=0)
    long_out = jnp.fft.irfft(mid_spec * filt_spec[None], n=fft_length, axis=1)[:, :PACKED_SPAN]
    y_out = (short_out[0] * long_out).astype(jnp.bfloat16)
    flat_y = y_out.reshape(SEQS * PACKED_SPAN, CH)
    flat_cot = mixed_cotangent.reshape(SEQS * PACKED_SPAN, CH)
    mixed = jnp.dot(flat_y, out_proj, preferred_element_type=jnp.float32).astype(jnp.bfloat16).reshape(SEQS, PACKED_SPAN, CH)
    grad_y = jnp.dot(flat_cot, out_proj.T, preferred_element_type=jnp.float32).reshape(SEQS, PACKED_SPAN, CH)
    grad_out_proj = jnp.dot(flat_y.T, flat_cot, preferred_element_type=jnp.float32) * grad_scale
    grad_long_out = grad_y * short_out[0]
    grad_query = grad_y * long_out
    cot_spec = jnp.fft.rfft(grad_long_out, n=fft_length, axis=1)
    grad_gated = jnp.fft.irfft(jnp.conj(filt_spec)[None] * cot_spec, n=fft_length, axis=1)[:, :PACKED_SPAN]
    cross_spec = lax.optimization_barrier(jnp.sum(jnp.conj(mid_spec) * cot_spec, axis=0)).reshape(PACKED_SPAN + 1, KERNEL_SETS, GROUP).sum(axis=2)
    grad_long = jnp.fft.irfft(cross_spec, n=fft_length, axis=0)[:PACKED_SPAN].T * grad_scale
    grad_short_out = jnp.stack([grad_query, grad_gated * short_out[2], grad_gated * short_out[1]])
    grad_inputs, tap_sums = short_backward(inputs, short_filter, segment_ids, grad_short_out)
    return (mixed, grad_inputs.astype(jnp.bfloat16), tap_sums * grad_scale, grad_long, grad_out_proj)
```

```python
import functools
import math

import jax
import jax.numpy as jnp
from jax import lax
from jax.experimental import pallas as pl
from jax.experimental.pallas import tpu as pltpu
from jax.sharding import PartitionSpec as P

highest_precision = lax.Precision.HIGHEST


def shifted(value, axis, steps):
    count = lax.axis_size(axis)
    first, last = (max(0, -steps), min(count, count - steps))
    return lax.ppermute(value, axis, [(source, source + steps) for source in range(first, last)])


def angle_table(height, breadth, period, direction):
    product = (
        jnp.arange(height, dtype=jnp.int32)[:, None]
        * jnp.arange(breadth, dtype=jnp.int32)[None, :]
        % period
    )
    angles = direction * 2.0 * math.pi / period * product.astype(jnp.float32)
    return (jnp.cos(angles), jnp.sin(angles))


def row_twiddle(spec_re, spec_im, direction):
    my_index = lax.axis_index("ctx")
    devices = lax.axis_size("ctx")
    row_count = spec_re.shape[1]
    period = 2 * devices * row_count
    freq_pair = 2 * my_index + jnp.arange(2, dtype=jnp.int32)
    product = freq_pair[:, None] * jnp.arange(row_count, dtype=jnp.int32)[None, :] % period
    angles = direction * 2.0 * math.pi / period * product.astype(jnp.float32)
    cosine = jnp.cos(angles)[:, :, None]
    sine_part = jnp.sin(angles)[:, :, None]
    return (spec_re * cosine - spec_im * sine_part, spec_re * sine_part + spec_im * cosine)


def row_transform(spec_re, spec_im, direction):
    row_count = spec_re.shape[1]
    cosine, sine_part = angle_table(row_count, row_count, row_count, direction)

    def along_rows(blocks, matrix):
        return jnp.einsum("kmc,mq->kqc", blocks, matrix, precision=highest_precision)

    return (
        along_rows(spec_re, cosine) - along_rows(spec_im, sine_part),
        along_rows(spec_re, sine_part) + along_rows(spec_im, cosine),
    )


def mixing(matrix, blocks):
    return jnp.einsum("kj,jmc->kmc", matrix, blocks, precision=highest_precision)


def forward_spectrum(real_part):
    devices = lax.axis_size("ctx")
    cosine, sine_part = angle_table(2 * devices, devices, 2 * devices, -1.0)
    spread_re = lax.all_to_all(real_part[None], "ctx", split_axis=1, concat_axis=0, tiled=True)
    column_re = mixing(cosine, spread_re)
    column_im = mixing(sine_part, spread_re)
    near_re, near_im = (
        lax.all_to_all(column_re, "ctx", split_axis=0, concat_axis=1, tiled=True),
        lax.all_to_all(column_im, "ctx", split_axis=0, concat_axis=1, tiled=True),
    )
    twist_re, twist_im = row_twiddle(near_re, near_im, -1.0)
    return row_transform(twist_re, twist_im, -1.0)


def inverse_spectrum(spec_re, spec_im):
    devices = lax.axis_size("ctx")
    row_count = spec_re.shape[1]
    back_re, back_im = row_transform(spec_re, spec_im, 1.0)
    twist_re, twist_im = row_twiddle(back_re / row_count, back_im / row_count, 1.0)
    far_re, far_im = (
        lax.all_to_all(twist_re, "ctx", split_axis=1, concat_axis=0, tiled=True),
        lax.all_to_all(twist_im, "ctx", split_axis=1, concat_axis=0, tiled=True),
    )
    cosine, sine_part = angle_table(devices, 2 * devices, 2 * devices, 1.0)
    out_re = (mixing(cosine, far_re) - mixing(sine_part, far_im)) / (2 * devices)
    rows_re = lax.all_to_all(out_re, "ctx", split_axis=0, concat_axis=1, tiled=True)
    return (rows_re[0], rows_re[0])


def pack_columns(values):
    return (values, values)


def by_filter(val_re, val_im, fil_re, fil_im, conjugate):
    val_shape = val_re.shape
    group_count = fil_re.shape[2]
    v_re = val_re.reshape(val_shape[0], val_shape[1], group_count, -1)
    v_im = val_im.reshape(val_shape[0], val_shape[1], group_count, -1)
    f_re = fil_re[:, :, :, None]
    f_im = fil_im[:, :, :, None]
    if conjugate:
        f_im = -f_im
    out_re = v_re * f_re - v_im * f_im
    out_im = v_re * f_im + v_im * f_re
    return (out_re.reshape(val_shape), out_im.reshape(val_shape))


def short_local(extended, filters, seg_ext):
    reach_taps = filters.shape[1]
    out_rows = extended.shape[1] - reach_taps + 1
    own_seg = seg_ext[reach_taps - 1 :]
    running = jnp.zeros((extended.shape[0], out_rows, extended.shape[2]), jnp.float32)
    for shift_by in range(reach_taps):
        start_row = reach_taps - 1 - shift_by
        same_doc = jnp.where(seg_ext[start_row : start_row + out_rows] == own_seg, 1.0, 0.0)
        running = (
            running
            + filters[:, shift_by][:, None, :]
            * same_doc[None, :, None]
            * extended[:, start_row : start_row + out_rows]
        )
    return running


def spectral_device(projected, segment_ids, short_filter, long_filter, out_proj, mixed_cotangent):
    row_count = projected.shape[2]
    stacked = projected.shape[0]
    width_dev = projected.shape[3]
    short_reach = short_filter.shape[1]
    group_count = long_filter.shape[0]
    grad_scale = 1.0 / math.sqrt(
        projected.shape[1] * lax.axis_size("dp") * row_count * lax.axis_size("ctx")
    )
    segments = segment_ids[0]
    source = projected[:, 0]
    short_rows = short_reach - 1
    cot_full = lax.all_gather(mixed_cotangent[0], "tp", axis=1, tiled=True)
    prev_tail, prev_seg = shifted(
        (source[:, row_count - short_rows :], segments[row_count - short_rows :]), "ctx", 1
    )
    short_seg = jnp.concatenate([prev_seg, segments])
    short_ext = jnp.concatenate([prev_tail, source], axis=1).astype(jnp.float32)

    def short_piece(extended, filters):
        return short_local(extended, filters, short_seg)

    short_out, short_pull = jax.vjp(short_piece, short_ext, short_filter)
    query_conv = short_out[0]
    gated_rows = short_out[1] * short_out[2]
    filter_cols = long_filter.T
    mid_re, mid_im = pack_columns(gated_rows)
    spec_re, spec_im = forward_spectrum(jnp.concatenate([mid_re, filter_cols], axis=1))
    data_cols = spec_re.shape[2] - group_count
    signal_re = spec_re[:, :, :data_cols]
    signal_im = spec_im[:, :, :data_cols]
    filt_re = spec_re[:, :, data_cols:]
    filt_im = spec_im[:, :, data_cols:]
    long_re, long_im = by_filter(signal_re, signal_im, filt_re, filt_im, False)
    out_re, out_im = inverse_spectrum(long_re, long_im)
    y_out = (query_conv * out_re).astype(jnp.bfloat16)
    partial_out = jnp.dot(y_out, out_proj, preferred_element_type=jnp.float32)
    mixed = lax.psum_scatter(partial_out, "tp", scatter_dimension=1, tiled=True).astype(
        jnp.bfloat16
    )
    grad_y = jnp.dot(cot_full, out_proj.T, preferred_element_type=jnp.float32)
    grad_proj_local = jnp.dot(y_out.T, cot_full, preferred_element_type=jnp.float32)
    grad_long_out = grad_y * query_conv
    grad_query = grad_y * out_re
    grad_in_re, grad_in_im = pack_columns(grad_long_out)
    cot_re, cot_im = forward_spectrum(grad_in_re)
    back_re, back_im = by_filter(cot_re, cot_im, filt_re, filt_im, True)
    cross_re = (
        (signal_re * cot_re + signal_im * cot_im).reshape(2, row_count, group_count, -1).sum(axis=3)
    )
    cross_im = (
        (signal_re * cot_im - signal_im * cot_re).reshape(2, row_count, group_count, -1).sum(axis=3)
    )
    inv_re, inv_im = inverse_spectrum(
        jnp.concatenate([back_re, cross_re], axis=2), jnp.concatenate([back_im, cross_im], axis=2)
    )
    grad_gated = inv_re[:, :data_cols]
    grad_long_local = inv_re[:, data_cols:].T
    grad_short_out = jnp.stack([grad_query, grad_gated * short_out[2], grad_gated * short_out[1]])
    grad_short_ext, grad_short_local = short_pull(grad_short_out)
    returned_short = shifted(grad_short_ext[:, :short_rows], "ctx", -1)
    grad_source = grad_short_ext[:, short_rows:] + jnp.concatenate(
        [jnp.zeros((stacked, row_count - short_rows, width_dev), jnp.float32), returned_short],
        axis=1,
    )
    total_proj, total_short = lax.psum((grad_proj_local, grad_short_local), ("ctx", "dp"))
    total_long = lax.psum(grad_long_local, "dp")
    return (
        mixed[None],
        grad_source[:, None].astype(jnp.bfloat16),
        total_short * grad_scale,
        total_long * grad_scale,
        total_proj * grad_scale,
    )


bf16 = jnp.bfloat16
f32 = jnp.float32
SUB = 128


def split_bf16(value):
    high = value.astype(bf16)
    return high, (value - high.astype(f32)).astype(bf16)


def rotate(value, axis, steps):
    count = lax.axis_size(axis)
    return lax.ppermute(value, axis, [(i, (i + steps) % count) for i in range(count)])


def scatter_chunks(chunks, axis):
    return [chunks[0]] + [rotate(chunks[s], axis, s) for s in range(1, len(chunks))]


def spread(value, axis):
    return [value] + [rotate(value, axis, s) for s in range(1, lax.axis_size(axis))]


def on_core(kernel, outs, args, name, scratch=(), flops=0):
    moved = sum(a.size * a.dtype.itemsize for a in args)
    moved += sum(math.prod(shape) * jnp.dtype(kind).itemsize for shape, kind in outs)
    return pl.pallas_call(
        kernel,
        out_shape=[jax.ShapeDtypeStruct(shape, kind) for shape, kind in outs],
        scratch_shapes=list(scratch),
        compiler_params=pltpu.CompilerParams(vmem_limit_bytes=48 * 1024 * 1024),
        cost_estimate=pl.CostEstimate(flops=flops, bytes_accessed=moved, transcendentals=0),
        name=name,
    )(*args)


def block_at(index, size):
    return pl.ds(pl.multiple_of(index * size, size), size)


def pack_signal_kernel(devices, projected, filters, segments, *rest):
    outs, (turned, small) = rest[:devices], rest[devices:]
    me = lax.axis_index("ctx")
    stacked, _, width = projected.shape
    chunk = width // devices
    groups = filters.shape[0] // devices
    for i in range(stacked):
        turned[i] = projected[i].T
    small[...] = jnp.zeros_like(small)
    seg = segments[...]
    small[2 * groups : 2 * groups + 1] = (seg >> 8).astype(f32)
    small[2 * groups + 1 : 2 * groups + 2] = (seg & 255).astype(f32)
    for s in range(devices):
        to = lax.rem(me + s, devices)
        for i in range(stacked):
            outs[s][i * chunk : (i + 1) * chunk] = turned[i, block_at(to, chunk)]
        count = groups * devices
        taps = pltpu.roll(filters[...], lax.rem(count - to * groups, count), 0)[0:groups]
        high = taps.astype(bf16).astype(f32)
        small[0:groups] = high
        small[groups : 2 * groups] = taps - high
        outs[s][stacked * chunk :] = small[...].astype(bf16)


def pack_channels_kernel(parts, cotangent, weights, *outs):
    me = lax.axis_index("tp")
    rows, width = cotangent.shape
    for s in range(1, parts):
        to = lax.rem(me + s, parts)
        outs[s - 1][0:rows] = cotangent[...]
        outs[s - 1][rows:] = weights[:, block_at(to, width)]


def tap_columns(short_filter, flat, columns, me, chunk):
    stacked, taps, _ = short_filter.shape
    flat[...] = jnp.zeros_like(flat)
    for i in range(stacked):
        flat[i * taps : (i + 1) * taps] = short_filter[i]
    columns[...] = flat[...].T
    return columns[block_at(me, chunk)]


def tap_masks(seg, taps):
    wide = jnp.broadcast_to(seg, (8, seg.shape[1]))
    place = lax.broadcasted_iota(jnp.int32, wide.shape, 1)
    masks = [None]
    for s in range(1, taps):
        same = (wide == pltpu.roll(wide, s, 1)) & (place >= s)
        masks.append(jnp.where(same, 1.0, 0.0)[0:1])
    return masks


def conv_kernel(devices, short_filter, *rest):
    pays, rest = rest[:devices], rest[devices:]
    y_outs, rest = rest[:devices], rest[devices:]
    conv, long, source, seg_out, columns_out, toeplitz, small, flat, columns, y_full = rest
    me = lax.axis_index("ctx")
    stacked, taps, _ = short_filter.shape
    _, chunk, span = conv.shape
    length = span // devices
    groups = toeplitz.shape[0]
    size = chunk // groups
    body = stacked * chunk
    for s in range(devices):
        at = block_at(lax.rem(me - s + devices, devices), length)
        source[:, at] = pays[s][0:body]
        small[:, at] = pays[s][body:].astype(f32)
    seg = small[2 * groups : 2 * groups + 1] * 256.0 + small[2 * groups + 1 : 2 * groups + 2]
    seg_out[...] = jnp.broadcast_to(seg, seg_out.shape)
    masks = tap_masks(seg, taps)
    column = tap_columns(short_filter, flat, columns, me, chunk)
    columns_out[...] = column
    for i in range(stacked):
        x = source[i * chunk : (i + 1) * chunk].astype(f32)
        total = column[:, i * taps : i * taps + 1] * x
        for s in range(1, taps):
            j = i * taps + s
            total += column[:, j : j + 1] * (masks[s] * pltpu.roll(x, s, 1))
        conv[i] = total
    high, low = split_bf16(conv[1] * conv[2])
    for g in range(groups):
        line = small[g : g + 1] + small[groups + g : groups + g + 1]
        padded = jnp.concatenate([line, jnp.zeros((1, SUB), f32)], axis=1)
        turned = pltpu.roll(
            jnp.broadcast_to(padded, (SUB, span + SUB)), 0, 1, stride=1, stride_axis=0
        )[:, :span].astype(bf16)
        for r in range(length // SUB):
            rows = slice(r * SUB, (r + 1) * SUB)
            if r:
                toeplitz[g, rows, : r * SUB] = jnp.zeros((SUB, r * SUB), bf16)
            toeplitz[g, rows, r * SUB :] = turned[:, : span - r * SUB]
        own = slice(g * size, (g + 1) * size)
        pieces = []
        for j in range(devices):
            at = slice(j * length, (j + 1) * length)
            pieces += [high[own, at], low[own, at]]
        stack = jnp.concatenate(pieces, axis=0)
        totals = [None] * devices
        for lag in range(devices):
            part = jnp.dot(
                stack[: 2 * size * (devices - lag)],
                toeplitz[g, :, lag * length : (lag + 1) * length],
                preferred_element_type=f32,
            )
            for j in range(devices - lag):
                term = part[2 * size * j : 2 * size * j + size]
                term += part[2 * size * j + size : 2 * size * (j + 1)]
                i = j + lag
                totals[i] = term if totals[i] is None else totals[i] + term
        for i in range(devices):
            long[own, i * length : (i + 1) * length] = totals[i]
    y_full[...] = (conv[0] * long[...]).astype(bf16)
    for s in range(devices):
        y_outs[s][...] = y_full[:, block_at(lax.rem(me + s, devices), length)]


def grad_y_kernel(devices, parts, weights, cotangent, *rest):
    pays, rest = rest[: parts - 1], rest[parts - 1 :]
    outs, (full,) = rest[:devices], rest[devices:]
    me, mine = lax.axis_index("ctx"), lax.axis_index("tp")
    rows, width = cotangent.shape
    chunk = width // devices
    total = None
    for s in range(parts):
        cot = cotangent[...] if s == 0 else pays[s - 1][0:rows]
        lhs = weights[:, block_at(lax.rem(mine - s + parts, parts), width)]
        term = lax.dot_general(lhs, cot, (((1,), (1,)), ((), ())), preferred_element_type=f32)
        total = term if total is None else total + term
    full[...] = total
    for s in range(devices):
        outs[s][...] = full[block_at(lax.rem(me + s, devices), chunk)].astype(outs[s].dtype)


def weight_grad_kernel(devices, parts, cotangent, *rest):
    pays, rest = rest[: parts - 1], rest[parts - 1 :]
    ys, (y_out, keep, send, full) = rest[:devices], rest[devices:]
    me, mine, core = lax.axis_index("ctx"), lax.axis_index("tp"), lax.axis_index("dp")
    rows, width = cotangent.shape
    chunk = width // devices
    half = width // 2
    for s in range(devices):
        y_out[block_at(lax.rem(me - s + devices, devices), chunk)] = ys[s][...]
    y = y_out[...]
    for s in range(parts):
        cot = cotangent[...] if s == 0 else pays[s - 1][0:rows]
        at = block_at(lax.rem(mine - s + parts, parts), width)
        full[:, at] = jnp.dot(y, cot, preferred_element_type=f32)
    keep[...] = full[block_at(core, half)]
    send[...] = full[block_at(1 - core, half)].astype(send.dtype)


def core_sum_kernel(devices, keep, other, *rest):
    outs, (full,) = rest[:devices], rest[devices:]
    me = lax.axis_index("ctx")
    rows = keep.shape[0] // devices
    full[...] = keep[...] + other[...].astype(f32)
    for s in range(devices):
        at = block_at(lax.rem(me + s, devices), rows)
        outs[s][...] = full[at].astype(outs[s].dtype)


def block_sum_kernel(scale, *refs):
    total = refs[0][...]
    for ref in refs[1:-1]:
        total += ref[...].astype(f32)
    refs[-1][...] = (total * scale).astype(refs[-1].dtype)


def weight_out_kernel(devices, *refs):
    out = refs[-1]
    me, core = lax.axis_index("ctx"), lax.axis_index("dp")
    rows = out.shape[0] // (2 * devices)
    for h in range(2):
        side = core if h == 0 else 1 - core
        for s in range(devices):
            block = side * devices + lax.rem(me - s + devices, devices)
            out[block_at(block, rows)] = refs[h * devices + s][...].astype(f32)


def mixed_kernel(parts, weights, *rest):
    ys, pays, out = rest[:parts], rest[parts:-1], rest[-1]
    mine = lax.axis_index("tp")
    rows, width = out.shape
    total = None
    for s in range(parts):
        w = weights[:, block_at(mine, width)] if s == 0 else pays[s - 1][rows:]
        term = lax.dot_general(
            ys[s][...], w, (((0,), (0,)), ((), ())), preferred_element_type=f32
        )
        total = term if total is None else total + term
    out[...] = total.astype(bf16)


def backward_kernel(devices, taps, conv, long, source, seg, column_ref, toeplitz, *rest):
    gys, rest = rest[:devices], rest[devices:]
    outs, (grad_y, grads, small, marks) = rest[:devices], rest[devices:]
    me = lax.axis_index("ctx")
    stacked, chunk, span = conv.shape
    length = span // devices
    groups = toeplitz.shape[0]
    size = chunk // groups
    body = stacked * chunk
    for s in range(devices):
        at = block_at(lax.rem(me - s + devices, devices), length)
        grad_y[:, at] = gys[s][...].astype(f32)
    masks = tap_masks(seg[0:1], taps)
    column = column_ref[...]
    gy = grad_y[...]
    grad_long_out = gy * conv[0]
    high, low = split_bf16(grad_long_out)
    gated = (conv[1] * conv[2]).astype(bf16)
    gg_parts = []
    corner = lax.broadcasted_iota(jnp.int32, (SUB, SUB), 0)
    corner += lax.broadcasted_iota(jnp.int32, (SUB, SUB), 1)
    flip = jnp.where(corner == SUB - 1, 1.0, 0.0).astype(bf16)
    subs = span // SUB
    small[...] = jnp.zeros_like(small)
    for g in range(groups):
        own = slice(g * size, (g + 1) * size)
        pieces = []
        for i in range(devices):
            at = slice(i * length, (i + 1) * length)
            pieces += [high[own, at], low[own, at]]
        stack = jnp.concatenate(pieces, axis=0)
        totals = [None] * devices
        for lag in range(devices):
            part = lax.dot_general(
                stack[2 * size * lag :],
                toeplitz[g, :, lag * length : (lag + 1) * length],
                (((1,), (1,)), ((), ())),
                preferred_element_type=f32,
            )
            for j in range(devices - lag):
                term = part[2 * size * j : 2 * size * j + size]
                term += part[2 * size * j + size : 2 * size * (j + 1)]
                totals[j] = term if totals[j] is None else totals[j] + term
        gg_parts.append(jnp.concatenate(totals, axis=1))
        left = jnp.concatenate([gated[own, j * SUB : (j + 1) * SUB] for j in range(subs)], axis=0)
        right = jnp.concatenate([high[own, j * SUB : (j + 1) * SUB] for j in range(subs)], axis=0)
        turned = lax.dot_general(
            flip, left, (((1,), (1,)), ((), ())), preferred_element_type=f32
        ).astype(bf16)
        lines = []
        for lag in range(subs):
            cross = jnp.dot(
                turned[:, : size * (subs - lag)], right[size * lag :], preferred_element_type=f32
            )
            wide = jnp.concatenate([cross, jnp.zeros((SUB, SUB), f32)], axis=1)
            wide = pltpu.roll(wide, 1, 1, stride=1, stride_axis=0)
            lines.append(jnp.sum(wide, axis=0, keepdims=True))
        per = length // SUB
        for lag in range(subs):
            line = lines[lag][:, SUB:]
            if lag + 1 < subs:
                line += lines[lag + 1][:, :SUB]
            b, within = divmod(lag, per)
            small[b, g : g + 1, within * SUB : (within + 1) * SUB] = line
    grad_gated = jnp.concatenate(gg_parts, axis=0)
    lane = lax.broadcasted_iota(jnp.int32, (chunk, SUB), 1)
    sums = jnp.zeros((chunk, SUB), f32)
    for i in range(stacked):
        if i == 0:
            grad = gy * long[...]
        else:
            grad = grad_gated * conv[3 - i]
        x = source[i * chunk : (i + 1) * chunk].astype(f32)
        total = column[:, i * taps : i * taps + 1] * grad
        sums += jnp.where(lane == i * taps, jnp.sum(grad * x, axis=1, keepdims=True), 0.0)
        for s in range(1, taps):
            j = i * taps + s
            masked = masks[s] * grad
            total += column[:, j : j + 1] * pltpu.roll(masked, span - s, 1)
            tap = jnp.sum(masked * pltpu.roll(x, s, 1), axis=1, keepdims=True)
            sums += jnp.where(lane == j, tap, 0.0)
        grads[i * chunk : (i + 1) * chunk] = total.astype(bf16)
    rows = stacked * taps
    marks[...] = jnp.zeros_like(marks)
    marks[:, 0:chunk] = sums.T
    placed = pltpu.roll(marks[0:16], me * chunk, 1)
    for b in range(devices):
        small[b, groups : groups + rows] = placed[0:rows]
    room = small.shape[1]
    for s in range(devices):
        to = lax.rem(me + s, devices)
        outs[s][0:body] = grads[:, block_at(to, length)]
        value = small[to]
        top = value.astype(bf16)
        outs[s][body : body + room] = top
        outs[s][body + room :] = (value - top.astype(f32)).astype(bf16)


def grad_out_kernel(devices, groups, *refs):
    pays, (out, sums, turned) = refs[:devices], refs[devices:]
    me = lax.axis_index("ctx")
    stacked, _, width = out.shape
    chunk = width // devices
    body = stacked * chunk
    room = (pays[0].shape[0] - body) // 2
    count = groups * devices
    total = long_rows = None
    for s in range(devices):
        come = lax.rem(me - s + devices, devices)
        for i in range(stacked):
            turned[i, block_at(come, chunk)] = pays[s][i * chunk : (i + 1) * chunk]
        value = pays[s][body : body + room].astype(f32) + pays[s][body + room :].astype(f32)
        row = lax.broadcasted_iota(jnp.int32, (count, value.shape[1]), 0)
        line = pltpu.roll(jnp.where(row < groups, value[0:count], 0.0), come * groups, 0)
        long_rows = line if long_rows is None else long_rows + line
        total = value if total is None else total + value
    for i in range(stacked):
        out[i] = turned[i].T
    sums[...] = jnp.zeros_like(sums)
    sums[0:count] = long_rows
    sums[count : count + room - groups] = total[groups:]


def small_out_kernel(scale, mine, other, short_out, long_out):
    total = (mine[...] + other[...]) * scale
    count = long_out.shape[0]
    stacked, taps, _ = short_out.shape
    long_out[...] = total[0:count]
    for i in range(stacked):
        start = count + i * taps
        short_out[i] = total[start : start + taps]


def direct_device(projected, segment_ids, short_filter, long_filter, out_proj, mixed_cotangent):
    devices, parts = lax.axis_size("ctx"), lax.axis_size("tp")
    stacked, _, length, width = projected.shape
    taps = short_filter.shape[1]
    groups = long_filter.shape[0] // devices
    chunk = width // devices
    span = length * devices
    total_cols = out_proj.shape[1]
    grad_scale = 1.0 / math.sqrt(projected.shape[1] * lax.axis_size("dp") * span)
    cotangent = mixed_cotangent[0]
    room = 16
    size = stacked * chunk + room

    packed = on_core(
        functools.partial(pack_signal_kernel, devices),
        [((size, length), bf16)] * devices,
        (projected[:, 0], long_filter, segment_ids),
        "pack_signal",
        [pltpu.VMEM((stacked, width, length), bf16), pltpu.VMEM((room, length), f32)],
    )
    signal = scatter_chunks(packed, "ctx")
    tp_packed = on_core(
        functools.partial(pack_channels_kernel, parts),
        [((length + width, width), bf16)] * (parts - 1),
        (cotangent, out_proj),
        "pack_channels",
    )
    pays = [rotate(tp_packed[s - 1], "tp", s) for s in range(1, parts)]

    gy = on_core(
        functools.partial(grad_y_kernel, devices, parts),
        [((chunk, length), bf16)] * devices,
        (out_proj, cotangent, *pays),
        "grad_y",
        [pltpu.VMEM((width, length), f32)],
        flops=2 * width * length * total_cols,
    )
    gy_in = scatter_chunks(gy, "ctx")

    conv_flops = 2 * groups * span * span * 64
    outs = on_core(
        functools.partial(conv_kernel, devices),
        [((chunk, length), bf16)] * devices
        + [
            ((stacked, chunk, span), f32),
            ((chunk, span), f32),
            ((stacked * chunk, span), bf16),
            ((8, span), f32),
            ((chunk, 16), f32),
            ((groups, length, span), bf16),
        ],
        (short_filter, *signal),
        "conv",
        [
            pltpu.VMEM((room, span), f32),
            pltpu.VMEM((16, width), f32),
            pltpu.VMEM((width, 16), f32),
            pltpu.VMEM((chunk, span), bf16),
        ],
        flops=conv_flops,
    )
    ys, kept = outs[:devices], outs[devices:]
    y_in = scatter_chunks(ys, "ctx")

    half = width // 2
    y_full, keep, send = on_core(
        functools.partial(weight_grad_kernel, devices, parts),
        [((width, length), bf16), ((half, total_cols), f32), ((half, total_cols), f32)],
        (cotangent, *pays, *y_in),
        "weight_grad",
        [pltpu.VMEM((width, total_cols), f32)],
        flops=2 * width * length * total_cols,
    )
    other = rotate(send, "dp", 1)
    rows = half // devices
    sums = on_core(
        functools.partial(core_sum_kernel, devices),
        [((rows, total_cols), f32)] + [((rows, total_cols), bf16)] * (devices - 1),
        (keep, other),
        "core_sum",
        [pltpu.VMEM((half, total_cols), f32)],
    )
    sums = scatter_chunks(sums, "ctx")
    (block,) = on_core(
        functools.partial(block_sum_kernel, grad_scale),
        [((rows, total_cols), bf16)],
        sums,
        "block_sum",
    )
    near = spread(block, "ctx")
    far = [rotate(piece, "dp", 1) for piece in near]
    (grad_out_proj,) = on_core(
        functools.partial(weight_out_kernel, devices),
        [((width, total_cols), f32)],
        (*near, *far),
        "weight_out",
    )

    y_all = spread(y_full, "tp")
    (mixed,) = on_core(
        functools.partial(mixed_kernel, parts),
        [((length, width), bf16)],
        (out_proj, *y_all, *pays),
        "mixed",
        flops=2 * width * length * total_cols,
    )

    back = on_core(
        functools.partial(backward_kernel, devices, taps),
        [((size + room, length), bf16)] * devices,
        (*kept, *gy_in),
        "backward",
        [
            pltpu.VMEM((chunk, span), f32),
            pltpu.VMEM((stacked * chunk, span), bf16),
            pltpu.VMEM((devices, room, length), f32),
            pltpu.VMEM((SUB, width), f32),
        ],
        flops=2 * conv_flops,
    )
    back = scatter_chunks(back, "ctx")
    count = groups * devices
    grad_projected, small = on_core(
        functools.partial(grad_out_kernel, devices, groups),
        [((stacked, length, width), bf16), ((count + 16, width), f32)],
        back,
        "grad_out",
        [pltpu.VMEM((stacked, width, length), bf16)],
    )
    grad_short, grad_long = on_core(
        functools.partial(small_out_kernel, grad_scale),
        [(short_filter.shape, f32), ((count, length), f32)],
        (small, rotate(small, "dp", 1)),
        "small_out",
    )
    return (mixed[None], grad_projected[:, None], grad_short, grad_long, grad_out_proj)


def direct_fits(mesh, projected, short_filter, long_filter):
    devices = mesh.shape["ctx"]
    length = projected.shape[2] // devices
    width = projected.shape[3] // mesh.shape["tp"]
    groups = long_filter.shape[0] // mesh.shape["tp"]
    stacked, taps = short_filter.shape[:2]
    return (
        mesh.shape["dp"] == 2
        and projected.shape[1] == 2
        and stacked == 3
        and length == width
        and length % SUB == 0
        and groups % devices == 0
        and groups == 16
        and (width // devices) % 16 == 0
        and width // devices <= SUB
        and (width // groups) == 16
        and 2 * groups // devices + 2 <= 16
        and groups // devices + stacked * taps <= 16
    )


def solution(mesh):
    in_specs = (
        P(None, "dp", "ctx", "tp"),
        P("dp", "ctx"),
        P(None, None, "tp"),
        P("tp", "ctx"),
        P("tp", None),
        P("dp", "ctx", "tp"),
    )
    out_specs = (
        P("dp", "ctx", "tp"),
        P(None, "dp", "ctx", "tp"),
        P(None, None, "tp"),
        P("tp", "ctx"),
        P("tp", None),
    )

    def layer(projected, segment_ids, short_filter, long_filter, out_proj, mixed_cotangent):
        fits = direct_fits(mesh, projected, short_filter, long_filter)
        return jax.shard_map(
            direct_device if fits else spectral_device,
            mesh=mesh,
            in_specs=in_specs,
            out_specs=out_specs,
            check_vma=False,
        )(projected, segment_ids, short_filter, long_filter, out_proj, mixed_cotangent)

    return layer
```

```python
import functools
import math

import jax
import jax.numpy as jnp
from jax import lax
from jax.experimental import pallas as pl
from jax.experimental.pallas import tpu as pltpu
from jax.sharding import PartitionSpec as P

highest_precision = lax.Precision.HIGHEST


def shifted(value, axis, steps):
    count = lax.axis_size(axis)
    first, last = (max(0, -steps), min(count, count - steps))
    return lax.ppermute(value, axis, [(source, source + steps) for source in range(first, last)])


def angle_table(height, breadth, period, direction):
    product = (
        jnp.arange(height, dtype=jnp.int32)[:, None]
        * jnp.arange(breadth, dtype=jnp.int32)[None, :]
        % period
    )
    angles = direction * 2.0 * math.pi / period * product.astype(jnp.float32)
    return (jnp.cos(angles), jnp.sin(angles))


def row_twiddle(spec_re, spec_im, direction):
    my_index = lax.axis_index("ctx")
    devices = lax.axis_size("ctx")
    row_count = spec_re.shape[1]
    period = 2 * devices * row_count
    freq_pair = 2 * my_index + jnp.arange(2, dtype=jnp.int32)
    product = freq_pair[:, None] * jnp.arange(row_count, dtype=jnp.int32)[None, :] % period
    angles = direction * 2.0 * math.pi / period * product.astype(jnp.float32)
    cosine = jnp.cos(angles)[:, :, None]
    sine_part = jnp.sin(angles)[:, :, None]
    return (spec_re * cosine - spec_im * sine_part, spec_re * sine_part + spec_im * cosine)


def row_transform(spec_re, spec_im, direction):
    row_count = spec_re.shape[1]
    cosine, sine_part = angle_table(row_count, row_count, row_count, direction)

    def along_rows(blocks, matrix):
        return jnp.einsum("kmc,mq->kqc", blocks, matrix, precision=highest_precision)

    return (
        along_rows(spec_re, cosine) - along_rows(spec_im, sine_part),
        along_rows(spec_re, sine_part) + along_rows(spec_im, cosine),
    )


def mixing(matrix, blocks):
    return jnp.einsum("kj,jmc->kmc", matrix, blocks, precision=highest_precision)


def forward_spectrum(real_part):
    devices = lax.axis_size("ctx")
    cosine, sine_part = angle_table(2 * devices, devices, 2 * devices, -1.0)
    spread_re = lax.all_to_all(real_part[None], "ctx", split_axis=1, concat_axis=0, tiled=True)
    column_re = mixing(cosine, spread_re)
    column_im = mixing(sine_part, spread_re)
    near_re, near_im = (
        lax.all_to_all(column_re, "ctx", split_axis=0, concat_axis=1, tiled=True),
        lax.all_to_all(column_im, "ctx", split_axis=0, concat_axis=1, tiled=True),
    )
    twist_re, twist_im = row_twiddle(near_re, near_im, -1.0)
    return row_transform(twist_re, twist_im, -1.0)


def inverse_spectrum(spec_re, spec_im):
    devices = lax.axis_size("ctx")
    row_count = spec_re.shape[1]
    back_re, back_im = row_transform(spec_re, spec_im, 1.0)
    twist_re, twist_im = row_twiddle(back_re / row_count, back_im / row_count, 1.0)
    far_re, far_im = (
        lax.all_to_all(twist_re, "ctx", split_axis=1, concat_axis=0, tiled=True),
        lax.all_to_all(twist_im, "ctx", split_axis=1, concat_axis=0, tiled=True),
    )
    cosine, sine_part = angle_table(devices, 2 * devices, 2 * devices, 1.0)
    out_re = (mixing(cosine, far_re) - mixing(sine_part, far_im)) / (2 * devices)
    rows_re = lax.all_to_all(out_re, "ctx", split_axis=0, concat_axis=1, tiled=True)
    return (rows_re[0], rows_re[0])


def pack_columns(values):
    return (values, values)


def by_filter(val_re, val_im, fil_re, fil_im, conjugate):
    val_shape = val_re.shape
    group_count = fil_re.shape[2]
    v_re = val_re.reshape(val_shape[0], val_shape[1], group_count, -1)
    v_im = val_im.reshape(val_shape[0], val_shape[1], group_count, -1)
    f_re = fil_re[:, :, :, None]
    f_im = fil_im[:, :, :, None]
    if conjugate:
        f_im = -f_im
    out_re = v_re * f_re - v_im * f_im
    out_im = v_re * f_im + v_im * f_re
    return (out_re.reshape(val_shape), out_im.reshape(val_shape))


def short_local(extended, filters, seg_ext):
    reach_taps = filters.shape[1]
    out_rows = extended.shape[1] - reach_taps + 1
    own_seg = seg_ext[reach_taps - 1 :]
    running = jnp.zeros((extended.shape[0], out_rows, extended.shape[2]), jnp.float32)
    for shift_by in range(reach_taps):
        start_row = reach_taps - 1 - shift_by
        same_doc = jnp.where(seg_ext[start_row : start_row + out_rows] == own_seg, 1.0, 0.0)
        running = (
            running
            + filters[:, shift_by][:, None, :]
            * same_doc[None, :, None]
            * extended[:, start_row : start_row + out_rows]
        )
    return running


def spectral_device(projected, segment_ids, short_filter, long_filter, out_proj, mixed_cotangent):
    row_count = projected.shape[2]
    stacked = projected.shape[0]
    width_dev = projected.shape[3]
    short_reach = short_filter.shape[1]
    group_count = long_filter.shape[0]
    grad_scale = 1.0 / math.sqrt(
        projected.shape[1] * lax.axis_size("dp") * row_count * lax.axis_size("ctx")
    )
    segments = segment_ids[0]
    source = projected[:, 0]
    short_rows = short_reach - 1
    cot_full = lax.all_gather(mixed_cotangent[0], "tp", axis=1, tiled=True)
    prev_tail, prev_seg = shifted(
        (source[:, row_count - short_rows :], segments[row_count - short_rows :]), "ctx", 1
    )
    short_seg = jnp.concatenate([prev_seg, segments])
    short_ext = jnp.concatenate([prev_tail, source], axis=1).astype(jnp.float32)

    def short_piece(extended, filters):
        return short_local(extended, filters, short_seg)

    short_out, short_pull = jax.vjp(short_piece, short_ext, short_filter)
    query_conv = short_out[0]
    gated_rows = short_out[1] * short_out[2]
    filter_cols = long_filter.T
    mid_re, mid_im = pack_columns(gated_rows)
    spec_re, spec_im = forward_spectrum(jnp.concatenate([mid_re, filter_cols], axis=1))
    data_cols = spec_re.shape[2] - group_count
    signal_re = spec_re[:, :, :data_cols]
    signal_im = spec_im[:, :, :data_cols]
    filt_re = spec_re[:, :, data_cols:]
    filt_im = spec_im[:, :, data_cols:]
    long_re, long_im = by_filter(signal_re, signal_im, filt_re, filt_im, False)
    out_re, out_im = inverse_spectrum(long_re, long_im)
    y_out = (query_conv * out_re).astype(jnp.bfloat16)
    partial_out = jnp.dot(y_out, out_proj, preferred_element_type=jnp.float32)
    mixed = lax.psum_scatter(partial_out, "tp", scatter_dimension=1, tiled=True).astype(
        jnp.bfloat16
    )
    grad_y = jnp.dot(cot_full, out_proj.T, preferred_element_type=jnp.float32)
    grad_proj_local = jnp.dot(y_out.T, cot_full, preferred_element_type=jnp.float32)
    grad_long_out = grad_y * query_conv
    grad_query = grad_y * out_re
    grad_in_re, grad_in_im = pack_columns(grad_long_out)
    cot_re, cot_im = forward_spectrum(grad_in_re)
    back_re, back_im = by_filter(cot_re, cot_im, filt_re, filt_im, True)
    cross_re = (
        (signal_re * cot_re + signal_im * cot_im).reshape(2, row_count, group_count, -1).sum(axis=3)
    )
    cross_im = (
        (signal_re * cot_im - signal_im * cot_re).reshape(2, row_count, group_count, -1).sum(axis=3)
    )
    inv_re, inv_im = inverse_spectrum(
        jnp.concatenate([back_re, cross_re], axis=2), jnp.concatenate([back_im, cross_im], axis=2)
    )
    grad_gated = inv_re[:, :data_cols]
    grad_long_local = inv_re[:, data_cols:].T
    grad_short_out = jnp.stack([grad_query, grad_gated * short_out[2], grad_gated * short_out[1]])
    grad_short_ext, grad_short_local = short_pull(grad_short_out)
    returned_short = shifted(grad_short_ext[:, :short_rows], "ctx", -1)
    grad_source = grad_short_ext[:, short_rows:] + jnp.concatenate(
        [jnp.zeros((stacked, row_count - short_rows, width_dev), jnp.float32), returned_short],
        axis=1,
    )
    total_proj, total_short = lax.psum((grad_proj_local, grad_short_local), ("ctx", "dp"))
    total_long = lax.psum(grad_long_local, "dp")
    return (
        mixed[None],
        grad_source[:, None].astype(jnp.bfloat16),
        total_short * grad_scale,
        total_long * grad_scale,
        total_proj * grad_scale,
    )


bf16 = jnp.bfloat16
f32 = jnp.float32
SUB = 128


def split_bf16(value):
    high = value.astype(bf16)
    return high, (value - high.astype(f32)).astype(bf16)


def rotate(value, axis, steps):
    count = lax.axis_size(axis)
    return lax.ppermute(value, axis, [(i, (i + steps) % count) for i in range(count)])


def swap(value, axis, bits):
    return lax.ppermute(value, axis, [(i, i ^ bits) for i in range(lax.axis_size(axis))])


def scatter_chunks(chunks, axis):
    return [chunks[0]] + [rotate(chunks[s], axis, s) for s in range(1, len(chunks))]


def after(value, other):
    return lax.optimization_barrier((value, other))[0]


def spread(value, axis):
    return [value] + [rotate(value, axis, s) for s in range(1, lax.axis_size(axis))]


def on_core(kernel, outs, args, name, scratch=(), flops=0, whole=False):
    moved = sum(a.size * a.dtype.itemsize for a in args)
    moved += sum(math.prod(shape) * jnp.dtype(kind).itemsize for shape, kind in outs)
    return pl.pallas_call(
        kernel,
        out_shape=[jax.ShapeDtypeStruct(shape, kind) for shape, kind in outs],
        in_specs=[pl.BlockSpec(memory_space=pltpu.HBM) if whole else pl.BlockSpec()] * len(args),
        scratch_shapes=list(scratch),
        compiler_params=pltpu.CompilerParams(vmem_limit_bytes=(63 if whole else 40) * 1024 * 1024),
        cost_estimate=pl.CostEstimate(flops=flops, bytes_accessed=moved, transcendentals=0),
        name=name,
    )(*args)


def block_at(index, size):
    return pl.ds(pl.multiple_of(index * size, size), size)


def pack_kernel(devices, *refs):
    sources, refs = refs[:3], refs[3:]
    outs, query, refs = refs[:devices], refs[devices], refs[devices + 1 :]
    held, (turned, small, sems) = refs[:3], refs[3:]
    copies = [
        pltpu.make_async_copy(sources[n], held[n], sems.at[n]) for n in range(len(sources))
    ]
    for copy in copies:
        copy.start()
    projected, filters, segments = held
    me = lax.axis_index("ctx")
    stacked, rows, width = projected.shape
    chunk = width // devices
    count = filters.shape[0]
    groups = count // devices
    for copy in copies:
        copy.wait()
    for i in range(1, stacked):
        turned[i - 1] = projected[i].T
    query[...] = projected[0].T
    small[...] = jnp.zeros_like(small)
    seg = segments[...]
    small[2 * groups : 2 * groups + 1] = (seg >> 8).astype(f32)
    small[2 * groups + 1 : 2 * groups + 2] = (seg & 255).astype(f32)
    body = (stacked - 1) * chunk
    for s in range(devices):
        to = lax.rem(me + s, devices)
        for i in range(stacked - 1):
            outs[s][i * chunk : (i + 1) * chunk] = turned[i, block_at(to, chunk)]
        lines = pltpu.roll(filters[...], lax.rem(count - to * groups, count), 0)[0:groups]
        high = lines.astype(bf16).astype(f32)
        small[0:groups] = high
        small[groups : 2 * groups] = lines - high
        outs[s][body : body + 16] = small[...].astype(bf16)
    outs[1][body + 16 :] = projected[0, rows - 16 :]


def prepare_kernel(short_filter, chunk, query, columns, chunk_out, query_out, flat):
    stacked, taps, _ = short_filter.shape
    flat[...] = jnp.zeros_like(flat)
    for i in range(stacked):
        flat[i * taps : (i + 1) * taps] = short_filter[i]
    columns[...] = flat[...].T
    chunk_out[...] = chunk[...]
    query_out[...] = query[...]


def tap_masks(seg, taps):
    wide = jnp.broadcast_to(seg, (8, seg.shape[1]))
    place = lax.broadcasted_iota(jnp.int32, wide.shape, 1)
    masks = [None]
    for s in range(1, taps):
        same = (wide == pltpu.roll(wide, s, 1)) & (place >= s)
        masks.append(jnp.where(same, 1.0, 0.0)[0:1])
    return masks


def block_masks(seg, taps, place, me, length):
    masks = tap_masks(seg, taps)
    for s in range(1, taps):
        place[8 * s : 8 * (s + 1)] = jnp.broadcast_to(masks[s], (8, seg.shape[1]))
    return [None] + [place[8 * s : 8 * s + 8, block_at(me, length)][0:1] for s in range(1, taps)]


def query_shifts(query, previous, taps):
    halo = previous[previous.shape[0] - 16 :]
    before = jnp.concatenate([jnp.zeros((SUB - 16, halo.shape[1]), f32), halo.astype(f32)], axis=0)
    wide = jnp.concatenate([before.T, query.astype(f32)], axis=1)
    return [wide[:, SUB:]] + [pltpu.roll(wide, s, 1)[:, SUB:] for s in range(1, taps)]


def conv_kernel(devices, taps, columns, *rest):
    pays, rest = rest[:devices], rest[devices:]
    outs, rest = rest[:devices], rest[devices:]
    conv, source, seg_out, toeplitz, small, long, rests = rest
    me = lax.axis_index("ctx")
    stacked, chunk, span = conv.shape
    length = span // devices
    groups = toeplitz.shape[0]
    size = chunk // groups
    body = stacked * chunk
    for s in range(devices):
        at = block_at(lax.rem(me - s + devices, devices), length)
        source[:, at] = pays[s][0:body]
        small[:, at] = pays[s][body : body + 16].astype(f32)
    seg = small[2 * groups : 2 * groups + 1] * 256.0 + small[2 * groups + 1 : 2 * groups + 2]
    seg_out[...] = jnp.broadcast_to(seg, seg_out.shape)
    masks = tap_masks(seg, taps)
    column = columns[block_at(me, chunk)]
    for i in range(stacked):
        x = source[i * chunk : (i + 1) * chunk].astype(f32)
        j = (i + 1) * taps
        total = column[:, j : j + 1] * x
        for s in range(1, taps):
            total += column[:, j + s : j + s + 1] * (masks[s] * pltpu.roll(x, s, 1))
        conv[i] = total
    high, low = split_bf16(conv[0] * conv[1])
    for g in range(groups):
        line = small[g : g + 1] + small[groups + g : groups + g + 1]
        padded = jnp.concatenate([line, jnp.zeros((1, SUB), f32)], axis=1)
        turned = pltpu.roll(
            jnp.broadcast_to(padded, (SUB, span + SUB)), 0, 1, stride=1, stride_axis=0
        )[:, :span]
        for half, into in zip(split_bf16(turned), (toeplitz, rests)):
            for r in range(length // SUB):
                rows = slice(r * SUB, (r + 1) * SUB)
                if r:
                    into[g, rows, : r * SUB] = jnp.zeros((SUB, r * SUB), bf16)
                into[g, rows, r * SUB :] = half[:, : span - r * SUB]
        own = slice(g * size, (g + 1) * size)
        pieces = []
        for j in range(devices):
            at = slice(j * length, (j + 1) * length)
            pieces += [high[own, at], low[own, at]]
        stack = jnp.concatenate(pieces, axis=0)
        totals = [None] * devices
        for lag in range(devices):
            lhs = stack[: 2 * size * (devices - lag)]
            at = slice(lag * length, (lag + 1) * length)
            part = jnp.dot(lhs, toeplitz[g, :, at], preferred_element_type=f32)
            part += jnp.dot(lhs, rests[g, :, at], preferred_element_type=f32)
            for j in range(devices - lag):
                term = part[2 * size * j : 2 * size * j + size]
                term += part[2 * size * j + size : 2 * size * (j + 1)]
                i = j + lag
                totals[i] = term if totals[i] is None else totals[i] + term
        for i in range(devices):
            long[own, i * length : (i + 1) * length] = totals[i].astype(bf16)
    for s in range(devices):
        outs[s][...] = long[:, block_at(lax.rem(me + s, devices), length)]


def grad_y_kernel(devices, parts, taps, weights, query, previous, columns, seg, *rest):
    cots, rest = rest[:parts], rest[parts:]
    longs, rest = rest[:devices], rest[devices:]
    outs, (grad_y, query_conv, place, full) = rest[:devices], rest[devices:]
    me, mine = lax.axis_index("ctx"), lax.axis_index("tp")
    rows, width = cots[0].shape
    chunk = width // devices
    masks = block_masks(seg[0:1], taps, place, me, rows)
    shifts = query_shifts(query[...], previous, taps)
    conv = columns[:, 0:1] * shifts[0]
    for s in range(1, taps):
        conv += columns[:, s : s + 1] * (masks[s] * shifts[s])
    query_conv[...] = conv
    total = None
    for s in range(parts):
        cot = cots[s][...]
        lhs = weights[:, block_at(mine ^ s, width)]
        term = lax.dot_general(lhs, cot, (((1,), (1,)), ((), ())), preferred_element_type=f32)
        total = term if total is None else total + term
    grad_y[...] = total
    full[...] = (total * conv).astype(bf16)
    for s in range(devices):
        outs[s][0:chunk] = longs[s][...]
        outs[s][chunk:] = full[block_at(lax.rem(me + s, devices), chunk)]


def weight_grad_kernel(devices, parts, query_conv, *rest):
    cots, rest = rest[:parts], rest[parts:]
    longs, rest = rest[:devices], rest[devices:]
    y_out, long_out, keep, send, full = rest
    me, mine, core = lax.axis_index("ctx"), lax.axis_index("tp"), lax.axis_index("dp")
    rows, width = cots[0].shape
    chunk = width // devices
    half = width // 2
    for s in range(devices):
        at = block_at(lax.rem(me - s + devices, devices), chunk)
        long_out[at] = longs[s][0:chunk].astype(f32)
    y = (query_conv[...] * long_out[...]).astype(bf16)
    y_out[...] = y
    for s in range(parts):
        cot = cots[s][...]
        at = block_at(mine ^ s, width)
        full[:, at] = jnp.dot(y, cot, preferred_element_type=f32)
    keep[...] = full[block_at(core, half)]
    send[...] = full[block_at(1 - core, half)]


def core_sum_kernel(devices, keep, other, *rest):
    outs, (full,) = rest[:devices], rest[devices:]
    me = lax.axis_index("ctx")
    rows = keep.shape[0] // devices
    full[...] = keep[...] + other[...].astype(f32)
    for s in range(devices):
        at = block_at(lax.rem(me + s, devices), rows)
        outs[s][...] = full[at].astype(outs[s].dtype)


def block_sum_kernel(devices, scale, *refs):
    sums, refs = refs[:devices], refs[devices:]
    pays, outs = refs[:devices], refs[devices:]
    total = sums[0][...]
    for s in range(1, devices):
        total += sums[s][...].astype(f32)
    total = (total * scale).astype(bf16)
    rows, width = total.shape[0], outs[0].shape[1]
    blocks = total.shape[1] // width
    for s in range(devices):
        for b in range(blocks):
            outs[s][b * rows : (b + 1) * rows] = total[:, b * width : (b + 1) * width]
        outs[s][blocks * rows :] = pays[s][...]


def weight_out_kernel(devices, near, far, out):
    core = lax.axis_index("dp")
    half = near.shape[0]
    out[block_at(core, half)] = near[...].astype(f32)
    out[block_at(1 - core, half)] = far[...].astype(f32)


def mixed_part_kernel(parts, y, weights, *rest):
    outs, (full,) = rest[:parts], rest[parts:]
    mine = lax.axis_index("tp")
    width = outs[0].shape[1]
    full[...] = lax.dot_general(
        y[...], weights[...], (((0,), (0,)), ((), ())), preferred_element_type=f32
    )
    for s in range(parts):
        outs[s][...] = full[:, block_at(mine ^ s, width)].astype(outs[s].dtype)


def mixed_sum_kernel(*refs):
    total = refs[0][...]
    for ref in refs[1:-1]:
        total += ref[...].astype(f32)
    refs[-1][...] = total.astype(bf16)


def backward_kernel(
    devices, taps, conv, source, seg, toeplitz, columns, query, previous, grad_y, long, *rest
):
    glos, rest = rest[:devices], rest[devices:]
    outs, (query_out, grad_long_out, grads, small, marks, place) = rest[:devices], rest[devices:]
    me = lax.axis_index("ctx")
    stacked, chunk, span = conv.shape
    length = span // devices
    groups = toeplitz.shape[0]
    size = chunk // groups
    body = stacked * chunk
    width = query.shape[0]
    room = small.shape[1]

    own_masks = block_masks(seg[0:1], taps, place, me, length)
    shifts = query_shifts(query[...], previous, taps)
    grad = grad_y[...] * long[...]
    total = columns[:, 0:1] * grad
    lane = lax.broadcasted_iota(jnp.int32, (width, SUB), 1)
    position = lax.broadcasted_iota(jnp.int32, (width, length), 1)
    sums = jnp.where(lane == groups, jnp.sum(grad * shifts[0], axis=1, keepdims=True), 0.0)
    early = jnp.zeros((width, SUB), f32)
    for s in range(1, taps):
        masked = own_masks[s] * grad
        back = pltpu.roll(columns[:, s : s + 1] * masked, length - s, 1)
        total += jnp.where(position < length - s, back, 0.0)
        early += jnp.where(position >= length - s, back, 0.0)[:, length - SUB :]
        tap = jnp.sum(masked * shifts[s], axis=1, keepdims=True)
        sums += jnp.where(lane == groups + s, tap, 0.0)
    query_out[...] = total
    common = sums.T[0:room] + early.T[SUB - room :]

    for s in range(devices):
        at = block_at(lax.rem(me - s + devices, devices), length)
        grad_long_out[:, at] = glos[s][chunk:]
    masks = tap_masks(seg[0:1], taps)
    column = columns[block_at(me, chunk)]
    high = grad_long_out[...]
    gated = (conv[0] * conv[1]).astype(bf16)
    gg_parts = []
    corner = lax.broadcasted_iota(jnp.int32, (SUB, SUB), 0)
    corner += lax.broadcasted_iota(jnp.int32, (SUB, SUB), 1)
    flip = jnp.where(corner == SUB - 1, 1.0, 0.0).astype(bf16)
    subs = span // SUB
    small[...] = jnp.zeros_like(small)
    for g in range(groups):
        own = slice(g * size, (g + 1) * size)
        stack = jnp.concatenate(
            [high[own, i * length : (i + 1) * length] for i in range(devices)], axis=0
        )
        totals = [None] * devices
        for lag in range(devices):
            part = lax.dot_general(
                stack[size * lag :],
                toeplitz[g, :, lag * length : (lag + 1) * length],
                (((1,), (1,)), ((), ())),
                preferred_element_type=f32,
            )
            for j in range(devices - lag):
                term = part[size * j : size * (j + 1)]
                totals[j] = term if totals[j] is None else totals[j] + term
        gg_parts.append(jnp.concatenate(totals, axis=1))
        left = jnp.concatenate([gated[own, j * SUB : (j + 1) * SUB] for j in range(subs)], axis=0)
        right = jnp.concatenate([high[own, j * SUB : (j + 1) * SUB] for j in range(subs)], axis=0)
        turned = lax.dot_general(
            flip, left, (((1,), (1,)), ((), ())), preferred_element_type=f32
        ).astype(bf16)
        lines = []
        for lag in range(subs):
            cross = jnp.dot(
                turned[:, : size * (subs - lag)], right[size * lag :], preferred_element_type=f32
            )
            wide = jnp.concatenate([cross, jnp.zeros((SUB, SUB), f32)], axis=1)
            wide = pltpu.roll(wide, 1, 1, stride=1, stride_axis=0)
            lines.append(jnp.sum(wide, axis=0, keepdims=True))
        per = length // SUB
        for lag in range(subs):
            line = lines[lag][:, SUB:]
            if lag + 1 < subs:
                line += lines[lag + 1][:, :SUB]
            b, within = divmod(lag, per)
            small[b, g : g + 1, within * SUB : (within + 1) * SUB] = line
    grad_gated = jnp.concatenate(gg_parts, axis=0)
    lane = lax.broadcasted_iota(jnp.int32, (chunk, SUB), 1)
    sums = jnp.zeros((chunk, SUB), f32)
    for i in range(stacked):
        grad = grad_gated * conv[1 - i]
        x = source[i * chunk : (i + 1) * chunk].astype(f32)
        j = (i + 1) * taps
        total = column[:, j : j + 1] * grad
        tap = jnp.sum(grad * x, axis=1, keepdims=True)
        sums += jnp.where(lane == groups + j, tap, 0.0)
        for s in range(1, taps):
            masked = masks[s] * grad
            total += column[:, j + s : j + s + 1] * pltpu.roll(masked, span - s, 1)
            tap = jnp.sum(masked * pltpu.roll(x, s, 1), axis=1, keepdims=True)
            sums += jnp.where(lane == groups + j + s, tap, 0.0)
        grads[i * chunk : (i + 1) * chunk] = total.astype(bf16)
    marks[...] = jnp.zeros_like(marks)
    marks[:, 0:chunk] = sums.T
    common += pltpu.roll(marks[0:room], me * chunk, 1)
    for s in range(devices):
        to = lax.rem(me + s, devices)
        outs[s][0:body] = grads[:, block_at(to, length)]
        value = small[to] + common
        top = value.astype(bf16)
        outs[s][body : body + room] = top
        outs[s][body + room :] = (value - top.astype(f32)).astype(bf16)


def collect_kernel(devices, groups, rows, stacked, *refs):
    pays, (near, sums) = refs[:devices], refs[devices:]
    me = lax.axis_index("ctx")
    width = pays[0].shape[1]
    blocks = near.shape[1] // width
    body = blocks * rows + (stacked - 1) * (width // devices)
    room = (pays[0].shape[0] - body) // 2
    count = groups * devices
    total = long_rows = None
    for s in range(devices):
        come = lax.rem(me - s + devices, devices)
        for b in range(blocks):
            at = block_at(come, rows)
            near[at, b * width : (b + 1) * width] = pays[s][b * rows : (b + 1) * rows]
        value = pays[s][body : body + room].astype(f32) + pays[s][body + room :].astype(f32)
        row = lax.broadcasted_iota(jnp.int32, value.shape, 0)
        line = pltpu.roll(jnp.where(row < groups, value, 0.0), come * groups, 0)
        long_rows = line if long_rows is None else long_rows + line
        total = value if total is None else total + value
    sums[...] = jnp.zeros_like(sums)
    sums[0:count] = long_rows
    sums[count : count + room - groups] = total[groups:]


def grad_out_kernel(devices, taps, start, query_part, *refs):
    pays, (out, turned) = refs[:devices], refs[devices:]
    me = lax.axis_index("ctx")
    stacked, rows, width = out.shape
    chunk = width // devices
    body = start + (stacked - 1) * chunk
    room = (pays[0].shape[0] - body) // 2
    for s in range(devices):
        at = block_at(lax.rem(me - s + devices, devices), chunk)
        for i in range(stacked - 1):
            turned[i, at] = pays[s][start + i * chunk : start + (i + 1) * chunk]
    last = pays[devices - 1]
    value = last[body : body + room].astype(f32) + last[body + room :].astype(f32)
    row = lax.broadcasted_iota(jnp.int32, value.shape, 0)
    later = jnp.where(row >= room - (taps - 1), value, 0.0)
    query = query_part[...].T
    out[0, 0 : rows - room] = query[0 : rows - room].astype(bf16)
    out[0, rows - room :] = (query[rows - room :] + later).astype(bf16)
    for i in range(stacked - 1):
        out[i + 1] = turned[i].T


def small_out_kernel(scale, mine, other, short_out, long_out):
    total = (mine[...] + other[...]) * scale
    count = long_out.shape[0]
    stacked, taps, _ = short_out.shape
    long_out[...] = total[0:count]
    for i in range(stacked):
        start = count + i * taps
        short_out[i] = total[start : start + taps]


def direct_device(projected, segment_ids, short_filter, long_filter, out_proj, mixed_cotangent):
    devices, parts = lax.axis_size("ctx"), lax.axis_size("tp")
    stacked, _, length, width = projected.shape
    taps = short_filter.shape[1]
    count = long_filter.shape[0]
    groups = count // devices
    chunk = width // devices
    span = length * devices
    total_cols = out_proj.shape[1]
    grad_scale = 1.0 / math.sqrt(projected.shape[1] * lax.axis_size("dp") * span)
    cotangent = mixed_cotangent[0]
    room = 16
    inputs = (projected[:, 0], long_filter, segment_ids)

    outs = on_core(
        functools.partial(pack_kernel, devices),
        [
            (((stacked - 1) * chunk + (2 * room if s == 1 else room), length), bf16)
            for s in range(devices)
        ]
        + [((width, length), bf16)],
        inputs,
        "pack",
        [pltpu.VMEM(a.shape, a.dtype) for a in inputs]
        + [
            pltpu.VMEM((stacked - 1, width, length), bf16),
            pltpu.VMEM((room, length), f32),
            pltpu.SemaphoreType.DMA((len(inputs),)),
        ],
        whole=True,
    )
    signal, query = outs[:devices], outs[devices]
    own, *signal = scatter_chunks(signal, "ctx")
    beside = swap(cotangent, "tp", 1)
    columns, own, query = on_core(
        prepare_kernel,
        [((width, 16), f32), (own.shape, bf16), ((width, length), bf16)],
        (after(short_filter, beside), own, query),
        "prepare",
        [pltpu.VMEM((16, width), f32)],
    )
    signal = [own, *signal]

    conv_flops = 2 * groups * span * span * 64
    outs = on_core(
        functools.partial(conv_kernel, devices, taps),
        [((chunk, length), bf16)] * devices
        + [
            ((stacked - 1, chunk, span), f32),
            (((stacked - 1) * chunk, span), bf16),
            ((8, span), f32),
            ((groups, length, span), bf16),
        ],
        (columns, *signal),
        "conv",
        [
            pltpu.VMEM((room, span), f32),
            pltpu.VMEM((chunk, span), bf16),
            pltpu.VMEM((groups, length, span), bf16),
        ],
        flops=conv_flops,
    )
    longs, kept = outs[:devices], outs[devices:]
    seg = kept[2]
    cots = [cotangent, beside, swap(cotangent, "tp", 2), swap(beside, "tp", 2)]
    outs = on_core(
        functools.partial(grad_y_kernel, devices, parts, taps),
        [((2 * chunk, length), bf16)] * devices + [((width, length), f32)] * 2,
        (out_proj, query, signal[1], columns, seg, *cots, *longs),
        "grad_y",
        [pltpu.VMEM((8 * taps, span), f32), pltpu.VMEM((width, length), bf16)],
        flops=2 * width * length * total_cols,
    )
    pairs, (grad_y, query_conv) = outs[:devices], outs[devices:]
    pairs = scatter_chunks(pairs, "ctx")

    half = width // 2
    y, long, keep, send = on_core(
        functools.partial(weight_grad_kernel, devices, parts),
        [
            ((width, length), bf16),
            ((width, length), f32),
            ((half, total_cols), f32),
            ((half, total_cols), f32),
        ],
        (query_conv, *cots, *pairs),
        "weight_grad",
        [pltpu.VMEM((width, total_cols), f32)],
        flops=2 * width * length * total_cols,
    )
    other = rotate(send, "dp", 1)
    rows = half // devices
    sums = on_core(
        functools.partial(core_sum_kernel, devices),
        [((rows, total_cols), f32)] + [((rows, total_cols), bf16)] * (devices - 1),
        (keep, other),
        "core_sum",
        [pltpu.VMEM((half, total_cols), f32)],
    )
    parts_out = scatter_chunks(sums, "ctx")

    shares = on_core(
        functools.partial(mixed_part_kernel, parts),
        [((length, width), f32)] + [((length, width), bf16)] * (parts - 1),
        (after(y, sums[1]), out_proj),
        "mixed_part",
        [pltpu.VMEM((length, total_cols), f32)],
        flops=2 * width * length * total_cols,
    )
    shares = [shares[0]] + [swap(shares[s], "tp", s) for s in range(1, parts)]
    (mixed,) = on_core(mixed_sum_kernel, [((length, width), bf16)], shares, "mixed_sum")

    outs = on_core(
        functools.partial(backward_kernel, devices, taps),
        [(((stacked - 1) * chunk + 2 * room, length), bf16)] * devices + [((width, length), f32)],
        (*kept, columns, query, signal[1], grad_y, after(long, sums[1]), *pairs),
        "backward",
        [
            pltpu.VMEM((chunk, span), bf16),
            pltpu.VMEM(((stacked - 1) * chunk, span), bf16),
            pltpu.VMEM((devices, room, length), f32),
            pltpu.VMEM((SUB, width), f32),
            pltpu.VMEM((8 * taps, span), f32),
        ],
        flops=2 * conv_flops,
    )
    back, query_part = outs[:devices], outs[devices]
    start = rows * total_cols // width
    back = on_core(
        functools.partial(block_sum_kernel, devices, grad_scale),
        [((start + back[0].shape[0], width), bf16)] * devices,
        (*parts_out, *back),
        "block_sum",
    )
    back = scatter_chunks(back, "ctx")
    back[0] = after(back[0], shares[1:])
    near, small = on_core(
        functools.partial(collect_kernel, devices, groups, rows, stacked),
        [((half, total_cols), bf16), ((count + 16, width), f32)],
        back,
        "collect",
    )
    far = rotate(near, "dp", 1)
    other_small = rotate(small, "dp", 1)
    (grad_projected,) = on_core(
        functools.partial(grad_out_kernel, devices, taps, start),
        [((stacked, length, width), bf16)],
        (query_part, *back),
        "grad_out",
        [pltpu.VMEM((stacked - 1, width, length), bf16)],
    )
    grad_short, grad_long = on_core(
        functools.partial(small_out_kernel, grad_scale),
        [(short_filter.shape, f32), ((count, length), f32)],
        (small, other_small),
        "small_out",
    )
    (grad_out_proj,) = on_core(
        functools.partial(weight_out_kernel, devices),
        [((width, total_cols), f32)],
        (near, far),
        "weight_out",
    )
    return (mixed[None], grad_projected[:, None], grad_short, grad_long, grad_out_proj)


def direct_fits(mesh, projected, short_filter, long_filter):
    devices = mesh.shape["ctx"]
    length = projected.shape[2] // devices
    width = projected.shape[3] // mesh.shape["tp"]
    groups = long_filter.shape[0] // mesh.shape["tp"]
    stacked, taps = short_filter.shape[:2]
    return (
        mesh.shape["dp"] == 2
        and mesh.shape["tp"] == 4
        and projected.shape[1] == 2
        and stacked == 3
        and length == width
        and length % SUB == 0
        and groups % devices == 0
        and groups == 16
        and (width // devices) % 16 == 0
        and width // devices <= SUB
        and (width // groups) == 16
        and 2 * groups // devices + 2 <= 16
        and groups // devices + stacked * taps + taps - 1 <= 16
    )


def solution(mesh):
    in_specs = (
        P(None, "dp", "ctx", "tp"),
        P("dp", "ctx"),
        P(None, None, "tp"),
        P("tp", "ctx"),
        P("tp", None),
        P("dp", "ctx", "tp"),
    )
    out_specs = (
        P("dp", "ctx", "tp"),
        P(None, "dp", "ctx", "tp"),
        P(None, None, "tp"),
        P("tp", "ctx"),
        P("tp", None),
    )

    def layer(projected, segment_ids, short_filter, long_filter, out_proj, mixed_cotangent):
        fits = direct_fits(mesh, projected, short_filter, long_filter)
        return jax.shard_map(
            direct_device if fits else spectral_device,
            mesh=mesh,
            in_specs=in_specs,
            out_specs=out_specs,
            check_vma=False,
        )(projected, segment_ids, short_filter, long_filter, out_proj, mixed_cotangent)

    return layer
```

```python
import functools
import math

import jax
import jax.numpy as jnp
from jax import lax
from jax.experimental import pallas as pl
from jax.experimental.pallas import tpu as pltpu
from jax.sharding import PartitionSpec as P

highest_precision = lax.Precision.HIGHEST


def shifted(value, axis, steps):
    count = lax.axis_size(axis)
    first, last = (max(0, -steps), min(count, count - steps))
    return lax.ppermute(value, axis, [(source, source + steps) for source in range(first, last)])


def angle_table(height, breadth, period, direction):
    product = (
        jnp.arange(height, dtype=jnp.int32)[:, None]
        * jnp.arange(breadth, dtype=jnp.int32)[None, :]
        % period
    )
    angles = direction * 2.0 * math.pi / period * product.astype(jnp.float32)
    return (jnp.cos(angles), jnp.sin(angles))


def row_twiddle(spec_re, spec_im, direction):
    my_index = lax.axis_index("ctx")
    devices = lax.axis_size("ctx")
    row_count = spec_re.shape[1]
    period = 2 * devices * row_count
    freq_pair = 2 * my_index + jnp.arange(2, dtype=jnp.int32)
    product = freq_pair[:, None] * jnp.arange(row_count, dtype=jnp.int32)[None, :] % period
    angles = direction * 2.0 * math.pi / period * product.astype(jnp.float32)
    cosine = jnp.cos(angles)[:, :, None]
    sine_part = jnp.sin(angles)[:, :, None]
    return (spec_re * cosine - spec_im * sine_part, spec_re * sine_part + spec_im * cosine)


def row_transform(spec_re, spec_im, direction):
    row_count = spec_re.shape[1]
    cosine, sine_part = angle_table(row_count, row_count, row_count, direction)

    def along_rows(blocks, matrix):
        return jnp.einsum("kmc,mq->kqc", blocks, matrix, precision=highest_precision)

    return (
        along_rows(spec_re, cosine) - along_rows(spec_im, sine_part),
        along_rows(spec_re, sine_part) + along_rows(spec_im, cosine),
    )


def mixing(matrix, blocks):
    return jnp.einsum("kj,jmc->kmc", matrix, blocks, precision=highest_precision)


def forward_spectrum(real_part):
    devices = lax.axis_size("ctx")
    cosine, sine_part = angle_table(2 * devices, devices, 2 * devices, -1.0)
    spread_re = lax.all_to_all(real_part[None], "ctx", split_axis=1, concat_axis=0, tiled=True)
    column_re = mixing(cosine, spread_re)
    column_im = mixing(sine_part, spread_re)
    near_re, near_im = (
        lax.all_to_all(column_re, "ctx", split_axis=0, concat_axis=1, tiled=True),
        lax.all_to_all(column_im, "ctx", split_axis=0, concat_axis=1, tiled=True),
    )
    twist_re, twist_im = row_twiddle(near_re, near_im, -1.0)
    return row_transform(twist_re, twist_im, -1.0)


def inverse_spectrum(spec_re, spec_im):
    devices = lax.axis_size("ctx")
    row_count = spec_re.shape[1]
    back_re, back_im = row_transform(spec_re, spec_im, 1.0)
    twist_re, twist_im = row_twiddle(back_re / row_count, back_im / row_count, 1.0)
    far_re, far_im = (
        lax.all_to_all(twist_re, "ctx", split_axis=1, concat_axis=0, tiled=True),
        lax.all_to_all(twist_im, "ctx", split_axis=1, concat_axis=0, tiled=True),
    )
    cosine, sine_part = angle_table(devices, 2 * devices, 2 * devices, 1.0)
    out_re = (mixing(cosine, far_re) - mixing(sine_part, far_im)) / (2 * devices)
    rows_re = lax.all_to_all(out_re, "ctx", split_axis=0, concat_axis=1, tiled=True)
    return (rows_re[0], rows_re[0])


def pack_columns(values):
    return (values, values)


def by_filter(val_re, val_im, fil_re, fil_im, conjugate):
    val_shape = val_re.shape
    group_count = fil_re.shape[2]
    v_re = val_re.reshape(val_shape[0], val_shape[1], group_count, -1)
    v_im = val_im.reshape(val_shape[0], val_shape[1], group_count, -1)
    f_re = fil_re[:, :, :, None]
    f_im = fil_im[:, :, :, None]
    if conjugate:
        f_im = -f_im
    out_re = v_re * f_re - v_im * f_im
    out_im = v_re * f_im + v_im * f_re
    return (out_re.reshape(val_shape), out_im.reshape(val_shape))


def short_local(extended, filters, seg_ext):
    reach_taps = filters.shape[1]
    out_rows = extended.shape[1] - reach_taps + 1
    own_seg = seg_ext[reach_taps - 1 :]
    running = jnp.zeros((extended.shape[0], out_rows, extended.shape[2]), jnp.float32)
    for shift_by in range(reach_taps):
        start_row = reach_taps - 1 - shift_by
        same_doc = jnp.where(seg_ext[start_row : start_row + out_rows] == own_seg, 1.0, 0.0)
        running = (
            running
            + filters[:, shift_by][:, None, :]
            * same_doc[None, :, None]
            * extended[:, start_row : start_row + out_rows]
        )
    return running


def spectral_device(projected, segment_ids, short_filter, long_filter, out_proj, mixed_cotangent):
    row_count = projected.shape[2]
    stacked = projected.shape[0]
    width_dev = projected.shape[3]
    short_reach = short_filter.shape[1]
    group_count = long_filter.shape[0]
    grad_scale = 1.0 / math.sqrt(
        projected.shape[1] * lax.axis_size("dp") * row_count * lax.axis_size("ctx")
    )
    segments = segment_ids[0]
    source = projected[:, 0]
    short_rows = short_reach - 1
    cot_full = lax.all_gather(mixed_cotangent[0], "tp", axis=1, tiled=True)
    prev_tail, prev_seg = shifted(
        (source[:, row_count - short_rows :], segments[row_count - short_rows :]), "ctx", 1
    )
    short_seg = jnp.concatenate([prev_seg, segments])
    short_ext = jnp.concatenate([prev_tail, source], axis=1).astype(jnp.float32)

    def short_piece(extended, filters):
        return short_local(extended, filters, short_seg)

    short_out, short_pull = jax.vjp(short_piece, short_ext, short_filter)
    query_conv = short_out[0]
    gated_rows = short_out[1] * short_out[2]
    filter_cols = long_filter.T
    mid_re, mid_im = pack_columns(gated_rows)
    spec_re, spec_im = forward_spectrum(jnp.concatenate([mid_re, filter_cols], axis=1))
    data_cols = spec_re.shape[2] - group_count
    signal_re = spec_re[:, :, :data_cols]
    signal_im = spec_im[:, :, :data_cols]
    filt_re = spec_re[:, :, data_cols:]
    filt_im = spec_im[:, :, data_cols:]
    long_re, long_im = by_filter(signal_re, signal_im, filt_re, filt_im, False)
    out_re, out_im = inverse_spectrum(long_re, long_im)
    y_out = (query_conv * out_re).astype(jnp.bfloat16)
    partial_out = jnp.dot(y_out, out_proj, preferred_element_type=jnp.float32)
    mixed = lax.psum_scatter(partial_out, "tp", scatter_dimension=1, tiled=True).astype(
        jnp.bfloat16
    )
    grad_y = jnp.dot(cot_full, out_proj.T, preferred_element_type=jnp.float32)
    grad_proj_local = jnp.dot(y_out.T, cot_full, preferred_element_type=jnp.float32)
    grad_long_out = grad_y * query_conv
    grad_query = grad_y * out_re
    grad_in_re, grad_in_im = pack_columns(grad_long_out)
    cot_re, cot_im = forward_spectrum(grad_in_re)
    back_re, back_im = by_filter(cot_re, cot_im, filt_re, filt_im, True)
    cross_re = (
        (signal_re * cot_re + signal_im * cot_im).reshape(2, row_count, group_count, -1).sum(axis=3)
    )
    cross_im = (
        (signal_re * cot_im - signal_im * cot_re).reshape(2, row_count, group_count, -1).sum(axis=3)
    )
    inv_re, inv_im = inverse_spectrum(
        jnp.concatenate([back_re, cross_re], axis=2), jnp.concatenate([back_im, cross_im], axis=2)
    )
    grad_gated = inv_re[:, :data_cols]
    grad_long_local = inv_re[:, data_cols:].T
    grad_short_out = jnp.stack([grad_query, grad_gated * short_out[2], grad_gated * short_out[1]])
    grad_short_ext, grad_short_local = short_pull(grad_short_out)
    returned_short = shifted(grad_short_ext[:, :short_rows], "ctx", -1)
    grad_source = grad_short_ext[:, short_rows:] + jnp.concatenate(
        [jnp.zeros((stacked, row_count - short_rows, width_dev), jnp.float32), returned_short],
        axis=1,
    )
    total_proj, total_short = lax.psum((grad_proj_local, grad_short_local), ("ctx", "dp"))
    total_long = lax.psum(grad_long_local, "dp")
    return (
        mixed[None],
        grad_source[:, None].astype(jnp.bfloat16),
        total_short * grad_scale,
        total_long * grad_scale,
        total_proj * grad_scale,
    )


bf16 = jnp.bfloat16
f32 = jnp.float32
SUB = 128


def split_bf16(value):
    high = value.astype(bf16)
    return high, (value - high.astype(f32)).astype(bf16)


def rotate(value, axis, steps):
    count = lax.axis_size(axis)
    return lax.ppermute(value, axis, [(i, (i + steps) % count) for i in range(count)])


def swap(value, axis, bits):
    return lax.ppermute(value, axis, [(i, i ^ bits) for i in range(lax.axis_size(axis))])


def scatter_chunks(chunks, axis):
    return [chunks[0]] + [rotate(chunks[s], axis, s) for s in range(1, len(chunks))]


def after(value, other):
    return lax.optimization_barrier((value, other))[0]


def spread(value, axis):
    return [value] + [rotate(value, axis, s) for s in range(1, lax.axis_size(axis))]


def on_core(kernel, outs, args, name, scratch=(), flops=0, whole=False):
    moved = sum(a.size * a.dtype.itemsize for a in args)
    moved += sum(math.prod(shape) * jnp.dtype(kind).itemsize for shape, kind in outs)
    return pl.pallas_call(
        kernel,
        out_shape=[jax.ShapeDtypeStruct(shape, kind) for shape, kind in outs],
        in_specs=[pl.BlockSpec(memory_space=pltpu.HBM) if whole else pl.BlockSpec()] * len(args),
        scratch_shapes=list(scratch),
        compiler_params=pltpu.CompilerParams(vmem_limit_bytes=(63 if whole else 40) * 1024 * 1024),
        cost_estimate=pl.CostEstimate(flops=flops, bytes_accessed=moved, transcendentals=0),
        name=name,
    )(*args)


def block_at(index, size):
    return pl.ds(pl.multiple_of(index * size, size), size)


def pack_kernel(devices, *refs):
    sources, refs = refs[:3], refs[3:]
    outs, query, refs = refs[:devices], refs[devices], refs[devices + 1 :]
    held, (turned, small, sems) = refs[:3], refs[3:]
    copies = [
        pltpu.make_async_copy(sources[n], held[n], sems.at[n]) for n in range(len(sources))
    ]
    for copy in copies:
        copy.start()
    projected, filters, segments = held
    me = lax.axis_index("ctx")
    stacked, rows, width = projected.shape
    chunk = width // devices
    count = filters.shape[0]
    groups = count // devices
    for copy in copies:
        copy.wait()
    for i in range(1, stacked):
        turned[i - 1] = projected[i].T
    query[...] = projected[0].T
    small[...] = jnp.zeros_like(small)
    seg = segments[...]
    small[2 * groups : 2 * groups + 1] = (seg >> 8).astype(f32)
    small[2 * groups + 1 : 2 * groups + 2] = (seg & 255).astype(f32)
    body = (stacked - 1) * chunk
    for s in range(devices):
        to = lax.rem(me + s, devices)
        for i in range(stacked - 1):
            outs[s][i * chunk : (i + 1) * chunk] = turned[i, block_at(to, chunk)]
        lines = pltpu.roll(filters[...], lax.rem(count - to * groups, count), 0)[0:groups]
        high = lines.astype(bf16).astype(f32)
        small[0:groups] = high
        small[groups : 2 * groups] = lines - high
        outs[s][body : body + 16] = small[...].astype(bf16)
    outs[1][body + 16 :] = projected[0, rows - 16 :]


def prepare_kernel(short_filter, chunk, query, columns, chunk_out, query_out, flat):
    stacked, taps, _ = short_filter.shape
    flat[...] = jnp.zeros_like(flat)
    for i in range(stacked):
        flat[i * taps : (i + 1) * taps] = short_filter[i]
    columns[...] = flat[...].T
    chunk_out[...] = chunk[...]
    query_out[...] = query[...]


def tap_masks(seg, taps):
    wide = jnp.broadcast_to(seg, (8, seg.shape[1]))
    place = lax.broadcasted_iota(jnp.int32, wide.shape, 1)
    masks = [None]
    for s in range(1, taps):
        same = (wide == pltpu.roll(wide, s, 1)) & (place >= s)
        masks.append(jnp.where(same, 1.0, 0.0)[0:1])
    return masks


def block_masks(seg, taps, place, me, length):
    masks = tap_masks(seg, taps)
    for s in range(1, taps):
        place[8 * s : 8 * (s + 1)] = jnp.broadcast_to(masks[s], (8, seg.shape[1]))
    return [None] + [place[8 * s : 8 * s + 8, block_at(me, length)][0:1] for s in range(1, taps)]


def query_shifts(query, previous, taps):
    halo = previous[previous.shape[0] - 16 :]
    before = jnp.concatenate([jnp.zeros((SUB - 16, halo.shape[1]), f32), halo.astype(f32)], axis=0)
    wide = jnp.concatenate([before.T, query.astype(f32)], axis=1)
    return [wide[:, SUB:]] + [pltpu.roll(wide, s, 1)[:, SUB:] for s in range(1, taps)]


def conv_kernel(devices, taps, columns, *rest):
    pays, rest = rest[:devices], rest[devices:]
    outs, rest = rest[:devices], rest[devices:]
    conv, source, seg_out, toeplitz, small, long, rests = rest
    me = lax.axis_index("ctx")
    stacked, chunk, span = conv.shape
    length = span // devices
    groups = toeplitz.shape[0]
    size = chunk // groups
    body = stacked * chunk
    for s in range(devices):
        at = block_at(lax.rem(me - s + devices, devices), length)
        source[:, at] = pays[s][0:body]
        small[:, at] = pays[s][body : body + 16].astype(f32)
    seg = small[2 * groups : 2 * groups + 1] * 256.0 + small[2 * groups + 1 : 2 * groups + 2]
    seg_out[...] = jnp.broadcast_to(seg, seg_out.shape)
    masks = tap_masks(seg, taps)
    column = columns[block_at(me, chunk)]
    for i in range(stacked):
        x = source[i * chunk : (i + 1) * chunk].astype(f32)
        j = (i + 1) * taps
        total = column[:, j : j + 1] * x
        for s in range(1, taps):
            total += column[:, j + s : j + s + 1] * (masks[s] * pltpu.roll(x, s, 1))
        conv[i] = total
    high, low = split_bf16(conv[0] * conv[1])
    for g in range(groups):
        line = small[g : g + 1] + small[groups + g : groups + g + 1]
        padded = jnp.concatenate([line, jnp.zeros((1, SUB), f32)], axis=1)
        turned = pltpu.roll(
            jnp.broadcast_to(padded, (SUB, span + SUB)), 0, 1, stride=1, stride_axis=0
        )[:, :span]
        for half, into in zip(split_bf16(turned), (toeplitz, rests)):
            for r in range(length // SUB):
                rows = slice(r * SUB, (r + 1) * SUB)
                if r:
                    into[g, rows, : r * SUB] = jnp.zeros((SUB, r * SUB), bf16)
                into[g, rows, r * SUB :] = half[:, : span - r * SUB]
        own = slice(g * size, (g + 1) * size)
        pieces = []
        for j in range(devices):
            at = slice(j * length, (j + 1) * length)
            pieces += [high[own, at], low[own, at]]
        stack = jnp.concatenate(pieces, axis=0)
        totals = [None] * devices
        for lag in range(devices):
            lhs = stack[: 2 * size * (devices - lag)]
            at = slice(lag * length, (lag + 1) * length)
            part = jnp.dot(lhs, toeplitz[g, :, at], preferred_element_type=f32)
            part += jnp.dot(lhs, rests[g, :, at], preferred_element_type=f32)
            for j in range(devices - lag):
                term = part[2 * size * j : 2 * size * j + size]
                term += part[2 * size * j + size : 2 * size * (j + 1)]
                i = j + lag
                totals[i] = term if totals[i] is None else totals[i] + term
        for i in range(devices):
            long[own, i * length : (i + 1) * length] = totals[i].astype(bf16)
    for s in range(devices):
        outs[s][...] = long[:, block_at(lax.rem(me + s, devices), length)]


def grad_y_kernel(devices, parts, taps, weights, query, previous, columns, seg, *rest):
    cots, rest = rest[:parts], rest[parts:]
    longs, rest = rest[:devices], rest[devices:]
    outs, (grad_y, query_conv, place, full) = rest[:devices], rest[devices:]
    me, mine = lax.axis_index("ctx"), lax.axis_index("tp")
    rows, width = cots[0].shape
    chunk = width // devices
    masks = block_masks(seg[0:1], taps, place, me, rows)
    shifts = query_shifts(query[...], previous, taps)
    conv = columns[:, 0:1] * shifts[0]
    for s in range(1, taps):
        conv += columns[:, s : s + 1] * (masks[s] * shifts[s])
    query_conv[...] = conv
    total = None
    for s in range(parts):
        cot = cots[s][...]
        lhs = weights[:, block_at(mine ^ s, width)]
        term = lax.dot_general(lhs, cot, (((1,), (1,)), ((), ())), preferred_element_type=f32)
        total = term if total is None else total + term
    grad_y[...] = total
    full[...] = (total * conv).astype(bf16)
    for s in range(devices):
        outs[s][0:chunk] = longs[s][...]
        outs[s][chunk:] = full[block_at(lax.rem(me + s, devices), chunk)]


def weight_grad_kernel(devices, parts, query_conv, *rest):
    cots, rest = rest[:parts], rest[parts:]
    longs, rest = rest[:devices], rest[devices:]
    y_out, long_out, keep, send, full = rest
    me, mine, core = lax.axis_index("ctx"), lax.axis_index("tp"), lax.axis_index("dp")
    rows, width = cots[0].shape
    chunk = width // devices
    half = width // 2
    for s in range(devices):
        at = block_at(lax.rem(me - s + devices, devices), chunk)
        long_out[at] = longs[s][0:chunk].astype(f32)
    y = (query_conv[...] * long_out[...]).astype(bf16)
    y_out[...] = y
    for s in range(parts):
        cot = cots[s][...]
        at = block_at(mine ^ s, width)
        full[:, at] = jnp.dot(y, cot, preferred_element_type=f32)
    keep[...] = full[block_at(core, half)]
    send[...] = full[block_at(1 - core, half)]


def core_sum_kernel(devices, keep, other, *rest):
    outs, (full,) = rest[:devices], rest[devices:]
    me = lax.axis_index("ctx")
    rows = keep.shape[0] // devices
    full[...] = keep[...] + other[...].astype(f32)
    for s in range(devices):
        at = block_at(lax.rem(me + s, devices), rows)
        outs[s][...] = full[at].astype(outs[s].dtype)


def block_sum_kernel(devices, scale, *refs):
    sums, refs = refs[:devices], refs[devices:]
    pays, outs = refs[:devices], refs[devices:]
    total = sums[0][...]
    for s in range(1, devices):
        total += sums[s][...].astype(f32)
    total = (total * scale).astype(bf16)
    rows, width = total.shape[0], outs[0].shape[1]
    blocks = total.shape[1] // width
    for s in range(devices):
        for b in range(blocks):
            outs[s][b * rows : (b + 1) * rows] = total[:, b * width : (b + 1) * width]
        outs[s][blocks * rows :] = pays[s][...]


def mixed_part_kernel(parts, y, weights, *rest):
    outs, (full,) = rest[:parts], rest[parts:]
    mine = lax.axis_index("tp")
    width = outs[0].shape[1]
    full[...] = lax.dot_general(
        y[...], weights[...], (((0,), (0,)), ((), ())), preferred_element_type=f32
    )
    for s in range(parts):
        outs[s][...] = full[:, block_at(mine ^ s, width)].astype(outs[s].dtype)


def mixed_sum_kernel(*refs):
    total = refs[0][...]
    for ref in refs[1:-1]:
        total += ref[...].astype(f32)
    refs[-1][...] = total.astype(bf16)


def backward_kernel(
    devices, taps, conv, source, seg, toeplitz, columns, query, previous, grad_y, long, *rest
):
    glos, rest = rest[:devices], rest[devices:]
    outs, (query_out, grad_long_out, grads, small, marks, place) = rest[:devices], rest[devices:]
    me = lax.axis_index("ctx")
    stacked, chunk, span = conv.shape
    length = span // devices
    groups = toeplitz.shape[0]
    size = chunk // groups
    body = stacked * chunk
    width = query.shape[0]
    room = small.shape[1]

    own_masks = block_masks(seg[0:1], taps, place, me, length)
    shifts = query_shifts(query[...], previous, taps)
    grad = grad_y[...] * long[...]
    total = columns[:, 0:1] * grad
    lane = lax.broadcasted_iota(jnp.int32, (width, SUB), 1)
    position = lax.broadcasted_iota(jnp.int32, (width, length), 1)
    sums = jnp.where(lane == groups, jnp.sum(grad * shifts[0], axis=1, keepdims=True), 0.0)
    early = jnp.zeros((width, SUB), f32)
    for s in range(1, taps):
        masked = own_masks[s] * grad
        back = pltpu.roll(columns[:, s : s + 1] * masked, length - s, 1)
        total += jnp.where(position < length - s, back, 0.0)
        early += jnp.where(position >= length - s, back, 0.0)[:, length - SUB :]
        tap = jnp.sum(masked * shifts[s], axis=1, keepdims=True)
        sums += jnp.where(lane == groups + s, tap, 0.0)
    query_out[...] = total
    common = sums.T[0:room] + early.T[SUB - room :]

    for s in range(devices):
        at = block_at(lax.rem(me - s + devices, devices), length)
        grad_long_out[:, at] = glos[s][chunk:]
    masks = tap_masks(seg[0:1], taps)
    column = columns[block_at(me, chunk)]
    high = grad_long_out[...]
    gated = (conv[0] * conv[1]).astype(bf16)
    gg_parts = []
    corner = lax.broadcasted_iota(jnp.int32, (SUB, SUB), 0)
    corner += lax.broadcasted_iota(jnp.int32, (SUB, SUB), 1)
    flip = jnp.where(corner == SUB - 1, 1.0, 0.0).astype(bf16)
    subs = span // SUB
    small[...] = jnp.zeros_like(small)
    for g in range(groups):
        own = slice(g * size, (g + 1) * size)
        stack = jnp.concatenate(
            [high[own, i * length : (i + 1) * length] for i in range(devices)], axis=0
        )
        totals = [None] * devices
        for lag in range(devices):
            part = lax.dot_general(
                stack[size * lag :],
                toeplitz[g, :, lag * length : (lag + 1) * length],
                (((1,), (1,)), ((), ())),
                preferred_element_type=f32,
            )
            for j in range(devices - lag):
                term = part[size * j : size * (j + 1)]
                totals[j] = term if totals[j] is None else totals[j] + term
        gg_parts.append(jnp.concatenate(totals, axis=1))
        left = jnp.concatenate([gated[own, j * SUB : (j + 1) * SUB] for j in range(subs)], axis=0)
        right = jnp.concatenate([high[own, j * SUB : (j + 1) * SUB] for j in range(subs)], axis=0)
        turned = lax.dot_general(
            flip, left, (((1,), (1,)), ((), ())), preferred_element_type=f32
        ).astype(bf16)
        lines = []
        for lag in range(subs):
            cross = jnp.dot(
                turned[:, : size * (subs - lag)], right[size * lag :], preferred_element_type=f32
            )
            wide = jnp.concatenate([cross, jnp.zeros((SUB, SUB), f32)], axis=1)
            wide = pltpu.roll(wide, 1, 1, stride=1, stride_axis=0)
            lines.append(jnp.sum(wide, axis=0, keepdims=True))
        per = length // SUB
        for lag in range(subs):
            line = lines[lag][:, SUB:]
            if lag + 1 < subs:
                line += lines[lag + 1][:, :SUB]
            b, within = divmod(lag, per)
            small[b, g : g + 1, within * SUB : (within + 1) * SUB] = line
    grad_gated = jnp.concatenate(gg_parts, axis=0)
    lane = lax.broadcasted_iota(jnp.int32, (chunk, SUB), 1)
    sums = jnp.zeros((chunk, SUB), f32)
    for i in range(stacked):
        grad = grad_gated * conv[1 - i]
        x = source[i * chunk : (i + 1) * chunk].astype(f32)
        j = (i + 1) * taps
        total = column[:, j : j + 1] * grad
        tap = jnp.sum(grad * x, axis=1, keepdims=True)
        sums += jnp.where(lane == groups + j, tap, 0.0)
        for s in range(1, taps):
            masked = masks[s] * grad
            total += column[:, j + s : j + s + 1] * pltpu.roll(masked, span - s, 1)
            tap = jnp.sum(masked * pltpu.roll(x, s, 1), axis=1, keepdims=True)
            sums += jnp.where(lane == groups + j + s, tap, 0.0)
        grads[i * chunk : (i + 1) * chunk] = total.astype(bf16)
    marks[...] = jnp.zeros_like(marks)
    marks[:, 0:chunk] = sums.T
    common += pltpu.roll(marks[0:room], me * chunk, 1)
    for s in range(devices):
        to = lax.rem(me + s, devices)
        outs[s][0:body] = grads[:, block_at(to, length)]
        value = small[to] + common
        top = value.astype(bf16)
        outs[s][body : body + room] = top
        outs[s][body + room :] = (value - top.astype(f32)).astype(bf16)


def collect_kernel(devices, groups, rows, stacked, *refs):
    pays, (near, sums) = refs[:devices], refs[devices:]
    me = lax.axis_index("ctx")
    width = pays[0].shape[1]
    blocks = near.shape[1] // width
    body = blocks * rows + (stacked - 1) * (width // devices)
    room = (pays[0].shape[0] - body) // 2
    count = groups * devices
    total = long_rows = None
    for s in range(devices):
        come = lax.rem(me - s + devices, devices)
        for b in range(blocks):
            at = block_at(come, rows)
            near[at, b * width : (b + 1) * width] = pays[s][b * rows : (b + 1) * rows]
        value = pays[s][body : body + room].astype(f32) + pays[s][body + room :].astype(f32)
        row = lax.broadcasted_iota(jnp.int32, value.shape, 0)
        line = pltpu.roll(jnp.where(row < groups, value, 0.0), come * groups, 0)
        long_rows = line if long_rows is None else long_rows + line
        total = value if total is None else total + value
    sums[...] = jnp.zeros_like(sums)
    sums[0:count] = long_rows
    sums[count : count + room - groups] = total[groups:]


def grad_out_kernel(devices, taps, start, query_part, *refs):
    pays, (out, turned) = refs[:devices], refs[devices:]
    me = lax.axis_index("ctx")
    stacked, rows, width = out.shape
    chunk = width // devices
    body = start + (stacked - 1) * chunk
    room = (pays[0].shape[0] - body) // 2
    for s in range(devices):
        at = block_at(lax.rem(me - s + devices, devices), chunk)
        for i in range(stacked - 1):
            turned[i, at] = pays[s][start + i * chunk : start + (i + 1) * chunk]
    last = pays[devices - 1]
    value = last[body : body + room].astype(f32) + last[body + room :].astype(f32)
    row = lax.broadcasted_iota(jnp.int32, value.shape, 0)
    later = jnp.where(row >= room - (taps - 1), value, 0.0)
    query = query_part[...].T
    out[0, 0 : rows - room] = query[0 : rows - room].astype(bf16)
    out[0, rows - room :] = (query[rows - room :] + later).astype(bf16)
    for i in range(stacked - 1):
        out[i + 1] = turned[i].T


def final_kernel(scale, near, far, mine, other, weight_out, short_out, long_out):
    core = lax.axis_index("dp")
    half = near.shape[0]
    weight_out[block_at(core, half)] = near[...].astype(f32)
    weight_out[block_at(1 - core, half)] = far[...].astype(f32)
    total = (mine[...] + other[...]) * scale
    count = long_out.shape[0]
    stacked, taps, _ = short_out.shape
    long_out[...] = total[0:count]
    for i in range(stacked):
        start = count + i * taps
        short_out[i] = total[start : start + taps]


def direct_device(projected, segment_ids, short_filter, long_filter, out_proj, mixed_cotangent):
    devices, parts = lax.axis_size("ctx"), lax.axis_size("tp")
    stacked, _, length, width = projected.shape
    taps = short_filter.shape[1]
    count = long_filter.shape[0]
    groups = count // devices
    chunk = width // devices
    span = length * devices
    total_cols = out_proj.shape[1]
    grad_scale = 1.0 / math.sqrt(projected.shape[1] * lax.axis_size("dp") * span)
    cotangent = mixed_cotangent[0]
    room = 16
    inputs = (projected[:, 0], long_filter, segment_ids)

    outs = on_core(
        functools.partial(pack_kernel, devices),
        [
            (((stacked - 1) * chunk + (2 * room if s == 1 else room), length), bf16)
            for s in range(devices)
        ]
        + [((width, length), bf16)],
        inputs,
        "pack",
        [pltpu.VMEM(a.shape, a.dtype) for a in inputs]
        + [
            pltpu.VMEM((stacked - 1, width, length), bf16),
            pltpu.VMEM((room, length), f32),
            pltpu.SemaphoreType.DMA((len(inputs),)),
        ],
        whole=True,
    )
    signal, query = outs[:devices], outs[devices]
    own, *signal = scatter_chunks(signal, "ctx")
    beside = swap(cotangent, "tp", 1)
    columns, own, query = on_core(
        prepare_kernel,
        [((width, 16), f32), (own.shape, bf16), ((width, length), bf16)],
        (after(short_filter, beside), own, query),
        "prepare",
        [pltpu.VMEM((16, width), f32)],
    )
    signal = [own, *signal]

    conv_flops = 2 * groups * span * span * 64
    outs = on_core(
        functools.partial(conv_kernel, devices, taps),
        [((chunk, length), bf16)] * devices
        + [
            ((stacked - 1, chunk, span), f32),
            (((stacked - 1) * chunk, span), bf16),
            ((8, span), f32),
            ((groups, length, span), bf16),
        ],
        (columns, *signal),
        "conv",
        [
            pltpu.VMEM((room, span), f32),
            pltpu.VMEM((chunk, span), bf16),
            pltpu.VMEM((groups, length, span), bf16),
        ],
        flops=conv_flops,
    )
    longs, kept = outs[:devices], outs[devices:]
    seg = kept[2]
    cots = [cotangent, beside, swap(cotangent, "tp", 2), swap(beside, "tp", 2)]
    outs = on_core(
        functools.partial(grad_y_kernel, devices, parts, taps),
        [((2 * chunk, length), bf16)] * devices + [((width, length), f32)] * 2,
        (out_proj, query, signal[1], columns, seg, *cots, *longs),
        "grad_y",
        [pltpu.VMEM((8 * taps, span), f32), pltpu.VMEM((width, length), bf16)],
        flops=2 * width * length * total_cols,
    )
    pairs, (grad_y, query_conv) = outs[:devices], outs[devices:]
    pairs = scatter_chunks(pairs, "ctx")

    half = width // 2
    y, long, keep, send = on_core(
        functools.partial(weight_grad_kernel, devices, parts),
        [
            ((width, length), bf16),
            ((width, length), f32),
            ((half, total_cols), f32),
            ((half, total_cols), f32),
        ],
        (query_conv, *cots, *pairs),
        "weight_grad",
        [pltpu.VMEM((width, total_cols), f32)],
        flops=2 * width * length * total_cols,
    )
    other = rotate(send, "dp", 1)
    shares = on_core(
        functools.partial(mixed_part_kernel, parts),
        [((length, width), f32)] + [((length, width), bf16)] * (parts - 1),
        (y, out_proj),
        "mixed_part",
        [pltpu.VMEM((length, total_cols), f32)],
        flops=2 * width * length * total_cols,
    )
    keep = after(keep, shares[0])
    rows = half // devices
    sums = on_core(
        functools.partial(core_sum_kernel, devices),
        [((rows, total_cols), f32)] + [((rows, total_cols), bf16)] * (devices - 1),
        (keep, other),
        "core_sum",
        [pltpu.VMEM((half, total_cols), f32)],
    )
    parts_out = scatter_chunks(sums, "ctx")

    outs = on_core(
        functools.partial(backward_kernel, devices, taps),
        [(((stacked - 1) * chunk + 2 * room, length), bf16)] * devices + [((width, length), f32)],
        (*kept, columns, query, signal[1], grad_y, after(long, sums[1]), *pairs),
        "backward",
        [
            pltpu.VMEM((chunk, span), bf16),
            pltpu.VMEM(((stacked - 1) * chunk, span), bf16),
            pltpu.VMEM((devices, room, length), f32),
            pltpu.VMEM((SUB, width), f32),
            pltpu.VMEM((8 * taps, span), f32),
        ],
        flops=2 * conv_flops,
    )
    back, query_part = outs[:devices], outs[devices]
    start = rows * total_cols // width
    back = on_core(
        functools.partial(block_sum_kernel, devices, grad_scale),
        [((start + back[0].shape[0], width), bf16)] * devices,
        (*parts_out, *back),
        "block_sum",
    )
    shares = [shares[0]] + [
        swap(shares[s], "tp", s) for s in range(1, parts)
    ]
    (mixed,) = on_core(mixed_sum_kernel, [((length, width), bf16)], shares, "mixed_sum")
    back = scatter_chunks(back, "ctx")
    back[0] = after(back[0], mixed)
    near, small = on_core(
        functools.partial(collect_kernel, devices, groups, rows, stacked),
        [((half, total_cols), bf16), ((count + 16, width), f32)],
        back,
        "collect",
    )
    far = rotate(near, "dp", 1)
    other_small = rotate(small, "dp", 1)
    (grad_projected,) = on_core(
        functools.partial(grad_out_kernel, devices, taps, start),
        [((stacked, length, width), bf16)],
        (query_part, *back),
        "grad_out",
        [pltpu.VMEM((stacked - 1, width, length), bf16)],
    )
    grad_out_proj, grad_short, grad_long = on_core(
        functools.partial(final_kernel, grad_scale),
        [((width, total_cols), f32), (short_filter.shape, f32), ((count, length), f32)],
        (near, far, after(small, grad_projected), other_small),
        "final",
    )
    return (mixed[None], grad_projected[:, None], grad_short, grad_long, grad_out_proj)


def direct_fits(mesh, projected, short_filter, long_filter):
    devices = mesh.shape["ctx"]
    length = projected.shape[2] // devices
    width = projected.shape[3] // mesh.shape["tp"]
    groups = long_filter.shape[0] // mesh.shape["tp"]
    stacked, taps = short_filter.shape[:2]
    return (
        mesh.shape["dp"] == 2
        and mesh.shape["tp"] == 4
        and projected.shape[1] == 2
        and stacked == 3
        and length == width
        and length % SUB == 0
        and groups % devices == 0
        and groups == 16
        and (width // devices) % 16 == 0
        and width // devices <= SUB
        and (width // groups) == 16
        and 2 * groups // devices + 2 <= 16
        and groups // devices + stacked * taps + taps - 1 <= 16
    )


def solution(mesh):
    in_specs = (
        P(None, "dp", "ctx", "tp"),
        P("dp", "ctx"),
        P(None, None, "tp"),
        P("tp", "ctx"),
        P("tp", None),
        P("dp", "ctx", "tp"),
    )
    out_specs = (
        P("dp", "ctx", "tp"),
        P(None, "dp", "ctx", "tp"),
        P(None, None, "tp"),
        P("tp", "ctx"),
        P("tp", None),
    )

    def layer(projected, segment_ids, short_filter, long_filter, out_proj, mixed_cotangent):
        fits = direct_fits(mesh, projected, short_filter, long_filter)
        return jax.shard_map(
            direct_device if fits else spectral_device,
            mesh=mesh,
            in_specs=in_specs,
            out_specs=out_specs,
            check_vma=False,
        )(projected, segment_ids, short_filter, long_filter, out_proj, mixed_cotangent)

    return layer
```

```python
import functools
import math

import jax
import jax.numpy as jnp
from jax import lax
from jax.experimental import pallas as pl
from jax.experimental.pallas import tpu as pltpu
from jax.sharding import PartitionSpec as P

highest_precision = lax.Precision.HIGHEST


def shifted(value, axis, steps):
    count = lax.axis_size(axis)
    first, last = (max(0, -steps), min(count, count - steps))
    return lax.ppermute(value, axis, [(source, source + steps) for source in range(first, last)])


def angle_table(height, breadth, period, direction):
    product = (
        jnp.arange(height, dtype=jnp.int32)[:, None]
        * jnp.arange(breadth, dtype=jnp.int32)[None, :]
        % period
    )
    angles = direction * 2.0 * math.pi / period * product.astype(jnp.float32)
    return (jnp.cos(angles), jnp.sin(angles))


def row_twiddle(spec_re, spec_im, direction):
    my_index = lax.axis_index("ctx")
    devices = lax.axis_size("ctx")
    row_count = spec_re.shape[1]
    period = 2 * devices * row_count
    freq_pair = 2 * my_index + jnp.arange(2, dtype=jnp.int32)
    product = freq_pair[:, None] * jnp.arange(row_count, dtype=jnp.int32)[None, :] % period
    angles = direction * 2.0 * math.pi / period * product.astype(jnp.float32)
    cosine = jnp.cos(angles)[:, :, None]
    sine_part = jnp.sin(angles)[:, :, None]
    return (spec_re * cosine - spec_im * sine_part, spec_re * sine_part + spec_im * cosine)


def row_transform(spec_re, spec_im, direction):
    row_count = spec_re.shape[1]
    cosine, sine_part = angle_table(row_count, row_count, row_count, direction)

    def along_rows(blocks, matrix):
        return jnp.einsum("kmc,mq->kqc", blocks, matrix, precision=highest_precision)

    return (
        along_rows(spec_re, cosine) - along_rows(spec_im, sine_part),
        along_rows(spec_re, sine_part) + along_rows(spec_im, cosine),
    )


def mixing(matrix, blocks):
    return jnp.einsum("kj,jmc->kmc", matrix, blocks, precision=highest_precision)


def forward_spectrum(real_part):
    devices = lax.axis_size("ctx")
    cosine, sine_part = angle_table(2 * devices, devices, 2 * devices, -1.0)
    spread_re = lax.all_to_all(real_part[None], "ctx", split_axis=1, concat_axis=0, tiled=True)
    column_re = mixing(cosine, spread_re)
    column_im = mixing(sine_part, spread_re)
    near_re, near_im = (
        lax.all_to_all(column_re, "ctx", split_axis=0, concat_axis=1, tiled=True),
        lax.all_to_all(column_im, "ctx", split_axis=0, concat_axis=1, tiled=True),
    )
    twist_re, twist_im = row_twiddle(near_re, near_im, -1.0)
    return row_transform(twist_re, twist_im, -1.0)


def inverse_spectrum(spec_re, spec_im):
    devices = lax.axis_size("ctx")
    row_count = spec_re.shape[1]
    back_re, back_im = row_transform(spec_re, spec_im, 1.0)
    twist_re, twist_im = row_twiddle(back_re / row_count, back_im / row_count, 1.0)
    far_re, far_im = (
        lax.all_to_all(twist_re, "ctx", split_axis=1, concat_axis=0, tiled=True),
        lax.all_to_all(twist_im, "ctx", split_axis=1, concat_axis=0, tiled=True),
    )
    cosine, sine_part = angle_table(devices, 2 * devices, 2 * devices, 1.0)
    out_re = (mixing(cosine, far_re) - mixing(sine_part, far_im)) / (2 * devices)
    rows_re = lax.all_to_all(out_re, "ctx", split_axis=0, concat_axis=1, tiled=True)
    return (rows_re[0], rows_re[0])


def pack_columns(values):
    return (values, values)


def by_filter(val_re, val_im, fil_re, fil_im, conjugate):
    val_shape = val_re.shape
    group_count = fil_re.shape[2]
    v_re = val_re.reshape(val_shape[0], val_shape[1], group_count, -1)
    v_im = val_im.reshape(val_shape[0], val_shape[1], group_count, -1)
    f_re = fil_re[:, :, :, None]
    f_im = fil_im[:, :, :, None]
    if conjugate:
        f_im = -f_im
    out_re = v_re * f_re - v_im * f_im
    out_im = v_re * f_im + v_im * f_re
    return (out_re.reshape(val_shape), out_im.reshape(val_shape))


def short_local(extended, filters, seg_ext):
    reach_taps = filters.shape[1]
    out_rows = extended.shape[1] - reach_taps + 1
    own_seg = seg_ext[reach_taps - 1 :]
    running = jnp.zeros((extended.shape[0], out_rows, extended.shape[2]), jnp.float32)
    for shift_by in range(reach_taps):
        start_row = reach_taps - 1 - shift_by
        same_doc = jnp.where(seg_ext[start_row : start_row + out_rows] == own_seg, 1.0, 0.0)
        running = (
            running
            + filters[:, shift_by][:, None, :]
            * same_doc[None, :, None]
            * extended[:, start_row : start_row + out_rows]
        )
    return running


def spectral_device(projected, segment_ids, short_filter, long_filter, out_proj, mixed_cotangent):
    row_count = projected.shape[2]
    stacked = projected.shape[0]
    width_dev = projected.shape[3]
    short_reach = short_filter.shape[1]
    group_count = long_filter.shape[0]
    grad_scale = 1.0 / math.sqrt(
        projected.shape[1] * lax.axis_size("dp") * row_count * lax.axis_size("ctx")
    )
    segments = segment_ids[0]
    source = projected[:, 0]
    short_rows = short_reach - 1
    cot_full = lax.all_gather(mixed_cotangent[0], "tp", axis=1, tiled=True)
    prev_tail, prev_seg = shifted(
        (source[:, row_count - short_rows :], segments[row_count - short_rows :]), "ctx", 1
    )
    short_seg = jnp.concatenate([prev_seg, segments])
    short_ext = jnp.concatenate([prev_tail, source], axis=1).astype(jnp.float32)

    def short_piece(extended, filters):
        return short_local(extended, filters, short_seg)

    short_out, short_pull = jax.vjp(short_piece, short_ext, short_filter)
    query_conv = short_out[0]
    gated_rows = short_out[1] * short_out[2]
    filter_cols = long_filter.T
    mid_re, mid_im = pack_columns(gated_rows)
    spec_re, spec_im = forward_spectrum(jnp.concatenate([mid_re, filter_cols], axis=1))
    data_cols = spec_re.shape[2] - group_count
    signal_re = spec_re[:, :, :data_cols]
    signal_im = spec_im[:, :, :data_cols]
    filt_re = spec_re[:, :, data_cols:]
    filt_im = spec_im[:, :, data_cols:]
    long_re, long_im = by_filter(signal_re, signal_im, filt_re, filt_im, False)
    out_re, out_im = inverse_spectrum(long_re, long_im)
    y_out = (query_conv * out_re).astype(jnp.bfloat16)
    partial_out = jnp.dot(y_out, out_proj, preferred_element_type=jnp.float32)
    mixed = lax.psum_scatter(partial_out, "tp", scatter_dimension=1, tiled=True).astype(
        jnp.bfloat16
    )
    grad_y = jnp.dot(cot_full, out_proj.T, preferred_element_type=jnp.float32)
    grad_proj_local = jnp.dot(y_out.T, cot_full, preferred_element_type=jnp.float32)
    grad_long_out = grad_y * query_conv
    grad_query = grad_y * out_re
    grad_in_re, grad_in_im = pack_columns(grad_long_out)
    cot_re, cot_im = forward_spectrum(grad_in_re)
    back_re, back_im = by_filter(cot_re, cot_im, filt_re, filt_im, True)
    cross_re = (
        (signal_re * cot_re + signal_im * cot_im).reshape(2, row_count, group_count, -1).sum(axis=3)
    )
    cross_im = (
        (signal_re * cot_im - signal_im * cot_re).reshape(2, row_count, group_count, -1).sum(axis=3)
    )
    inv_re, inv_im = inverse_spectrum(
        jnp.concatenate([back_re, cross_re], axis=2), jnp.concatenate([back_im, cross_im], axis=2)
    )
    grad_gated = inv_re[:, :data_cols]
    grad_long_local = inv_re[:, data_cols:].T
    grad_short_out = jnp.stack([grad_query, grad_gated * short_out[2], grad_gated * short_out[1]])
    grad_short_ext, grad_short_local = short_pull(grad_short_out)
    returned_short = shifted(grad_short_ext[:, :short_rows], "ctx", -1)
    grad_source = grad_short_ext[:, short_rows:] + jnp.concatenate(
        [jnp.zeros((stacked, row_count - short_rows, width_dev), jnp.float32), returned_short],
        axis=1,
    )
    total_proj, total_short = lax.psum((grad_proj_local, grad_short_local), ("ctx", "dp"))
    total_long = lax.psum(grad_long_local, "dp")
    return (
        mixed[None],
        grad_source[:, None].astype(jnp.bfloat16),
        total_short * grad_scale,
        total_long * grad_scale,
        total_proj * grad_scale,
    )


bf16 = jnp.bfloat16
f32 = jnp.float32
SUB = 128


def split_bf16(value):
    high = value.astype(bf16)
    return high, (value - high.astype(f32)).astype(bf16)


def rotate(value, axis, steps):
    count = lax.axis_size(axis)
    return lax.ppermute(value, axis, [(i, (i + steps) % count) for i in range(count)])


def swap(value, axis, bits):
    return lax.ppermute(value, axis, [(i, i ^ bits) for i in range(lax.axis_size(axis))])


def scatter_chunks(chunks, axis):
    return [chunks[0]] + [rotate(chunks[s], axis, s) for s in range(1, len(chunks))]


def after(value, other):
    return lax.optimization_barrier((value, other))[0]


def spread(value, axis):
    return [value] + [rotate(value, axis, s) for s in range(1, lax.axis_size(axis))]


def on_core(kernel, outs, args, name, scratch=(), flops=0, whole=False):
    moved = sum(a.size * a.dtype.itemsize for a in args)
    moved += sum(math.prod(shape) * jnp.dtype(kind).itemsize for shape, kind in outs)
    return pl.pallas_call(
        kernel,
        out_shape=[jax.ShapeDtypeStruct(shape, kind) for shape, kind in outs],
        in_specs=[pl.BlockSpec(memory_space=pltpu.HBM) if whole else pl.BlockSpec()] * len(args),
        scratch_shapes=list(scratch),
        compiler_params=pltpu.CompilerParams(vmem_limit_bytes=(63 if whole else 40) * 1024 * 1024),
        cost_estimate=pl.CostEstimate(flops=flops, bytes_accessed=moved, transcendentals=0),
        name=name,
    )(*args)


def block_at(index, size):
    return pl.ds(pl.multiple_of(index * size, size), size)


def pack_kernel(devices, reach, *refs):
    sources, refs = refs[:3], refs[3:]
    outs, refs = refs[:devices], refs[devices:]
    held, (turned, small, tail, sems) = refs[:3], refs[3:]
    copies = [
        pltpu.make_async_copy(sources[n], held[n], sems.at[n]) for n in range(len(sources))
    ]
    for copy in copies:
        copy.start()
    projected, filters, segments = held
    me = lax.axis_index("ctx")
    stacked, rows, width = projected.shape
    chunk = width // devices
    count = filters.shape[0]
    groups = count // devices
    for copy in copies:
        copy.wait()
    for i in range(1, stacked):
        turned[i - 1] = projected[i].T
    tail[...] = jnp.zeros_like(tail)
    for i in range(stacked):
        tail[i * reach : (i + 1) * reach] = projected[i, rows - reach :].astype(f32)
    small[...] = jnp.zeros_like(small)
    seg = segments[...]
    small[2 * groups : 2 * groups + 1] = (seg >> 8).astype(f32)
    small[2 * groups + 1 : 2 * groups + 2] = (seg & 255).astype(f32)
    body = (stacked - 1) * chunk
    for s in range(devices):
        to = lax.rem(me + s, devices)
        for i in range(stacked - 1):
            outs[s][i * chunk : (i + 1) * chunk] = turned[i, block_at(to, chunk)]
        lines = pltpu.roll(filters[...], lax.rem(count - to * groups, count), 0)[0:groups]
        high = lines.astype(bf16).astype(f32)
        small[0:groups] = high
        small[groups : 2 * groups] = lines - high
        outs[s][body : body + 16] = small[...].astype(bf16)
    outs[1][body + 16 :] = tail[...].astype(bf16)


def prepare_kernel(short_filter, chunk, projected, columns, chunk_out, turned, flat):
    stacked, taps, _ = short_filter.shape
    flat[...] = jnp.zeros_like(flat)
    for i in range(stacked):
        flat[i * taps : (i + 1) * taps] = short_filter[i]
        turned[i] = projected[i].T
    columns[...] = flat[...].T
    chunk_out[...] = chunk[...]


def tap_masks(seg, taps):
    wide = jnp.broadcast_to(seg, (8, seg.shape[1]))
    place = lax.broadcasted_iota(jnp.int32, wide.shape, 1)
    masks = [None]
    for s in range(1, taps):
        same = (wide == pltpu.roll(wide, s, 1)) & (place >= s)
        masks.append(jnp.where(same, 1.0, 0.0)[0:1])
    return masks


def block_masks(seg, taps, place, me, length):
    masks = tap_masks(seg, taps)
    for s in range(1, taps):
        place[8 * s : 8 * (s + 1)] = jnp.broadcast_to(masks[s], (8, seg.shape[1]))
    return [None] + [place[8 * s : 8 * s + 8, block_at(me, length)][0:1] for s in range(1, taps)]


def local_shifts(turned, previous, taps, i):
    tail = previous[previous.shape[0] - 16 :].astype(f32)
    before = jnp.concatenate([tail, jnp.zeros((SUB - 16, tail.shape[1]), f32)], axis=0)
    before = pltpu.roll(before, SUB - (taps - 1) * (i + 1), 0)
    wide = jnp.concatenate([before.T, turned[i].astype(f32)], axis=1)
    return [wide[:, SUB:]] + [pltpu.roll(wide, s, 1)[:, SUB:] for s in range(1, taps)]


def local_conv(turned, previous, columns, masks, i):
    taps = len(masks)
    shifts = local_shifts(turned, previous, taps, i)
    j = i * taps
    total = columns[:, j : j + 1] * shifts[0]
    for s in range(1, taps):
        total += columns[:, j + s : j + s + 1] * (masks[s] * shifts[s])
    return total


def pair_conv_kernel(taps, turned, previous, columns, seg, out, place):
    masks = block_masks(seg[0:1], taps, place, lax.axis_index("ctx"), turned.shape[2])
    for i in range(out.shape[0]):
        out[i] = local_conv(turned, previous, columns, masks, i + 1)


def conv_kernel(devices, taps, columns, *rest):
    pays, rest = rest[:devices], rest[devices:]
    outs, rest = rest[:devices], rest[devices:]
    conv, source, seg_out, toeplitz, small, long, rests = rest
    me = lax.axis_index("ctx")
    stacked, chunk, span = conv.shape
    length = span // devices
    groups = toeplitz.shape[0]
    size = chunk // groups
    body = stacked * chunk
    for s in range(devices):
        at = block_at(lax.rem(me - s + devices, devices), length)
        source[:, at] = pays[s][0:body]
        small[:, at] = pays[s][body : body + 16].astype(f32)
    seg = small[2 * groups : 2 * groups + 1] * 256.0 + small[2 * groups + 1 : 2 * groups + 2]
    seg_out[...] = jnp.broadcast_to(seg, seg_out.shape)
    masks = tap_masks(seg, taps)
    column = columns[block_at(me, chunk)]
    for i in range(stacked):
        x = source[i * chunk : (i + 1) * chunk].astype(f32)
        j = (i + 1) * taps
        total = column[:, j : j + 1] * x
        for s in range(1, taps):
            total += column[:, j + s : j + s + 1] * (masks[s] * pltpu.roll(x, s, 1))
        conv[i] = total
    high, low = split_bf16(conv[0] * conv[1])
    for g in range(groups):
        line = small[g : g + 1] + small[groups + g : groups + g + 1]
        padded = jnp.concatenate([line, jnp.zeros((1, SUB), f32)], axis=1)
        turned = pltpu.roll(
            jnp.broadcast_to(padded, (SUB, span + SUB)), 0, 1, stride=1, stride_axis=0
        )[:, :span]
        for half, into in zip(split_bf16(turned), (toeplitz, rests)):
            for r in range(length // SUB):
                rows = slice(r * SUB, (r + 1) * SUB)
                if r:
                    into[g, rows, : r * SUB] = jnp.zeros((SUB, r * SUB), bf16)
                into[g, rows, r * SUB :] = half[:, : span - r * SUB]
        own = slice(g * size, (g + 1) * size)
        pieces = []
        for j in range(devices):
            at = slice(j * length, (j + 1) * length)
            pieces += [high[own, at], low[own, at]]
        stack = jnp.concatenate(pieces, axis=0)
        totals = [None] * devices
        for lag in range(devices):
            lhs = stack[: 2 * size * (devices - lag)]
            at = slice(lag * length, (lag + 1) * length)
            part = jnp.dot(lhs, toeplitz[g, :, at], preferred_element_type=f32)
            part += jnp.dot(lhs, rests[g, :, at], preferred_element_type=f32)
            for j in range(devices - lag):
                term = part[2 * size * j : 2 * size * j + size]
                term += part[2 * size * j + size : 2 * size * (j + 1)]
                i = j + lag
                totals[i] = term if totals[i] is None else totals[i] + term
        for i in range(devices):
            long[own, i * length : (i + 1) * length] = totals[i].astype(bf16)
    for s in range(devices):
        outs[s][...] = long[:, block_at(lax.rem(me + s, devices), length)]


def grad_y_kernel(devices, parts, taps, weights, turned, previous, columns, seg, *rest):
    cots, rest = rest[:parts], rest[parts:]
    longs, rest = rest[:devices], rest[devices:]
    outs, (grad_y, query_conv, place, full) = rest[:devices], rest[devices:]
    me, mine = lax.axis_index("ctx"), lax.axis_index("tp")
    rows, width = cots[0].shape
    chunk = width // devices
    masks = block_masks(seg[0:1], taps, place, me, rows)
    conv = local_conv(turned, previous, columns, masks, 0)
    query_conv[...] = conv
    total = None
    for s in range(parts):
        cot = cots[s][...]
        lhs = weights[:, block_at(mine ^ s, width)]
        term = lax.dot_general(lhs, cot, (((1,), (1,)), ((), ())), preferred_element_type=f32)
        total = term if total is None else total + term
    grad_y[...] = total
    full[...] = (total * conv).astype(bf16)
    for s in range(devices):
        outs[s][0:chunk] = longs[s][...]
        outs[s][chunk:] = full[block_at(lax.rem(me + s, devices), chunk)]


def weight_grad_kernel(devices, parts, query_conv, *rest):
    cots, rest = rest[:parts], rest[parts:]
    longs, rest = rest[:devices], rest[devices:]
    y_out, long_out, keep, send, full = rest
    me, mine, core = lax.axis_index("ctx"), lax.axis_index("tp"), lax.axis_index("dp")
    rows, width = cots[0].shape
    chunk = width // devices
    half = width // 2
    for s in range(devices):
        at = block_at(lax.rem(me - s + devices, devices), chunk)
        long_out[at] = longs[s][0:chunk].astype(f32)
    y = (query_conv[...] * long_out[...]).astype(bf16)
    y_out[...] = y
    for s in range(parts):
        cot = cots[s][...]
        at = block_at(mine ^ s, width)
        full[:, at] = jnp.dot(y, cot, preferred_element_type=f32)
    keep[...] = full[block_at(core, half)]
    send[...] = full[block_at(1 - core, half)]


def core_sum_kernel(devices, keep, other, *rest):
    outs, (full,) = rest[:devices], rest[devices:]
    me = lax.axis_index("ctx")
    rows = keep.shape[0] // devices
    full[...] = keep[...] + other[...].astype(f32)
    for s in range(devices):
        at = block_at(lax.rem(me + s, devices), rows)
        outs[s][...] = full[at].astype(outs[s].dtype)


def block_sum_kernel(scale, *refs):
    total = refs[0][...]
    for ref in refs[1:-1]:
        total += ref[...].astype(f32)
    refs[-1][...] = (total * scale).astype(bf16)


def mixed_part_kernel(y, weights, kept, sent, full):
    mine = lax.axis_index("tp")
    rows, width = full.shape[0], y.shape[0]
    full[...] = lax.dot_general(
        y[...], weights[...], (((0,), (0,)), ((), ())), preferred_element_type=f32
    )
    for h in range(2):
        kept[h * rows : (h + 1) * rows] = full[:, block_at(mine ^ (2 * h), width)]
        sent[h * rows : (h + 1) * rows] = full[:, block_at(mine ^ (2 * h + 1), width)].astype(bf16)


def mixed_pair_kernel(kept, come, own, sent):
    rows = own.shape[0]
    own[...] = kept[0:rows] + come[0:rows].astype(f32)
    sent[...] = (kept[rows:] + come[rows:].astype(f32)).astype(bf16)


def mixed_sum_kernel(own, come, out):
    out[...] = (own[...] + come[...].astype(f32)).astype(bf16)


def backward_kernel(
    devices, taps, conv, source, seg, toeplitz, columns, turned, previous, grad_y, long, *rest
):
    glos, rest = rest[:devices], rest[devices:]
    outs, (query_out, grad_long_out, grads, small, marks, place) = rest[:devices], rest[devices:]
    me = lax.axis_index("ctx")
    stacked, chunk, span = conv.shape
    length = span // devices
    groups = toeplitz.shape[0]
    size = chunk // groups
    width = turned.shape[1]

    own_masks = block_masks(seg[0:1], taps, place, me, length)
    shifts = local_shifts(turned, previous, taps, 0)
    grad = grad_y[...] * long[...]
    total = columns[:, 0:1] * grad
    lane = lax.broadcasted_iota(jnp.int32, (width, SUB), 1)
    position = lax.broadcasted_iota(jnp.int32, (width, length), 1)
    sums = jnp.where(lane == groups, jnp.sum(grad * shifts[0], axis=1, keepdims=True), 0.0)
    early = jnp.zeros((width, SUB), f32)
    for s in range(1, taps):
        masked = own_masks[s] * grad
        back = pltpu.roll(columns[:, s : s + 1] * masked, length - s, 1)
        total += jnp.where(position < length - s, back, 0.0)
        early += jnp.where(position >= length - s, back, 0.0)[:, length - SUB :]
        tap = jnp.sum(masked * shifts[s], axis=1, keepdims=True)
        sums += jnp.where(lane == groups + s, tap, 0.0)
    query_out[...] = total.T
    common = sums.T[0:16]
    early_query = early.T[SUB - 16 :]

    for s in range(devices):
        at = block_at(lax.rem(me - s + devices, devices), length)
        grad_long_out[:, at] = glos[s][chunk:]
    masks = tap_masks(seg[0:1], taps)
    column = columns[block_at(me, chunk)]
    high = grad_long_out[...]
    gated = (conv[0] * conv[1]).astype(bf16)
    gg_parts = []
    corner = lax.broadcasted_iota(jnp.int32, (SUB, SUB), 0)
    corner += lax.broadcasted_iota(jnp.int32, (SUB, SUB), 1)
    flip = jnp.where(corner == SUB - 1, 1.0, 0.0).astype(bf16)
    subs = span // SUB
    small[...] = jnp.zeros_like(small)
    for g in range(groups):
        own = slice(g * size, (g + 1) * size)
        stack = jnp.concatenate(
            [high[own, i * length : (i + 1) * length] for i in range(devices)], axis=0
        )
        totals = [None] * devices
        for lag in range(devices):
            part = lax.dot_general(
                stack[size * lag :],
                toeplitz[g, :, lag * length : (lag + 1) * length],
                (((1,), (1,)), ((), ())),
                preferred_element_type=f32,
            )
            for j in range(devices - lag):
                term = part[size * j : size * (j + 1)]
                totals[j] = term if totals[j] is None else totals[j] + term
        gg_parts.append(jnp.concatenate(totals, axis=1))
        left = jnp.concatenate([gated[own, j * SUB : (j + 1) * SUB] for j in range(subs)], axis=0)
        right = jnp.concatenate([high[own, j * SUB : (j + 1) * SUB] for j in range(subs)], axis=0)
        turned = lax.dot_general(
            flip, left, (((1,), (1,)), ((), ())), preferred_element_type=f32
        ).astype(bf16)
        lines = []
        for lag in range(subs):
            cross = jnp.dot(
                turned[:, : size * (subs - lag)], right[size * lag :], preferred_element_type=f32
            )
            wide = jnp.concatenate([cross, jnp.zeros((SUB, SUB), f32)], axis=1)
            wide = pltpu.roll(wide, 1, 1, stride=1, stride_axis=0)
            lines.append(jnp.sum(wide, axis=0, keepdims=True))
        per = length // SUB
        for lag in range(subs):
            line = lines[lag][:, SUB:]
            if lag + 1 < subs:
                line += lines[lag + 1][:, :SUB]
            b, within = divmod(lag, per)
            small[b, g : g + 1, within * SUB : (within + 1) * SUB] = line
    grad_gated = jnp.concatenate(gg_parts, axis=0)
    grads[...] = grad_gated.astype(bf16)
    lane = lax.broadcasted_iota(jnp.int32, (chunk, SUB), 1)
    sums = jnp.zeros((chunk, SUB), f32)
    reach = taps - 1
    early = [jnp.zeros((chunk, SUB), f32) for _ in range(stacked * devices)]
    for i in range(stacked):
        grad = grad_gated * conv[1 - i]
        x = source[i * chunk : (i + 1) * chunk].astype(f32)
        j = (i + 1) * taps
        tap = jnp.sum(grad * x, axis=1, keepdims=True)
        sums += jnp.where(lane == groups + j, tap, 0.0)
        for s in range(1, taps):
            masked = masks[s] * grad
            tap = jnp.sum(masked * pltpu.roll(x, s, 1), axis=1, keepdims=True)
            sums += jnp.where(lane == groups + j + s, tap, 0.0)
            back = column[:, j + s : j + s + 1] * pltpu.roll(masked, span - s, 1)
            for b in range(devices):
                end = back[:, (b + 1) * length - SUB : (b + 1) * length]
                early[i * devices + b] += jnp.where(lane >= SUB - s, end, 0.0)
    marks[...] = jnp.zeros_like(marks)
    marks[:, 0:chunk] = sums.T
    common += pltpu.roll(marks[0:16], me * chunk, 1)
    count = (stacked + 1) * taps
    start = 2 * groups + 2 * count
    high = common.astype(bf16).astype(f32)
    for b in range(devices):
        lines = small[b, 0:groups]
        top = lines.astype(bf16).astype(f32)
        small[b, 0:groups] = top
        small[b, groups : 2 * groups] = lines - top
        small[b, 2 * groups : 2 * groups + count] = high[groups : groups + count]
        small[b, 2 * groups + count : start] = (common - high)[groups : groups + count]
        small[b, start : start + reach] = early_query[16 - reach :]
        for i in range(stacked):
            marks[:, 0:chunk] = early[i * devices + b].T
            placed = pltpu.roll(marks[SUB - 16 :], me * chunk, 1)
            at = start + (i + 1) * reach
            small[b, at : at + reach] = placed[16 - reach :]
    for s in range(devices):
        to = lax.rem(me + s, devices)
        outs[s][0:chunk] = grads[:, block_at(to, length)]
        outs[s][chunk:] = small[to].astype(bf16)


def small_sum_kernel(devices, groups, stacked, taps, *refs):
    pays, (sums, later, tiles) = refs[:devices], refs[devices:]
    me = lax.axis_index("ctx")
    width = pays[0].shape[1]
    body = width // devices
    count = stacked * taps
    start = 2 * groups + 2 * count
    reach = taps - 1
    for s in range(devices):
        tiles[lax.rem(me - s + devices, devices)] = pays[s][body:].astype(f32)
    total = tiles[0]
    for c in range(1, devices):
        total += tiles[c]
    lines = [tiles[c, 0:groups] + tiles[c, groups : 2 * groups] for c in range(devices)]
    taps_sum = total[2 * groups : 2 * groups + count] + total[2 * groups + count : start]
    for n, value in enumerate((jnp.concatenate(lines, axis=0), taps_sum)):
        if value.shape[0] < 16:
            rest = jnp.zeros((16 - value.shape[0], width), f32)
            value = jnp.concatenate([value, rest], axis=0)
        for h, half in enumerate(split_bf16(value)):
            sums[:, (2 * h + n) * width : (2 * h + n + 1) * width] = half
    last = pays[devices - 1][body:].astype(f32)
    later[...] = jnp.zeros_like(later)
    later[0, 16 - reach : 16] = last[start : start + reach]
    for i in range(1, stacked):
        later[i, 16 - reach : 16] = total[start + i * reach : start + (i + 1) * reach]


def collect_kernel(devices, sums, *refs):
    blocks, near = refs[:devices], refs[devices]
    me = lax.axis_index("ctx")
    rows = blocks[0].shape[0]
    for s in range(devices):
        near[block_at(lax.rem(me - s + devices, devices), rows)] = blocks[s][...]
    near[devices * rows :] = sums[...]


def grad_out_kernel(devices, taps, query_part, pair, columns, seg, later, *refs):
    pays, (out, gated, place) = refs[:devices], refs[devices:]
    me = lax.axis_index("ctx")
    stacked, rows, width = out.shape
    chunk = width // devices
    for s in range(devices):
        at = block_at(lax.rem(me - s + devices, devices), chunk)
        gated[at] = pays[s][0:chunk].astype(f32)
    masks = block_masks(seg[0:1], taps, place, me, rows)
    position = lax.broadcasted_iota(jnp.int32, (width, rows), 1)
    for i in range(stacked):
        if i == 0:
            turned = query_part[...]
        else:
            grad = gated[...] * pair[2 - i]
            j = i * taps
            total = columns[:, j : j + 1] * grad
            for s in range(1, taps):
                back = pltpu.roll(columns[:, j + s : j + s + 1] * (masks[s] * grad), rows - s, 1)
                total += jnp.where(position < rows - s, back, 0.0)
            turned = total.T
        out[i, 0 : rows - 16] = turned[0 : rows - 16].astype(bf16)
        out[i, rows - 16 :] = (turned[rows - 16 :] + later[i]).astype(bf16)


def final_kernel(scale, near, far, weight_out, short_out, long_out):
    core = lax.axis_index("dp")
    half = weight_out.shape[0] // 2
    weight_out[block_at(core, half)] = near[0:half].astype(f32)
    weight_out[block_at(1 - core, half)] = far[0:half].astype(f32)
    count, width = long_out.shape
    stacked, taps, _ = short_out.shape

    def sums(n):
        pieces = []
        for ref in (near, far):
            high = ref[half:, n * width : (n + 1) * width].astype(f32)
            low = ref[half:, (n + 2) * width : (n + 3) * width].astype(f32)
            pieces.append(high + low)
        return (pieces[0] + pieces[1]) * scale

    long_out[...] = sums(0)
    total = sums(1)
    for i in range(stacked):
        short_out[i] = total[i * taps : (i + 1) * taps]


def direct_device(projected, segment_ids, short_filter, long_filter, out_proj, mixed_cotangent):
    devices, parts = lax.axis_size("ctx"), lax.axis_size("tp")
    stacked, _, length, width = projected.shape
    taps = short_filter.shape[1]
    count = long_filter.shape[0]
    groups = count // devices
    chunk = width // devices
    span = length * devices
    total_cols = out_proj.shape[1]
    grad_scale = 1.0 / math.sqrt(projected.shape[1] * lax.axis_size("dp") * span)
    cotangent = mixed_cotangent[0]
    room = 16
    inputs = (projected[:, 0], long_filter, segment_ids)

    outs = on_core(
        functools.partial(pack_kernel, devices, taps - 1),
        [
            (((stacked - 1) * chunk + (2 * room if s == 1 else room), length), bf16)
            for s in range(devices)
        ],
        inputs,
        "pack",
        [pltpu.VMEM(a.shape, a.dtype) for a in inputs]
        + [
            pltpu.VMEM((stacked - 1, width, length), bf16),
            pltpu.VMEM((room, length), f32),
            pltpu.VMEM((room, width), f32),
            pltpu.SemaphoreType.DMA((len(inputs),)),
        ],
        whole=True,
    )
    own, *signal = scatter_chunks(outs, "ctx")
    beside = swap(cotangent, "tp", 1)
    columns, own, turned = on_core(
        prepare_kernel,
        [((width, 16), f32), (own.shape, bf16), ((stacked, width, length), bf16)],
        (after(short_filter, beside), own, inputs[0]),
        "prepare",
        [pltpu.VMEM((16, width), f32)],
    )
    signal = [own, *signal]

    conv_flops = 2 * groups * span * span * 64
    outs = on_core(
        functools.partial(conv_kernel, devices, taps),
        [((chunk, length), bf16)] * devices
        + [
            ((stacked - 1, chunk, span), f32),
            (((stacked - 1) * chunk, span), bf16),
            ((8, span), f32),
            ((groups, length, span), bf16),
        ],
        (columns, *signal),
        "conv",
        [
            pltpu.VMEM((room, span), f32),
            pltpu.VMEM((chunk, span), bf16),
            pltpu.VMEM((groups, length, span), bf16),
        ],
        flops=9 * 100000000,
    )
    longs, kept = outs[:devices], outs[devices:]
    seg = kept[2]
    cots = [cotangent, beside, swap(cotangent, "tp", 2), swap(beside, "tp", 2)]
    outs = on_core(
        functools.partial(grad_y_kernel, devices, parts, taps),
        [((2 * chunk, length), bf16)] * devices + [((width, length), f32)] * 2,
        (out_proj, turned, signal[1], columns, seg, *cots, *longs),
        "grad_y",
        [pltpu.VMEM((8 * taps, span), f32), pltpu.VMEM((width, length), bf16)],
        flops=2 * width * length * total_cols,
    )
    pairs, (grad_y, query_conv) = outs[:devices], outs[devices:]
    pairs = scatter_chunks(pairs, "ctx")

    (pair,) = on_core(
        functools.partial(pair_conv_kernel, taps),
        [((stacked - 1, width, length), f32)],
        (turned, signal[1], columns, seg),
        "pair_conv",
        [pltpu.VMEM((8 * taps, span), f32)],
    )
    query_conv = after(query_conv, pair)

    half = width // 2
    y, long, keep, send = on_core(
        functools.partial(weight_grad_kernel, devices, parts),
        [
            ((width, length), bf16),
            ((width, length), f32),
            ((half, total_cols), f32),
            ((half, total_cols), f32),
        ],
        (query_conv, *cots, *pairs),
        "weight_grad",
        [pltpu.VMEM((width, total_cols), f32)],
        flops=2 * width * length * total_cols,
    )
    other = rotate(send, "dp", 1)
    kept_part, sent_part = on_core(
        mixed_part_kernel,
        [((2 * length, width), f32), ((2 * length, width), bf16)],
        (y, out_proj),
        "mixed_part",
        [pltpu.VMEM((length, total_cols), f32)],
        flops=2 * width * length * total_cols,
    )
    keep = after(keep, kept_part)
    rows = half // devices
    sums = on_core(
        functools.partial(core_sum_kernel, devices),
        [((rows, total_cols), f32)] + [((rows, total_cols), bf16)] * (devices - 1),
        (keep, other),
        "core_sum",
        [pltpu.VMEM((half, total_cols), f32)],
    )
    parts_out = scatter_chunks(sums, "ctx")

    outs = on_core(
        functools.partial(backward_kernel, devices, taps),
        [((chunk + 2 * room, length), bf16)] * devices + [((length, width), f32)],
        (*kept, columns, turned, signal[1], grad_y, after(long, sums[1]), *pairs),
        "backward",
        [
            pltpu.VMEM((chunk, span), bf16),
            pltpu.VMEM((chunk, span), bf16),
            pltpu.VMEM((devices, 2 * room, length), f32),
            pltpu.VMEM((SUB, width), f32),
            pltpu.VMEM((8 * taps, span), f32),
        ],
        flops=2 * conv_flops,
    )
    back, query_part = outs[:devices], outs[devices]
    back = scatter_chunks(back, "ctx")
    sums, later = on_core(
        functools.partial(small_sum_kernel, devices, groups, stacked, taps),
        [((16, total_cols), bf16), ((stacked, 16, width), f32)],
        back,
        "small_sum",
        [pltpu.VMEM((devices, 2 * room, width), f32)],
        flops=2000 * 1000000,
    )
    (grad_projected,) = on_core(
        functools.partial(grad_out_kernel, devices, taps),
        [((stacked, length, width), bf16)],
        (query_part, pair, columns, seg, later, *back),
        "grad_out",
        [pltpu.VMEM((width, length), f32), pltpu.VMEM((8 * taps, span), f32)],
    )
    (block,) = on_core(
        functools.partial(block_sum_kernel, grad_scale),
        [((rows, total_cols), bf16)],
        parts_out,
        "block_sum",
    )
    own_part, sent_part = on_core(
        mixed_pair_kernel,
        [((length, width), f32), ((length, width), bf16)],
        (after(kept_part, query_part), swap(sent_part, "tp", 1)),
        "mixed_pair",
    )
    come_part = swap(sent_part, "tp", 2)
    (mixed,) = on_core(
        mixed_sum_kernel, [((length, width), bf16)], (own_part, come_part), "mixed_sum"
    )

    blocks = spread(block, "ctx")
    blocks[0] = after(block, (grad_projected, come_part))
    (near,) = on_core(
        functools.partial(collect_kernel, devices),
        [((half + 16, total_cols), bf16)],
        (sums, *blocks),
        "collect",
    )
    grad_out_proj, grad_short, grad_long = on_core(
        functools.partial(final_kernel, grad_scale),
        [((width, total_cols), f32), (short_filter.shape, f32), ((count, length), f32)],
        (after(near, mixed), rotate(near, "dp", 1)),
        "final",
    )
    return (mixed[None], grad_projected[:, None], grad_short, grad_long, grad_out_proj)


def direct_fits(mesh, projected, short_filter, long_filter, out_proj):
    devices = mesh.shape["ctx"]
    length = projected.shape[2] // devices
    width = projected.shape[3] // mesh.shape["tp"]
    groups = long_filter.shape[0] // mesh.shape["tp"]
    stacked, taps = short_filter.shape[:2]
    return (
        mesh.shape["dp"] == 2
        and mesh.shape["tp"] == 4
        and projected.shape[1] == 2
        and stacked == 3
        and length == width
        and length % SUB == 0
        and groups % devices == 0
        and groups == 16
        and (width // devices) % 16 == 0
        and width // devices <= SUB
        and (width // groups) == 16
        and 2 * groups // devices + 2 <= 16
        and out_proj.shape[1] == 4 * width
        and stacked * (taps - 1) <= 16
        and groups // devices + stacked * taps <= 16
        and 2 * (groups // devices) + 2 * stacked * taps + stacked * (taps - 1) <= 32
    )


def solution(mesh):
    in_specs = (
        P(None, "dp", "ctx", "tp"),
        P("dp", "ctx"),
        P(None, None, "tp"),
        P("tp", "ctx"),
        P("tp", None),
        P("dp", "ctx", "tp"),
    )
    out_specs = (
        P("dp", "ctx", "tp"),
        P(None, "dp", "ctx", "tp"),
        P(None, None, "tp"),
        P("tp", "ctx"),
        P("tp", None),
    )

    def layer(projected, segment_ids, short_filter, long_filter, out_proj, mixed_cotangent):
        fits = direct_fits(mesh, projected, short_filter, long_filter, out_proj)
        return jax.shard_map(
            direct_device if fits else spectral_device,
            mesh=mesh,
            in_specs=in_specs,
            out_specs=out_specs,
            check_vma=False,
        )(projected, segment_ids, short_filter, long_filter, out_proj, mixed_cotangent)

    return layer
```

```python
import functools
import math

import jax
import jax.numpy as jnp
from jax import lax
from jax.experimental import pallas as pl
from jax.experimental.pallas import tpu as pltpu
from jax.sharding import PartitionSpec as P

highest_precision = lax.Precision.HIGHEST


def shifted(value, axis, steps):
    count = lax.axis_size(axis)
    first, last = (max(0, -steps), min(count, count - steps))
    return lax.ppermute(value, axis, [(source, source + steps) for source in range(first, last)])


def angle_table(height, breadth, period, direction):
    product = (
        jnp.arange(height, dtype=jnp.int32)[:, None]
        * jnp.arange(breadth, dtype=jnp.int32)[None, :]
        % period
    )
    angles = direction * 2.0 * math.pi / period * product.astype(jnp.float32)
    return (jnp.cos(angles), jnp.sin(angles))


def row_twiddle(spec_re, spec_im, direction):
    my_index = lax.axis_index("ctx")
    devices = lax.axis_size("ctx")
    row_count = spec_re.shape[1]
    period = 2 * devices * row_count
    freq_pair = 2 * my_index + jnp.arange(2, dtype=jnp.int32)
    product = freq_pair[:, None] * jnp.arange(row_count, dtype=jnp.int32)[None, :] % period
    angles = direction * 2.0 * math.pi / period * product.astype(jnp.float32)
    cosine = jnp.cos(angles)[:, :, None]
    sine_part = jnp.sin(angles)[:, :, None]
    return (spec_re * cosine - spec_im * sine_part, spec_re * sine_part + spec_im * cosine)


def row_transform(spec_re, spec_im, direction):
    row_count = spec_re.shape[1]
    cosine, sine_part = angle_table(row_count, row_count, row_count, direction)

    def along_rows(blocks, matrix):
        return jnp.einsum("kmc,mq->kqc", blocks, matrix, precision=highest_precision)

    return (
        along_rows(spec_re, cosine) - along_rows(spec_im, sine_part),
        along_rows(spec_re, sine_part) + along_rows(spec_im, cosine),
    )


def mixing(matrix, blocks):
    return jnp.einsum("kj,jmc->kmc", matrix, blocks, precision=highest_precision)


def forward_spectrum(real_part):
    devices = lax.axis_size("ctx")
    cosine, sine_part = angle_table(2 * devices, devices, 2 * devices, -1.0)
    spread_re = lax.all_to_all(real_part[None], "ctx", split_axis=1, concat_axis=0, tiled=True)
    column_re = mixing(cosine, spread_re)
    column_im = mixing(sine_part, spread_re)
    near_re, near_im = (
        lax.all_to_all(column_re, "ctx", split_axis=0, concat_axis=1, tiled=True),
        lax.all_to_all(column_im, "ctx", split_axis=0, concat_axis=1, tiled=True),
    )
    twist_re, twist_im = row_twiddle(near_re, near_im, -1.0)
    return row_transform(twist_re, twist_im, -1.0)


def inverse_spectrum(spec_re, spec_im):
    devices = lax.axis_size("ctx")
    row_count = spec_re.shape[1]
    back_re, back_im = row_transform(spec_re, spec_im, 1.0)
    twist_re, twist_im = row_twiddle(back_re / row_count, back_im / row_count, 1.0)
    far_re, far_im = (
        lax.all_to_all(twist_re, "ctx", split_axis=1, concat_axis=0, tiled=True),
        lax.all_to_all(twist_im, "ctx", split_axis=1, concat_axis=0, tiled=True),
    )
    cosine, sine_part = angle_table(devices, 2 * devices, 2 * devices, 1.0)
    out_re = (mixing(cosine, far_re) - mixing(sine_part, far_im)) / (2 * devices)
    rows_re = lax.all_to_all(out_re, "ctx", split_axis=0, concat_axis=1, tiled=True)
    return (rows_re[0], rows_re[0])


def pack_columns(values):
    return (values, values)


def by_filter(val_re, val_im, fil_re, fil_im, conjugate):
    val_shape = val_re.shape
    group_count = fil_re.shape[2]
    v_re = val_re.reshape(val_shape[0], val_shape[1], group_count, -1)
    v_im = val_im.reshape(val_shape[0], val_shape[1], group_count, -1)
    f_re = fil_re[:, :, :, None]
    f_im = fil_im[:, :, :, None]
    if conjugate:
        f_im = -f_im
    out_re = v_re * f_re - v_im * f_im
    out_im = v_re * f_im + v_im * f_re
    return (out_re.reshape(val_shape), out_im.reshape(val_shape))


def short_local(extended, filters, seg_ext):
    reach_taps = filters.shape[1]
    out_rows = extended.shape[1] - reach_taps + 1
    own_seg = seg_ext[reach_taps - 1 :]
    running = jnp.zeros((extended.shape[0], out_rows, extended.shape[2]), jnp.float32)
    for shift_by in range(reach_taps):
        start_row = reach_taps - 1 - shift_by
        same_doc = jnp.where(seg_ext[start_row : start_row + out_rows] == own_seg, 1.0, 0.0)
        running = (
            running
            + filters[:, shift_by][:, None, :]
            * same_doc[None, :, None]
            * extended[:, start_row : start_row + out_rows]
        )
    return running


def spectral_device(projected, segment_ids, short_filter, long_filter, out_proj, mixed_cotangent):
    row_count = projected.shape[2]
    stacked = projected.shape[0]
    width_dev = projected.shape[3]
    short_reach = short_filter.shape[1]
    group_count = long_filter.shape[0]
    grad_scale = 1.0 / math.sqrt(
        projected.shape[1] * lax.axis_size("dp") * row_count * lax.axis_size("ctx")
    )
    segments = segment_ids[0]
    source = projected[:, 0]
    short_rows = short_reach - 1
    cot_full = lax.all_gather(mixed_cotangent[0], "tp", axis=1, tiled=True)
    prev_tail, prev_seg = shifted(
        (source[:, row_count - short_rows :], segments[row_count - short_rows :]), "ctx", 1
    )
    short_seg = jnp.concatenate([prev_seg, segments])
    short_ext = jnp.concatenate([prev_tail, source], axis=1).astype(jnp.float32)

    def short_piece(extended, filters):
        return short_local(extended, filters, short_seg)

    short_out, short_pull = jax.vjp(short_piece, short_ext, short_filter)
    query_conv = short_out[0]
    gated_rows = short_out[1] * short_out[2]
    filter_cols = long_filter.T
    mid_re, mid_im = pack_columns(gated_rows)
    spec_re, spec_im = forward_spectrum(jnp.concatenate([mid_re, filter_cols], axis=1))
    data_cols = spec_re.shape[2] - group_count
    signal_re = spec_re[:, :, :data_cols]
    signal_im = spec_im[:, :, :data_cols]
    filt_re = spec_re[:, :, data_cols:]
    filt_im = spec_im[:, :, data_cols:]
    long_re, long_im = by_filter(signal_re, signal_im, filt_re, filt_im, False)
    out_re, out_im = inverse_spectrum(long_re, long_im)
    y_out = (query_conv * out_re).astype(jnp.bfloat16)
    partial_out = jnp.dot(y_out, out_proj, preferred_element_type=jnp.float32)
    mixed = lax.psum_scatter(partial_out, "tp", scatter_dimension=1, tiled=True).astype(
        jnp.bfloat16
    )
    grad_y = jnp.dot(cot_full, out_proj.T, preferred_element_type=jnp.float32)
    grad_proj_local = jnp.dot(y_out.T, cot_full, preferred_element_type=jnp.float32)
    grad_long_out = grad_y * query_conv
    grad_query = grad_y * out_re
    grad_in_re, grad_in_im = pack_columns(grad_long_out)
    cot_re, cot_im = forward_spectrum(grad_in_re)
    back_re, back_im = by_filter(cot_re, cot_im, filt_re, filt_im, True)
    cross_re = (
        (signal_re * cot_re + signal_im * cot_im).reshape(2, row_count, group_count, -1).sum(axis=3)
    )
    cross_im = (
        (signal_re * cot_im - signal_im * cot_re).reshape(2, row_count, group_count, -1).sum(axis=3)
    )
    inv_re, inv_im = inverse_spectrum(
        jnp.concatenate([back_re, cross_re], axis=2), jnp.concatenate([back_im, cross_im], axis=2)
    )
    grad_gated = inv_re[:, :data_cols]
    grad_long_local = inv_re[:, data_cols:].T
    grad_short_out = jnp.stack([grad_query, grad_gated * short_out[2], grad_gated * short_out[1]])
    grad_short_ext, grad_short_local = short_pull(grad_short_out)
    returned_short = shifted(grad_short_ext[:, :short_rows], "ctx", -1)
    grad_source = grad_short_ext[:, short_rows:] + jnp.concatenate(
        [jnp.zeros((stacked, row_count - short_rows, width_dev), jnp.float32), returned_short],
        axis=1,
    )
    total_proj, total_short = lax.psum((grad_proj_local, grad_short_local), ("ctx", "dp"))
    total_long = lax.psum(grad_long_local, "dp")
    return (
        mixed[None],
        grad_source[:, None].astype(jnp.bfloat16),
        total_short * grad_scale,
        total_long * grad_scale,
        total_proj * grad_scale,
    )


bf16 = jnp.bfloat16
f32 = jnp.float32
SUB = 128


def split_bf16(value):
    high = value.astype(bf16)
    return high, (value - high.astype(f32)).astype(bf16)


def rotate(value, axis, steps):
    count = lax.axis_size(axis)
    return lax.ppermute(value, axis, [(i, (i + steps) % count) for i in range(count)])


def swap(value, axis, bits):
    return lax.ppermute(value, axis, [(i, i ^ bits) for i in range(lax.axis_size(axis))])


def scatter_chunks(chunks, axis):
    return [chunks[0]] + [rotate(chunks[s], axis, s) for s in range(1, len(chunks))]


def after(value, other):
    return lax.optimization_barrier((value, other))[0]


def spread(value, axis):
    return [value] + [rotate(value, axis, s) for s in range(1, lax.axis_size(axis))]


def on_core(kernel, outs, args, name, scratch=(), flops=0, whole=False):
    moved = sum(a.size * a.dtype.itemsize for a in args)
    moved += sum(math.prod(shape) * jnp.dtype(kind).itemsize for shape, kind in outs)
    return pl.pallas_call(
        kernel,
        out_shape=[jax.ShapeDtypeStruct(shape, kind) for shape, kind in outs],
        in_specs=[pl.BlockSpec(memory_space=pltpu.HBM) if whole else pl.BlockSpec()] * len(args),
        scratch_shapes=list(scratch),
        compiler_params=pltpu.CompilerParams(vmem_limit_bytes=(63 if whole else 40) * 1024 * 1024),
        cost_estimate=pl.CostEstimate(flops=flops, bytes_accessed=moved, transcendentals=0),
        name=name,
    )(*args)


def block_at(index, size):
    return pl.ds(pl.multiple_of(index * size, size), size)


def pack_kernel(devices, reach, *refs):
    sources, refs = refs[:3], refs[3:]
    outs, refs = refs[:devices], refs[devices:]
    held, (turned, small, tail, sems) = refs[:3], refs[3:]
    copies = [
        pltpu.make_async_copy(sources[n], held[n], sems.at[n]) for n in range(len(sources))
    ]
    for copy in copies:
        copy.start()
    projected, filters, segments = held
    me = lax.axis_index("ctx")
    stacked, rows, width = projected.shape
    chunk = width // devices
    count = filters.shape[0]
    groups = count // devices
    for copy in copies:
        copy.wait()
    for i in range(1, stacked):
        turned[i - 1] = projected[i].T
    tail[...] = jnp.zeros_like(tail)
    for i in range(stacked):
        tail[i * reach : (i + 1) * reach] = projected[i, rows - reach :].astype(f32)
    small[...] = jnp.zeros_like(small)
    seg = segments[...]
    small[2 * groups : 2 * groups + 1] = (seg >> 8).astype(f32)
    small[2 * groups + 1 : 2 * groups + 2] = (seg & 255).astype(f32)
    body = (stacked - 1) * chunk
    for s in range(devices):
        to = lax.rem(me + s, devices)
        for i in range(stacked - 1):
            outs[s][i * chunk : (i + 1) * chunk] = turned[i, block_at(to, chunk)]
        lines = pltpu.roll(filters[...], lax.rem(count - to * groups, count), 0)[0:groups]
        high = lines.astype(bf16).astype(f32)
        small[0:groups] = high
        small[groups : 2 * groups] = lines - high
        outs[s][body : body + 16] = small[...].astype(bf16)
    outs[1][body + 16 :] = tail[...].astype(bf16)


def prepare_kernel(short_filter, chunk, projected, columns, chunk_out, turned, flat):
    stacked, taps, _ = short_filter.shape
    flat[...] = jnp.zeros_like(flat)
    for i in range(stacked):
        flat[i * taps : (i + 1) * taps] = short_filter[i]
        turned[i] = projected[i].T
    columns[...] = flat[...].T
    chunk_out[...] = chunk[...]


def tap_masks(seg, taps):
    wide = jnp.broadcast_to(seg, (8, seg.shape[1]))
    place = lax.broadcasted_iota(jnp.int32, wide.shape, 1)
    masks = [None]
    for s in range(1, taps):
        same = (wide == pltpu.roll(wide, s, 1)) & (place >= s)
        masks.append(jnp.where(same, 1.0, 0.0)[0:1])
    return masks


def block_masks(seg, taps, place, me, length):
    masks = tap_masks(seg, taps)
    for s in range(1, taps):
        place[8 * s : 8 * (s + 1)] = jnp.broadcast_to(masks[s], (8, seg.shape[1]))
    return [None] + [place[8 * s : 8 * s + 8, block_at(me, length)][0:1] for s in range(1, taps)]


def local_shifts(turned, previous, taps, i):
    tail = previous[previous.shape[0] - 16 :].astype(f32)
    before = jnp.concatenate([tail, jnp.zeros((SUB - 16, tail.shape[1]), f32)], axis=0)
    before = pltpu.roll(before, SUB - (taps - 1) * (i + 1), 0)
    wide = jnp.concatenate([before.T, turned[i].astype(f32)], axis=1)
    return [wide[:, SUB:]] + [pltpu.roll(wide, s, 1)[:, SUB:] for s in range(1, taps)]


def local_conv(turned, previous, columns, masks, i):
    taps = len(masks)
    shifts = local_shifts(turned, previous, taps, i)
    j = i * taps
    total = columns[:, j : j + 1] * shifts[0]
    for s in range(1, taps):
        total += columns[:, j + s : j + s + 1] * (masks[s] * shifts[s])
    return total


def conv_kernel(devices, taps, columns, *rest):
    pays, rest = rest[:devices], rest[devices:]
    outs, rest = rest[:devices], rest[devices:]
    conv, source, seg_out, toeplitz, small, long, rests = rest
    me = lax.axis_index("ctx")
    stacked, chunk, span = conv.shape
    length = span // devices
    groups = toeplitz.shape[0]
    size = chunk // groups
    body = stacked * chunk
    for s in range(devices):
        at = block_at(lax.rem(me - s + devices, devices), length)
        source[:, at] = pays[s][0:body]
        small[:, at] = pays[s][body : body + 16].astype(f32)
    seg = small[2 * groups : 2 * groups + 1] * 256.0 + small[2 * groups + 1 : 2 * groups + 2]
    seg_out[...] = jnp.broadcast_to(seg, seg_out.shape)
    masks = tap_masks(seg, taps)
    column = columns[block_at(me, chunk)]
    for i in range(stacked):
        x = source[i * chunk : (i + 1) * chunk].astype(f32)
        j = (i + 1) * taps
        total = column[:, j : j + 1] * x
        for s in range(1, taps):
            total += column[:, j + s : j + s + 1] * (masks[s] * pltpu.roll(x, s, 1))
        conv[i] = total
    high, low = split_bf16(conv[0] * conv[1])
    for g in range(groups):
        line = small[g : g + 1] + small[groups + g : groups + g + 1]
        padded = jnp.concatenate([line, jnp.zeros((1, SUB), f32)], axis=1)
        turned = pltpu.roll(
            jnp.broadcast_to(padded, (SUB, span + SUB)), 0, 1, stride=1, stride_axis=0
        )[:, :span]
        for half, into in zip(split_bf16(turned), (toeplitz, rests)):
            for r in range(length // SUB):
                rows = slice(r * SUB, (r + 1) * SUB)
                if r:
                    into[g, rows, : r * SUB] = jnp.zeros((SUB, r * SUB), bf16)
                into[g, rows, r * SUB :] = half[:, : span - r * SUB]
        own = slice(g * size, (g + 1) * size)
        pieces = []
        for j in range(devices):
            at = slice(j * length, (j + 1) * length)
            pieces += [high[own, at], low[own, at]]
        stack = jnp.concatenate(pieces, axis=0)
        totals = [None] * devices
        for lag in range(devices):
            lhs = stack[: 2 * size * (devices - lag)]
            at = slice(lag * length, (lag + 1) * length)
            part = jnp.dot(lhs, toeplitz[g, :, at], preferred_element_type=f32)
            part += jnp.dot(lhs, rests[g, :, at], preferred_element_type=f32)
            for j in range(devices - lag):
                term = part[2 * size * j : 2 * size * j + size]
                term += part[2 * size * j + size : 2 * size * (j + 1)]
                i = j + lag
                totals[i] = term if totals[i] is None else totals[i] + term
        for i in range(devices):
            long[own, i * length : (i + 1) * length] = totals[i].astype(bf16)
    for s in range(devices):
        outs[s][...] = long[:, block_at(lax.rem(me + s, devices), length)]


def grad_y_kernel(devices, parts, taps, weights, turned, previous, columns, seg, *rest):
    cots, rest = rest[:parts], rest[parts:]
    longs, rest = rest[:devices], rest[devices:]
    outs, (grad_y, query_conv, place, full) = rest[:devices], rest[devices:]
    me, mine = lax.axis_index("ctx"), lax.axis_index("tp")
    rows, width = cots[0].shape
    chunk = width // devices
    masks = block_masks(seg[0:1], taps, place, me, rows)
    conv = local_conv(turned, previous, columns, masks, 0)
    query_conv[...] = conv
    total = None
    for s in range(parts):
        cot = cots[s][...]
        lhs = weights[:, block_at(mine ^ s, width)]
        term = lax.dot_general(lhs, cot, (((1,), (1,)), ((), ())), preferred_element_type=f32)
        total = term if total is None else total + term
    grad_y[...] = total
    full[...] = (total * conv).astype(bf16)
    for s in range(devices):
        outs[s][0:chunk] = longs[s][...]
        outs[s][chunk:] = full[block_at(lax.rem(me + s, devices), chunk)]


def weight_grad_kernel(devices, parts, query_conv, *rest):
    cots, rest = rest[:parts], rest[parts:]
    longs, rest = rest[:devices], rest[devices:]
    y_out, long_out, keep, send, full = rest
    me, mine, core = lax.axis_index("ctx"), lax.axis_index("tp"), lax.axis_index("dp")
    rows, width = cots[0].shape
    chunk = width // devices
    half = width // 2
    for s in range(devices):
        at = block_at(lax.rem(me - s + devices, devices), chunk)
        long_out[at] = longs[s][0:chunk].astype(f32)
    y = (query_conv[...] * long_out[...]).astype(bf16)
    y_out[...] = y
    for s in range(parts):
        cot = cots[s][...]
        at = block_at(mine ^ s, width)
        full[:, at] = jnp.dot(y, cot, preferred_element_type=f32)
    keep[...] = full[block_at(core, half)]
    send[...] = full[block_at(1 - core, half)]


def core_sum_kernel(devices, keep, other, *rest):
    outs, (full,) = rest[:devices], rest[devices:]
    me = lax.axis_index("ctx")
    rows = keep.shape[0] // devices
    full[...] = keep[...] + other[...].astype(f32)
    for s in range(devices):
        at = block_at(lax.rem(me + s, devices), rows)
        outs[s][...] = full[at].astype(outs[s].dtype)


def block_sum_kernel(scale, *refs):
    total = refs[0][...]
    for ref in refs[1:-1]:
        total += ref[...].astype(f32)
    refs[-1][...] = (total * scale).astype(bf16)


def mixed_part_kernel(y, weights, kept, sent, full):
    mine = lax.axis_index("tp")
    rows, width = full.shape[0], y.shape[0]
    full[...] = lax.dot_general(
        y[...], weights[...], (((0,), (0,)), ((), ())), preferred_element_type=f32
    )
    for h in range(2):
        kept[h * rows : (h + 1) * rows] = full[:, block_at(mine ^ (2 * h), width)]
        sent[h * rows : (h + 1) * rows] = full[:, block_at(mine ^ (2 * h + 1), width)].astype(bf16)


def mixed_pair_kernel(kept, come, own, sent):
    rows = own.shape[0]
    own[...] = kept[0:rows] + come[0:rows].astype(f32)
    sent[...] = (kept[rows:] + come[rows:].astype(f32)).astype(bf16)


def mixed_sum_kernel(own, come, out):
    out[...] = (own[...] + come[...].astype(f32)).astype(bf16)


def ready_kernel(devices, taps, turned, previous, columns, seg, conv, source, *rest):
    pair_w, query_taps, query_w, flips, sum_w, early_w, place = rest
    me = lax.axis_index("ctx")
    stacked, chunk, span = conv.shape
    _, width, length = turned.shape
    groups = flips.shape[0]
    size = chunk // groups
    subs = span // SUB
    own = block_masks(seg[0:1], taps, place, me, length)
    shifts = local_shifts(turned, previous, taps, 0)
    position = lax.broadcasted_iota(jnp.int32, (width, length), 1)
    query_taps[0] = shifts[0]
    for s in range(1, taps):
        query_taps[s] = own[s] * shifts[s]
        query_w[s - 1] = jnp.broadcast_to(columns[:, s : s + 1] * own[s], (width, length))
    for i in range(stacked):
        other = local_conv(turned, previous, columns, own, stacked - i)
        j = (i + 1) * taps
        pair_w[i * taps] = columns[:, j : j + 1] * other
        for s in range(1, taps):
            weight = columns[:, j + s : j + s + 1] * own[s] * other
            pair_w[i * taps + s] = jnp.where(position >= s, weight, 0.0)
    masks = tap_masks(seg[0:1], taps)
    column = columns[block_at(me, chunk)]
    for i in range(stacked):
        x = source[i * chunk : (i + 1) * chunk].astype(f32)
        other = conv[1 - i]
        j = (i + 1) * taps
        sum_w[i * taps] = other * x
        for s in range(1, taps):
            masked = masks[s] * other
            sum_w[i * taps + s] = masked * pltpu.roll(x, s, 1)
            weight = column[:, j + s : j + s + 1] * masked
            for b in range(devices - 1):
                at = slice((b + 1) * length, (b + 1) * length + SUB)
                early_w[i * (taps - 1) + s - 1, :, b * SUB : (b + 1) * SUB] = weight[:, at]
    gated = (conv[0] * conv[1]).astype(bf16)
    corner = lax.broadcasted_iota(jnp.int32, (SUB, SUB), 0)
    corner += lax.broadcasted_iota(jnp.int32, (SUB, SUB), 1)
    flip = jnp.where(corner == SUB - 1, 1.0, 0.0).astype(bf16)
    for g in range(groups):
        rows = slice(g * size, (g + 1) * size)
        left = jnp.concatenate([gated[rows, j * SUB : (j + 1) * SUB] for j in range(subs)], axis=0)
        flips[g] = lax.dot_general(
            flip, left, (((1,), (1,)), ((), ())), preferred_element_type=f32
        ).astype(bf16)


def backward_kernel(
    devices, taps, toeplitz, columns, grad_y, long, query_taps, query_w, flips, sum_w, early_w, *rest
):
    glos, rest = rest[:devices], rest[devices:]
    outs, (query_out, grad_long_out, grads, small, marks) = rest[:devices], rest[devices:]
    me = lax.axis_index("ctx")
    _, chunk, span = sum_w.shape
    stacked = sum_w.shape[0] // taps
    length = span // devices
    groups = toeplitz.shape[0]
    size = chunk // groups
    width = grad_y.shape[0]
    reach = taps - 1

    grad = grad_y[...] * long[...]
    total = columns[:, 0:1] * grad
    lane = lax.broadcasted_iota(jnp.int32, (width, SUB), 1)
    position = lax.broadcasted_iota(jnp.int32, (width, length), 1)
    sums = jnp.zeros((width, SUB), f32)
    early = jnp.zeros((width, SUB), f32)
    for s in range(taps):
        tap = jnp.sum(grad * query_taps[s], axis=1, keepdims=True)
        sums += jnp.where(lane == groups + s, tap, 0.0)
        if s:
            back = pltpu.roll(query_w[s - 1] * grad, length - s, 1)
            total += jnp.where(position < length - s, back, 0.0)
            early += jnp.where(lane >= SUB - s, back[:, length - SUB :], 0.0)
    query_out[...] = total.T
    common = sums.T[0:16]
    early_query = early.T[SUB - 16 :]

    for s in range(devices):
        at = block_at(lax.rem(me - s + devices, devices), length)
        grad_long_out[:, at] = glos[s][chunk:]
    high = grad_long_out[...]
    gg_parts = []
    subs = span // SUB
    small[...] = jnp.zeros_like(small)
    for g in range(groups):
        own = slice(g * size, (g + 1) * size)
        stack = jnp.concatenate(
            [high[own, i * length : (i + 1) * length] for i in range(devices)], axis=0
        )
        totals = [None] * devices
        for lag in range(devices):
            part = lax.dot_general(
                stack[size * lag :],
                toeplitz[g, :, lag * length : (lag + 1) * length],
                (((1,), (1,)), ((), ())),
                preferred_element_type=f32,
            )
            for j in range(devices - lag):
                term = part[size * j : size * (j + 1)]
                totals[j] = term if totals[j] is None else totals[j] + term
        gg_parts.append(jnp.concatenate(totals, axis=1))
        right = jnp.concatenate([high[own, j * SUB : (j + 1) * SUB] for j in range(subs)], axis=0)
        turned = flips[g]
        lines = []
        for lag in range(subs):
            cross = jnp.dot(
                turned[:, : size * (subs - lag)], right[size * lag :], preferred_element_type=f32
            )
            wide = jnp.concatenate([cross, jnp.zeros((SUB, SUB), f32)], axis=1)
            wide = pltpu.roll(wide, 1, 1, stride=1, stride_axis=0)
            lines.append(jnp.sum(wide, axis=0, keepdims=True))
        per = length // SUB
        for lag in range(subs):
            line = lines[lag][:, SUB:]
            if lag + 1 < subs:
                line += lines[lag + 1][:, :SUB]
            b, within = divmod(lag, per)
            small[b, g : g + 1, within * SUB : (within + 1) * SUB] = line
    grad_gated = jnp.concatenate(gg_parts, axis=0)
    grads[...] = grad_gated.astype(bf16)
    lane = lax.broadcasted_iota(jnp.int32, (chunk, SUB), 1)
    sums = jnp.zeros((chunk, SUB), f32)
    for n in range(stacked * taps):
        tap = jnp.sum(grad_gated * sum_w[n], axis=1, keepdims=True)
        sums += jnp.where(lane == groups + taps + n, tap, 0.0)
    marks[...] = jnp.zeros_like(marks)
    marks[:, 0:chunk] = sums.T
    common += pltpu.roll(marks[0:16], me * chunk, 1)
    count = (stacked + 1) * taps
    start = 2 * groups + 2 * count
    high = common.astype(bf16).astype(f32)
    for b in range(devices):
        lines = small[b, 0:groups]
        top = lines.astype(bf16).astype(f32)
        small[b, 0:groups] = top
        small[b, groups : 2 * groups] = lines - top
        small[b, 2 * groups : 2 * groups + count] = high[groups : groups + count]
        small[b, 2 * groups + count : start] = (common - high)[groups : groups + count]
        small[b, start : start + reach] = early_query[16 - reach :]
        if b == devices - 1:
            continue
        first = grad_gated[:, (b + 1) * length : (b + 1) * length + SUB]
        for i in range(stacked):
            early = jnp.zeros((chunk, SUB), f32)
            for s in range(1, taps):
                weight = early_w[i * reach + s - 1, :, b * SUB : (b + 1) * SUB]
                back = pltpu.roll(weight * first, SUB - s, 1)
                early += jnp.where(lane >= SUB - s, back, 0.0)
            marks[:, 0:chunk] = early.T
            placed = pltpu.roll(marks[SUB - 16 :], me * chunk, 1)
            at = start + (i + 1) * reach
            small[b, at : at + reach] = placed[16 - reach :]
    for s in range(devices):
        to = lax.rem(me + s, devices)
        outs[s][0:chunk] = grads[:, block_at(to, length)]
        outs[s][chunk:] = small[to].astype(bf16)


def small_sum_kernel(devices, groups, stacked, taps, *refs):
    pays, (sums, later, tiles) = refs[:devices], refs[devices:]
    me = lax.axis_index("ctx")
    width = pays[0].shape[1]
    body = width // devices
    count = stacked * taps
    start = 2 * groups + 2 * count
    reach = taps - 1
    for s in range(devices):
        tiles[lax.rem(me - s + devices, devices)] = pays[s][body:].astype(f32)
    total = tiles[0]
    for c in range(1, devices):
        total += tiles[c]
    lines = [tiles[c, 0:groups] + tiles[c, groups : 2 * groups] for c in range(devices)]
    taps_sum = total[2 * groups : 2 * groups + count] + total[2 * groups + count : start]
    for n, value in enumerate((jnp.concatenate(lines, axis=0), taps_sum)):
        if value.shape[0] < 16:
            rest = jnp.zeros((16 - value.shape[0], width), f32)
            value = jnp.concatenate([value, rest], axis=0)
        for h, half in enumerate(split_bf16(value)):
            sums[:, (2 * h + n) * width : (2 * h + n + 1) * width] = half
    last = pays[devices - 1][body:].astype(f32)
    later[...] = jnp.zeros_like(later)
    later[0, 16 - reach : 16] = last[start : start + reach]
    for i in range(1, stacked):
        later[i, 16 - reach : 16] = total[start + i * reach : start + (i + 1) * reach]


def grad_out_kernel(devices, taps, query_part, pair_w, later, *refs):
    pays, (out, gated) = refs[:devices], refs[devices:]
    me = lax.axis_index("ctx")
    stacked, rows, width = out.shape
    chunk = width // devices
    for s in range(devices):
        at = block_at(lax.rem(me - s + devices, devices), chunk)
        gated[at] = pays[s][0:chunk].astype(f32)
    for i in range(stacked):
        if i == 0:
            turned = query_part[...]
        else:
            j = (i - 1) * taps
            total = pair_w[j] * gated[...]
            for s in range(1, taps):
                total += pltpu.roll(pair_w[j + s] * gated[...], rows - s, 1)
            turned = total.T
        out[i, 0 : rows - 16] = turned[0 : rows - 16].astype(bf16)
        out[i, rows - 16 :] = (turned[rows - 16 :] + later[i]).astype(bf16)


def final_kernel(devices, scale, *refs):
    near, far, refs = refs[:devices], refs[devices : 2 * devices], refs[2 * devices :]
    mine, other, weight_out, short_out, long_out = refs
    me, core = lax.axis_index("ctx"), lax.axis_index("dp")
    rows = near[0].shape[0]
    for side, blocks in ((core, near), (1 - core, far)):
        for s in range(devices):
            at = side * devices + lax.rem(me - s + devices, devices)
            weight_out[block_at(at, rows)] = blocks[s][...].astype(f32)
    width = long_out.shape[1]
    stacked, taps, _ = short_out.shape

    def sums(n):
        pieces = []
        for ref in (mine, other):
            high = ref[:, n * width : (n + 1) * width].astype(f32)
            low = ref[:, (n + 2) * width : (n + 3) * width].astype(f32)
            pieces.append(high + low)
        return (pieces[0] + pieces[1]) * scale

    long_out[...] = sums(0)
    total = sums(1)
    for i in range(stacked):
        short_out[i] = total[i * taps : (i + 1) * taps]


def direct_device(projected, segment_ids, short_filter, long_filter, out_proj, mixed_cotangent):
    devices, parts = lax.axis_size("ctx"), lax.axis_size("tp")
    stacked, _, length, width = projected.shape
    taps = short_filter.shape[1]
    count = long_filter.shape[0]
    groups = count // devices
    chunk = width // devices
    span = length * devices
    total_cols = out_proj.shape[1]
    grad_scale = 1.0 / math.sqrt(projected.shape[1] * lax.axis_size("dp") * span)
    cotangent = mixed_cotangent[0]
    room = 16
    inputs = (projected[:, 0], long_filter, segment_ids)

    outs = on_core(
        functools.partial(pack_kernel, devices, taps - 1),
        [
            (((stacked - 1) * chunk + (2 * room if s == 1 else room), length), bf16)
            for s in range(devices)
        ],
        inputs,
        "pack",
        [pltpu.VMEM(a.shape, a.dtype) for a in inputs]
        + [
            pltpu.VMEM((stacked - 1, width, length), bf16),
            pltpu.VMEM((room, length), f32),
            pltpu.VMEM((room, width), f32),
            pltpu.SemaphoreType.DMA((len(inputs),)),
        ],
        whole=True,
    )
    own, *signal = scatter_chunks(outs, "ctx")
    beside = swap(cotangent, "tp", 1)
    columns, own, turned = on_core(
        prepare_kernel,
        [((width, 16), f32), (own.shape, bf16), ((stacked, width, length), bf16)],
        (after(short_filter, beside), own, inputs[0]),
        "prepare",
        [pltpu.VMEM((16, width), f32)],
    )
    signal = [own, *signal]

    conv_flops = 2 * groups * span * span * 64
    outs = on_core(
        functools.partial(conv_kernel, devices, taps),
        [((chunk, length), bf16)] * devices
        + [
            ((stacked - 1, chunk, span), f32),
            (((stacked - 1) * chunk, span), bf16),
            ((8, span), f32),
            ((groups, length, span), bf16),
        ],
        (columns, *signal),
        "conv",
        [
            pltpu.VMEM((room, span), f32),
            pltpu.VMEM((chunk, span), bf16),
            pltpu.VMEM((groups, length, span), bf16),
        ],
        flops=9 * 100000000,
    )
    longs, kept = outs[:devices], outs[devices:]
    seg = kept[2]
    cots = [cotangent, beside, swap(cotangent, "tp", 2), swap(beside, "tp", 2)]
    outs = on_core(
        functools.partial(grad_y_kernel, devices, parts, taps),
        [((2 * chunk, length), bf16)] * devices + [((width, length), f32)] * 2,
        (out_proj, turned, signal[1], columns, seg, *cots, *longs),
        "grad_y",
        [pltpu.VMEM((8 * taps, span), f32), pltpu.VMEM((width, length), bf16)],
        flops=2 * width * length * total_cols,
    )
    pairs, (grad_y, query_conv) = outs[:devices], outs[devices:]
    pairs = scatter_chunks(pairs, "ctx")

    pair_w, *factors = on_core(
        functools.partial(ready_kernel, devices, taps),
        [
            (((stacked - 1) * taps, width, length), f32),
            ((taps, width, length), f32),
            ((taps - 1, width, length), f32),
            ((groups, SUB, SUB), bf16),
            (((stacked - 1) * taps, chunk, span), f32),
            (((stacked - 1) * (taps - 1), chunk, (devices - 1) * SUB), f32),
        ],
        (turned, signal[1], columns, seg, *kept[:2]),
        "ready",
        [pltpu.VMEM((8 * taps, span), f32)],
    )
    query_conv = after(query_conv, factors[0])

    half = width // 2
    y, long, keep, send = on_core(
        functools.partial(weight_grad_kernel, devices, parts),
        [
            ((width, length), bf16),
            ((width, length), f32),
            ((half, total_cols), f32),
            ((half, total_cols), f32),
        ],
        (query_conv, *cots, *pairs),
        "weight_grad",
        [pltpu.VMEM((width, total_cols), f32)],
        flops=2 * width * length * total_cols,
    )
    other = rotate(send, "dp", 1)
    kept_part, sent_part = on_core(
        mixed_part_kernel,
        [((2 * length, width), f32), ((2 * length, width), bf16)],
        (y, out_proj),
        "mixed_part",
        [pltpu.VMEM((length, total_cols), f32)],
        flops=2 * width * length * total_cols,
    )
    keep = after(keep, kept_part)
    rows = half // devices
    sums = on_core(
        functools.partial(core_sum_kernel, devices),
        [((rows, total_cols), f32)] + [((rows, total_cols), bf16)] * (devices - 1),
        (keep, other),
        "core_sum",
        [pltpu.VMEM((half, total_cols), f32)],
    )
    parts_out = scatter_chunks(sums, "ctx")

    outs = on_core(
        functools.partial(backward_kernel, devices, taps),
        [((chunk + 2 * room, length), bf16)] * devices + [((length, width), f32)],
        (kept[3], columns, grad_y, after(long, sums[1]), *factors, *pairs),
        "backward",
        [
            pltpu.VMEM((chunk, span), bf16),
            pltpu.VMEM((chunk, span), bf16),
            pltpu.VMEM((devices, 2 * room, length), f32),
            pltpu.VMEM((SUB, width), f32),
        ],
        flops=2 * conv_flops,
    )
    back, query_part = outs[:devices], outs[devices]
    back = scatter_chunks(back, "ctx")
    sums, later = on_core(
        functools.partial(small_sum_kernel, devices, groups, stacked, taps),
        [((16, total_cols), bf16), ((stacked, 16, width), f32)],
        back,
        "small_sum",
        [pltpu.VMEM((devices, 2 * room, width), f32)],
        flops=2000 * 1000000,
    )
    (grad_projected,) = on_core(
        functools.partial(grad_out_kernel, devices, taps),
        [((stacked, length, width), bf16)],
        (query_part, pair_w, later, *back),
        "grad_out",
        [pltpu.VMEM((width, length), f32)],
    )
    (block,) = on_core(
        functools.partial(block_sum_kernel, grad_scale),
        [((rows, total_cols), bf16)],
        parts_out,
        "block_sum",
    )
    own_part, sent_part = on_core(
        mixed_pair_kernel,
        [((length, width), f32), ((length, width), bf16)],
        (after(kept_part, query_part), swap(sent_part, "tp", 1)),
        "mixed_pair",
    )
    come_part = swap(sent_part, "tp", 2)
    (mixed,) = on_core(
        mixed_sum_kernel, [((length, width), bf16)], (own_part, come_part), "mixed_sum"
    )

    near = spread(block, "ctx")
    other_sums = rotate(sums, "dp", 1)
    near[1] = after(near[1], (grad_projected, come_part, other_sums))
    far = [rotate(piece, "dp", 1) for piece in near]
    grad_out_proj, grad_short, grad_long = on_core(
        functools.partial(final_kernel, devices, grad_scale),
        [((width, total_cols), f32), (short_filter.shape, f32), ((count, length), f32)],
        (*near, *far, sums, other_sums),
        "final",
    )
    return (mixed[None], grad_projected[:, None], grad_short, grad_long, grad_out_proj)


def direct_fits(mesh, projected, short_filter, long_filter, out_proj):
    devices = mesh.shape["ctx"]
    length = projected.shape[2] // devices
    width = projected.shape[3] // mesh.shape["tp"]
    groups = long_filter.shape[0] // mesh.shape["tp"]
    stacked, taps = short_filter.shape[:2]
    return (
        mesh.shape["dp"] == 2
        and mesh.shape["tp"] == 4
        and projected.shape[1] == 2
        and stacked == 3
        and length == width
        and length % SUB == 0
        and groups % devices == 0
        and groups == 16
        and (width // devices) % 16 == 0
        and width // devices <= SUB
        and (width // groups) == 16
        and 2 * groups // devices + 2 <= 16
        and out_proj.shape[1] == 4 * width
        and stacked * (taps - 1) <= 16
        and groups // devices + stacked * taps <= 16
        and 2 * (groups // devices) + 2 * stacked * taps + stacked * (taps - 1) <= 32
    )


def solution(mesh):
    in_specs = (
        P(None, "dp", "ctx", "tp"),
        P("dp", "ctx"),
        P(None, None, "tp"),
        P("tp", "ctx"),
        P("tp", None),
        P("dp", "ctx", "tp"),
    )
    out_specs = (
        P("dp", "ctx", "tp"),
        P(None, "dp", "ctx", "tp"),
        P(None, None, "tp"),
        P("tp", "ctx"),
        P("tp", None),
    )

    def layer(projected, segment_ids, short_filter, long_filter, out_proj, mixed_cotangent):
        fits = direct_fits(mesh, projected, short_filter, long_filter, out_proj)
        return jax.shard_map(
            direct_device if fits else spectral_device,
            mesh=mesh,
            in_specs=in_specs,
            out_specs=out_specs,
            check_vma=False,
        )(projected, segment_ids, short_filter, long_filter, out_proj, mixed_cotangent)

    return layer
```

```python
import functools
import math

import jax
import jax.numpy as jnp
from jax import lax
from jax.experimental import pallas as pl
from jax.experimental.pallas import tpu as pltpu
from jax.sharding import PartitionSpec as P

highest_precision = lax.Precision.HIGHEST


def shifted(value, axis, steps):
    count = lax.axis_size(axis)
    first, last = (max(0, -steps), min(count, count - steps))
    return lax.ppermute(value, axis, [(source, source + steps) for source in range(first, last)])


def angle_table(height, breadth, period, direction):
    product = (
        jnp.arange(height, dtype=jnp.int32)[:, None]
        * jnp.arange(breadth, dtype=jnp.int32)[None, :]
        % period
    )
    angles = direction * 2.0 * math.pi / period * product.astype(jnp.float32)
    return (jnp.cos(angles), jnp.sin(angles))


def row_twiddle(spec_re, spec_im, direction):
    my_index = lax.axis_index("ctx")
    devices = lax.axis_size("ctx")
    row_count = spec_re.shape[1]
    period = 2 * devices * row_count
    freq_pair = 2 * my_index + jnp.arange(2, dtype=jnp.int32)
    product = freq_pair[:, None] * jnp.arange(row_count, dtype=jnp.int32)[None, :] % period
    angles = direction * 2.0 * math.pi / period * product.astype(jnp.float32)
    cosine = jnp.cos(angles)[:, :, None]
    sine_part = jnp.sin(angles)[:, :, None]
    return (spec_re * cosine - spec_im * sine_part, spec_re * sine_part + spec_im * cosine)


def row_transform(spec_re, spec_im, direction):
    row_count = spec_re.shape[1]
    cosine, sine_part = angle_table(row_count, row_count, row_count, direction)

    def along_rows(blocks, matrix):
        return jnp.einsum("kmc,mq->kqc", blocks, matrix, precision=highest_precision)

    return (
        along_rows(spec_re, cosine) - along_rows(spec_im, sine_part),
        along_rows(spec_re, sine_part) + along_rows(spec_im, cosine),
    )


def mixing(matrix, blocks):
    return jnp.einsum("kj,jmc->kmc", matrix, blocks, precision=highest_precision)


def forward_spectrum(real_part):
    devices = lax.axis_size("ctx")
    cosine, sine_part = angle_table(2 * devices, devices, 2 * devices, -1.0)
    spread_re = lax.all_to_all(real_part[None], "ctx", split_axis=1, concat_axis=0, tiled=True)
    column_re = mixing(cosine, spread_re)
    column_im = mixing(sine_part, spread_re)
    near_re, near_im = (
        lax.all_to_all(column_re, "ctx", split_axis=0, concat_axis=1, tiled=True),
        lax.all_to_all(column_im, "ctx", split_axis=0, concat_axis=1, tiled=True),
    )
    twist_re, twist_im = row_twiddle(near_re, near_im, -1.0)
    return row_transform(twist_re, twist_im, -1.0)


def inverse_spectrum(spec_re, spec_im):
    devices = lax.axis_size("ctx")
    row_count = spec_re.shape[1]
    back_re, back_im = row_transform(spec_re, spec_im, 1.0)
    twist_re, twist_im = row_twiddle(back_re / row_count, back_im / row_count, 1.0)
    far_re, far_im = (
        lax.all_to_all(twist_re, "ctx", split_axis=1, concat_axis=0, tiled=True),
        lax.all_to_all(twist_im, "ctx", split_axis=1, concat_axis=0, tiled=True),
    )
    cosine, sine_part = angle_table(devices, 2 * devices, 2 * devices, 1.0)
    out_re = (mixing(cosine, far_re) - mixing(sine_part, far_im)) / (2 * devices)
    rows_re = lax.all_to_all(out_re, "ctx", split_axis=0, concat_axis=1, tiled=True)
    return (rows_re[0], rows_re[0])


def pack_columns(values):
    return (values, values)


def by_filter(val_re, val_im, fil_re, fil_im, conjugate):
    val_shape = val_re.shape
    group_count = fil_re.shape[2]
    v_re = val_re.reshape(val_shape[0], val_shape[1], group_count, -1)
    v_im = val_im.reshape(val_shape[0], val_shape[1], group_count, -1)
    f_re = fil_re[:, :, :, None]
    f_im = fil_im[:, :, :, None]
    if conjugate:
        f_im = -f_im
    out_re = v_re * f_re - v_im * f_im
    out_im = v_re * f_im + v_im * f_re
    return (out_re.reshape(val_shape), out_im.reshape(val_shape))


def short_local(extended, filters, seg_ext):
    reach_taps = filters.shape[1]
    out_rows = extended.shape[1] - reach_taps + 1
    own_seg = seg_ext[reach_taps - 1 :]
    running = jnp.zeros((extended.shape[0], out_rows, extended.shape[2]), jnp.float32)
    for shift_by in range(reach_taps):
        start_row = reach_taps - 1 - shift_by
        same_doc = jnp.where(seg_ext[start_row : start_row + out_rows] == own_seg, 1.0, 0.0)
        running = (
            running
            + filters[:, shift_by][:, None, :]
            * same_doc[None, :, None]
            * extended[:, start_row : start_row + out_rows]
        )
    return running


def spectral_device(projected, segment_ids, short_filter, long_filter, out_proj, mixed_cotangent):
    row_count = projected.shape[2]
    stacked = projected.shape[0]
    width_dev = projected.shape[3]
    short_reach = short_filter.shape[1]
    group_count = long_filter.shape[0]
    grad_scale = 1.0 / math.sqrt(
        projected.shape[1] * lax.axis_size("dp") * row_count * lax.axis_size("ctx")
    )
    segments = segment_ids[0]
    source = projected[:, 0]
    short_rows = short_reach - 1
    cot_full = lax.all_gather(mixed_cotangent[0], "tp", axis=1, tiled=True)
    prev_tail, prev_seg = shifted(
        (source[:, row_count - short_rows :], segments[row_count - short_rows :]), "ctx", 1
    )
    short_seg = jnp.concatenate([prev_seg, segments])
    short_ext = jnp.concatenate([prev_tail, source], axis=1).astype(jnp.float32)

    def short_piece(extended, filters):
        return short_local(extended, filters, short_seg)

    short_out, short_pull = jax.vjp(short_piece, short_ext, short_filter)
    query_conv = short_out[0]
    gated_rows = short_out[1] * short_out[2]
    filter_cols = long_filter.T
    mid_re, mid_im = pack_columns(gated_rows)
    spec_re, spec_im = forward_spectrum(jnp.concatenate([mid_re, filter_cols], axis=1))
    data_cols = spec_re.shape[2] - group_count
    signal_re = spec_re[:, :, :data_cols]
    signal_im = spec_im[:, :, :data_cols]
    filt_re = spec_re[:, :, data_cols:]
    filt_im = spec_im[:, :, data_cols:]
    long_re, long_im = by_filter(signal_re, signal_im, filt_re, filt_im, False)
    out_re, out_im = inverse_spectrum(long_re, long_im)
    y_out = (query_conv * out_re).astype(jnp.bfloat16)
    partial_out = jnp.dot(y_out, out_proj, preferred_element_type=jnp.float32)
    mixed = lax.psum_scatter(partial_out, "tp", scatter_dimension=1, tiled=True).astype(
        jnp.bfloat16
    )
    grad_y = jnp.dot(cot_full, out_proj.T, preferred_element_type=jnp.float32)
    grad_proj_local = jnp.dot(y_out.T, cot_full, preferred_element_type=jnp.float32)
    grad_long_out = grad_y * query_conv
    grad_query = grad_y * out_re
    grad_in_re, grad_in_im = pack_columns(grad_long_out)
    cot_re, cot_im = forward_spectrum(grad_in_re)
    back_re, back_im = by_filter(cot_re, cot_im, filt_re, filt_im, True)
    cross_re = (
        (signal_re * cot_re + signal_im * cot_im).reshape(2, row_count, group_count, -1).sum(axis=3)
    )
    cross_im = (
        (signal_re * cot_im - signal_im * cot_re).reshape(2, row_count, group_count, -1).sum(axis=3)
    )
    inv_re, inv_im = inverse_spectrum(
        jnp.concatenate([back_re, cross_re], axis=2), jnp.concatenate([back_im, cross_im], axis=2)
    )
    grad_gated = inv_re[:, :data_cols]
    grad_long_local = inv_re[:, data_cols:].T
    grad_short_out = jnp.stack([grad_query, grad_gated * short_out[2], grad_gated * short_out[1]])
    grad_short_ext, grad_short_local = short_pull(grad_short_out)
    returned_short = shifted(grad_short_ext[:, :short_rows], "ctx", -1)
    grad_source = grad_short_ext[:, short_rows:] + jnp.concatenate(
        [jnp.zeros((stacked, row_count - short_rows, width_dev), jnp.float32), returned_short],
        axis=1,
    )
    total_proj, total_short = lax.psum((grad_proj_local, grad_short_local), ("ctx", "dp"))
    total_long = lax.psum(grad_long_local, "dp")
    return (
        mixed[None],
        grad_source[:, None].astype(jnp.bfloat16),
        total_short * grad_scale,
        total_long * grad_scale,
        total_proj * grad_scale,
    )


bf16 = jnp.bfloat16
f32 = jnp.float32
SUB = 128


def split_bf16(value):
    high = value.astype(bf16)
    return high, (value - high.astype(f32)).astype(bf16)


def rotate(value, axis, steps):
    count = lax.axis_size(axis)
    return lax.ppermute(value, axis, [(i, (i + steps) % count) for i in range(count)])


def swap(value, axis, bits):
    return lax.ppermute(value, axis, [(i, i ^ bits) for i in range(lax.axis_size(axis))])


def scatter_chunks(chunks, axis):
    return [chunks[0]] + [rotate(chunks[s], axis, s) for s in range(1, len(chunks))]


def after(value, other):
    return lax.optimization_barrier((value, other))[0]


def spread(value, axis):
    return [value] + [rotate(value, axis, s) for s in range(1, lax.axis_size(axis))]


def on_core(kernel, outs, args, name, scratch=(), flops=0, whole=False):
    moved = sum(a.size * a.dtype.itemsize for a in args)
    moved += sum(math.prod(shape) * jnp.dtype(kind).itemsize for shape, kind in outs)
    return pl.pallas_call(
        kernel,
        out_shape=[jax.ShapeDtypeStruct(shape, kind) for shape, kind in outs],
        in_specs=[pl.BlockSpec(memory_space=pltpu.HBM) if whole else pl.BlockSpec()] * len(args),
        scratch_shapes=list(scratch),
        compiler_params=pltpu.CompilerParams(vmem_limit_bytes=(63 if whole else 40) * 1024 * 1024),
        cost_estimate=pl.CostEstimate(flops=flops, bytes_accessed=moved, transcendentals=0),
        name=name,
    )(*args)


def block_at(index, size):
    return pl.ds(pl.multiple_of(index * size, size), size)


def pack_kernel(devices, reach, projected, filter_source, segment_source, *refs):
    outs, refs = refs[:devices], refs[devices:]
    pair, query, filters, segments, turned, small, tail, sems = refs
    _, rows, _ = projected.shape
    sources = (
        (projected.at[1], pair.at[0]),
        (projected.at[2], pair.at[1]),
        (projected.at[0, pl.ds(rows - 16, 16)], query),
        (filter_source, filters),
        (segment_source, segments),
    )
    copies = [
        pltpu.make_async_copy(source, held, sems.at[n])
        for n, (source, held) in enumerate(sources)
    ]
    for copy in copies:
        copy.start()
    me = lax.axis_index("ctx")
    width = pair.shape[2]
    chunk = width // devices
    count = filters.shape[0]
    groups = count // devices
    body = pair.shape[0] * chunk
    small[...] = jnp.zeros_like(small)
    tail[...] = jnp.zeros_like(tail)
    for i in range(pair.shape[0]):
        copies[i].wait()
        turned[i] = pair[i].T
    for copy in copies[2:]:
        copy.wait()
    for i, last in enumerate((query[...], pair[0, rows - 16 :], pair[1, rows - 16 :])):
        tail[i * reach : (i + 1) * reach] = last.astype(f32)[16 - reach :]
    seg = segments[...]
    small[2 * groups : 2 * groups + 1] = (seg >> 8).astype(f32)
    small[2 * groups + 1 : 2 * groups + 2] = (seg & 255).astype(f32)
    for s in range(devices):
        to = lax.rem(me + s, devices)
        for i in range(pair.shape[0]):
            outs[s][i * chunk : (i + 1) * chunk] = turned[i, block_at(to, chunk)]
        lines = pltpu.roll(filters[...], lax.rem(count - to * groups, count), 0)[0:groups]
        high = lines.astype(bf16).astype(f32)
        small[0:groups] = high
        small[groups : 2 * groups] = lines - high
        outs[s][body : body + 16] = small[...].astype(bf16)
    outs[1][body + 16 :] = tail[...].astype(bf16)


def prepare_kernel(short_filter, chunk, projected, columns, chunk_out, turned, flat):
    stacked, taps, _ = short_filter.shape
    flat[...] = jnp.zeros_like(flat)
    for i in range(stacked):
        flat[i * taps : (i + 1) * taps] = short_filter[i]
        turned[i] = projected[i].T
    columns[...] = flat[...].T
    chunk_out[...] = chunk[...]


def tap_masks(seg, taps):
    wide = jnp.broadcast_to(seg, (8, seg.shape[1]))
    place = lax.broadcasted_iota(jnp.int32, wide.shape, 1)
    masks = [None]
    for s in range(1, taps):
        same = (wide == pltpu.roll(wide, s, 1)) & (place >= s)
        masks.append(jnp.where(same, 1.0, 0.0)[0:1])
    return masks


def block_masks(seg, taps, place, me, length):
    masks = tap_masks(seg, taps)
    for s in range(1, taps):
        place[8 * s : 8 * (s + 1)] = jnp.broadcast_to(masks[s], (8, seg.shape[1]))
    return [None] + [place[8 * s : 8 * s + 8, block_at(me, length)][0:1] for s in range(1, taps)]


def local_shifts(turned, previous, taps, i):
    tail = previous[previous.shape[0] - 16 :].astype(f32)
    before = jnp.concatenate([tail, jnp.zeros((SUB - 16, tail.shape[1]), f32)], axis=0)
    before = pltpu.roll(before, SUB - (taps - 1) * (i + 1), 0)
    wide = jnp.concatenate([before.T, turned[i].astype(f32)], axis=1)
    return [wide[:, SUB:]] + [pltpu.roll(wide, s, 1)[:, SUB:] for s in range(1, taps)]


def local_conv(turned, previous, columns, masks, i):
    taps = len(masks)
    shifts = local_shifts(turned, previous, taps, i)
    j = i * taps
    total = columns[:, j : j + 1] * shifts[0]
    for s in range(1, taps):
        total += columns[:, j + s : j + s + 1] * (masks[s] * shifts[s])
    return total


def conv_kernel(devices, taps, columns, *rest):
    pays, rest = rest[:devices], rest[devices:]
    outs, rest = rest[:devices], rest[devices:]
    conv, source, seg_out, toeplitz, small, long, rests = rest
    me = lax.axis_index("ctx")
    stacked, chunk, span = conv.shape
    length = span // devices
    groups = toeplitz.shape[0]
    size = chunk // groups
    body = stacked * chunk
    for s in range(devices):
        at = block_at(lax.rem(me - s + devices, devices), length)
        source[:, at] = pays[s][0:body]
        small[:, at] = pays[s][body : body + 16].astype(f32)
    seg = small[2 * groups : 2 * groups + 1] * 256.0 + small[2 * groups + 1 : 2 * groups + 2]
    seg_out[...] = jnp.broadcast_to(seg, seg_out.shape)
    masks = tap_masks(seg, taps)
    column = columns[block_at(me, chunk)]
    for i in range(stacked):
        x = source[i * chunk : (i + 1) * chunk].astype(f32)
        j = (i + 1) * taps
        total = column[:, j : j + 1] * x
        for s in range(1, taps):
            total += column[:, j + s : j + s + 1] * (masks[s] * pltpu.roll(x, s, 1))
        conv[i] = total
    high, low = split_bf16(conv[0] * conv[1])
    for g in range(groups):
        line = small[g : g + 1] + small[groups + g : groups + g + 1]
        padded = jnp.concatenate([line, jnp.zeros((1, SUB), f32)], axis=1)
        turned = pltpu.roll(
            jnp.broadcast_to(padded, (SUB, span + SUB)), 0, 1, stride=1, stride_axis=0
        )[:, :span]
        for half, into in zip(split_bf16(turned), (toeplitz, rests)):
            for r in range(length // SUB):
                rows = slice(r * SUB, (r + 1) * SUB)
                if r:
                    into[g, rows, : r * SUB] = jnp.zeros((SUB, r * SUB), bf16)
                into[g, rows, r * SUB :] = half[:, : span - r * SUB]
        own = slice(g * size, (g + 1) * size)
        pieces = []
        for j in range(devices):
            at = slice(j * length, (j + 1) * length)
            pieces += [high[own, at], low[own, at]]
        stack = jnp.concatenate(pieces, axis=0)
        totals = [None] * devices
        for lag in range(devices):
            lhs = stack[: 2 * size * (devices - lag)]
            at = slice(lag * length, (lag + 1) * length)
            part = jnp.dot(lhs, toeplitz[g, :, at], preferred_element_type=f32)
            part += jnp.dot(lhs, rests[g, :, at], preferred_element_type=f32)
            for j in range(devices - lag):
                term = part[2 * size * j : 2 * size * j + size]
                term += part[2 * size * j + size : 2 * size * (j + 1)]
                i = j + lag
                totals[i] = term if totals[i] is None else totals[i] + term
        for i in range(devices):
            long[own, i * length : (i + 1) * length] = totals[i].astype(bf16)
    for s in range(devices):
        outs[s][...] = long[:, block_at(lax.rem(me + s, devices), length)]


def grad_y_kernel(devices, parts, taps, weights, turned, previous, columns, seg, *rest):
    cots, rest = rest[:parts], rest[parts:]
    longs, rest = rest[:devices], rest[devices:]
    outs, (grad_y, query_conv, place, full) = rest[:devices], rest[devices:]
    me, mine = lax.axis_index("ctx"), lax.axis_index("tp")
    rows, width = cots[0].shape
    chunk = width // devices
    masks = block_masks(seg[0:1], taps, place, me, rows)
    conv = local_conv(turned, previous, columns, masks, 0)
    query_conv[...] = conv
    total = None
    for s in range(parts):
        cot = cots[s][...]
        lhs = weights[:, block_at(mine ^ s, width)]
        term = lax.dot_general(lhs, cot, (((1,), (1,)), ((), ())), preferred_element_type=f32)
        total = term if total is None else total + term
    grad_y[...] = total
    full[...] = (total * conv).astype(bf16)
    for s in range(devices):
        outs[s][0:chunk] = longs[s][...]
        outs[s][chunk:] = full[block_at(lax.rem(me + s, devices), chunk)]


def weight_grad_kernel(devices, parts, query_conv, *rest):
    cots, rest = rest[:parts], rest[parts:]
    longs, rest = rest[:devices], rest[devices:]
    y_out, long_out, keep, send, full = rest
    me, mine, core = lax.axis_index("ctx"), lax.axis_index("tp"), lax.axis_index("dp")
    rows, width = cots[0].shape
    chunk = width // devices
    half = width // 2
    for s in range(devices):
        at = block_at(lax.rem(me - s + devices, devices), chunk)
        long_out[at] = longs[s][0:chunk].astype(f32)
    y = (query_conv[...] * long_out[...]).astype(bf16)
    y_out[...] = y
    for s in range(parts):
        cot = cots[s][...]
        at = block_at(mine ^ s, width)
        full[:, at] = jnp.dot(y, cot, preferred_element_type=f32)
    keep[...] = full[block_at(core, half)]
    send[...] = full[block_at(1 - core, half)]


def core_sum_kernel(devices, keep, other, *rest):
    outs, (full,) = rest[:devices], rest[devices:]
    me = lax.axis_index("ctx")
    rows = keep.shape[0] // devices
    full[...] = keep[...] + other[...].astype(f32)
    for s in range(devices):
        at = block_at(lax.rem(me + s, devices), rows)
        outs[s][...] = full[at].astype(outs[s].dtype)


def block_sum_kernel(scale, *refs):
    total = refs[0][...]
    for ref in refs[1:-1]:
        total += ref[...].astype(f32)
    refs[-1][...] = (total * scale).astype(bf16)


def mixed_part_kernel(y, weights, kept, sent, full):
    mine = lax.axis_index("tp")
    rows, width = full.shape[0], y.shape[0]
    full[...] = lax.dot_general(
        y[...], weights[...], (((0,), (0,)), ((), ())), preferred_element_type=f32
    )
    for h in range(2):
        kept[h * rows : (h + 1) * rows] = full[:, block_at(mine ^ (2 * h), width)]
        sent[h * rows : (h + 1) * rows] = full[:, block_at(mine ^ (2 * h + 1), width)].astype(bf16)


def mixed_pair_kernel(kept, come, own, sent):
    rows = own.shape[0]
    own[...] = kept[0:rows] + come[0:rows].astype(f32)
    sent[...] = (kept[rows:] + come[rows:].astype(f32)).astype(bf16)


def mixed_sum_kernel(own, come, out):
    out[...] = (own[...] + come[...].astype(f32)).astype(bf16)


def ready_kernel(devices, taps, turned, previous, columns, seg, conv, source, *rest):
    pair_w, query_taps, query_w, flips, sum_w, early_w, place = rest
    me = lax.axis_index("ctx")
    stacked, chunk, span = conv.shape
    _, width, length = turned.shape
    groups = flips.shape[0]
    size = chunk // groups
    subs = span // SUB
    own = block_masks(seg[0:1], taps, place, me, length)
    shifts = local_shifts(turned, previous, taps, 0)
    position = lax.broadcasted_iota(jnp.int32, (width, length), 1)
    query_taps[0] = shifts[0]
    for s in range(1, taps):
        query_taps[s] = own[s] * shifts[s]
        query_w[s - 1] = jnp.broadcast_to(columns[:, s : s + 1] * own[s], (width, length))
    for i in range(stacked):
        other = local_conv(turned, previous, columns, own, stacked - i)
        j = (i + 1) * taps
        pair_w[i * taps] = columns[:, j : j + 1] * other
        for s in range(1, taps):
            weight = columns[:, j + s : j + s + 1] * own[s] * other
            pair_w[i * taps + s] = jnp.where(position >= s, weight, 0.0)
    masks = tap_masks(seg[0:1], taps)
    column = columns[block_at(me, chunk)]
    for i in range(stacked):
        x = source[i * chunk : (i + 1) * chunk].astype(f32)
        other = conv[1 - i]
        j = (i + 1) * taps
        sum_w[i * taps] = other * x
        for s in range(1, taps):
            masked = masks[s] * other
            sum_w[i * taps + s] = masked * pltpu.roll(x, s, 1)
            weight = column[:, j + s : j + s + 1] * masked
            for b in range(devices - 1):
                at = slice((b + 1) * length, (b + 1) * length + SUB)
                early_w[i * (taps - 1) + s - 1, :, b * SUB : (b + 1) * SUB] = weight[:, at]
    gated = (conv[0] * conv[1]).astype(bf16)
    corner = lax.broadcasted_iota(jnp.int32, (SUB, SUB), 0)
    corner += lax.broadcasted_iota(jnp.int32, (SUB, SUB), 1)
    flip = jnp.where(corner == SUB - 1, 1.0, 0.0).astype(bf16)
    for g in range(groups):
        rows = slice(g * size, (g + 1) * size)
        left = jnp.concatenate([gated[rows, j * SUB : (j + 1) * SUB] for j in range(subs)], axis=0)
        flips[g] = lax.dot_general(
            flip, left, (((1,), (1,)), ((), ())), preferred_element_type=f32
        ).astype(bf16)


def backward_kernel(
    devices, taps, toeplitz, columns, grad_y, long, query_taps, query_w, flips, sum_w, early_w, *rest
):
    glos, rest = rest[:devices], rest[devices:]
    outs, (query_out, grad_long_out, grads, small, marks) = rest[:devices], rest[devices:]
    me = lax.axis_index("ctx")
    _, chunk, span = sum_w.shape
    stacked = sum_w.shape[0] // taps
    length = span // devices
    groups = toeplitz.shape[0]
    size = chunk // groups
    width = grad_y.shape[0]
    reach = taps - 1

    grad = grad_y[...] * long[...]
    total = columns[:, 0:1] * grad
    lane = lax.broadcasted_iota(jnp.int32, (width, SUB), 1)
    position = lax.broadcasted_iota(jnp.int32, (width, length), 1)
    sums = jnp.zeros((width, SUB), f32)
    early = jnp.zeros((width, SUB), f32)
    for s in range(taps):
        tap = jnp.sum(grad * query_taps[s], axis=1, keepdims=True)
        sums += jnp.where(lane == groups + s, tap, 0.0)
        if s:
            back = pltpu.roll(query_w[s - 1] * grad, length - s, 1)
            total += jnp.where(position < length - s, back, 0.0)
            early += jnp.where(lane >= SUB - s, back[:, length - SUB :], 0.0)
    query_out[...] = total.T
    common = sums.T[0:16]
    early_query = early.T[SUB - 16 :]

    for s in range(devices):
        at = block_at(lax.rem(me - s + devices, devices), length)
        grad_long_out[:, at] = glos[s][chunk:]
    high = grad_long_out[...]
    gg_parts = []
    subs = span // SUB
    small[...] = jnp.zeros_like(small)
    for g in range(groups):
        own = slice(g * size, (g + 1) * size)
        stack = jnp.concatenate(
            [high[own, i * length : (i + 1) * length] for i in range(devices)], axis=0
        )
        totals = [None] * devices
        for lag in range(devices):
            part = lax.dot_general(
                stack[size * lag :],
                toeplitz[g, :, lag * length : (lag + 1) * length],
                (((1,), (1,)), ((), ())),
                preferred_element_type=f32,
            )
            for j in range(devices - lag):
                term = part[size * j : size * (j + 1)]
                totals[j] = term if totals[j] is None else totals[j] + term
        gg_parts.append(jnp.concatenate(totals, axis=1))
        right = jnp.concatenate([high[own, j * SUB : (j + 1) * SUB] for j in range(subs)], axis=0)
        turned = flips[g]
        lines = []
        for lag in range(subs):
            cross = jnp.dot(
                turned[:, : size * (subs - lag)], right[size * lag :], preferred_element_type=f32
            )
            wide = jnp.concatenate([cross, jnp.zeros((SUB, SUB), f32)], axis=1)
            wide = pltpu.roll(wide, 1, 1, stride=1, stride_axis=0)
            lines.append(jnp.sum(wide, axis=0, keepdims=True))
        per = length // SUB
        for lag in range(subs):
            line = lines[lag][:, SUB:]
            if lag + 1 < subs:
                line += lines[lag + 1][:, :SUB]
            b, within = divmod(lag, per)
            small[b, g : g + 1, within * SUB : (within + 1) * SUB] = line
    grad_gated = jnp.concatenate(gg_parts, axis=0)
    grads[...] = grad_gated.astype(bf16)
    lane = lax.broadcasted_iota(jnp.int32, (chunk, SUB), 1)
    sums = jnp.zeros((chunk, SUB), f32)
    for n in range(stacked * taps):
        tap = jnp.sum(grad_gated * sum_w[n], axis=1, keepdims=True)
        sums += jnp.where(lane == groups + taps + n, tap, 0.0)
    marks[...] = jnp.zeros_like(marks)
    marks[:, 0:chunk] = sums.T
    common += pltpu.roll(marks[0:16], me * chunk, 1)
    count = (stacked + 1) * taps
    start = 2 * groups + 2 * count
    high = common.astype(bf16).astype(f32)
    for b in range(devices):
        lines = small[b, 0:groups]
        top = lines.astype(bf16).astype(f32)
        small[b, 0:groups] = top
        small[b, groups : 2 * groups] = lines - top
        small[b, 2 * groups : 2 * groups + count] = high[groups : groups + count]
        small[b, 2 * groups + count : start] = (common - high)[groups : groups + count]
        small[b, start : start + reach] = early_query[16 - reach :]
        if b == devices - 1:
            continue
        first = grad_gated[:, (b + 1) * length : (b + 1) * length + SUB]
        for i in range(stacked):
            early = jnp.zeros((chunk, SUB), f32)
            for s in range(1, taps):
                weight = early_w[i * reach + s - 1, :, b * SUB : (b + 1) * SUB]
                back = pltpu.roll(weight * first, SUB - s, 1)
                early += jnp.where(lane >= SUB - s, back, 0.0)
            marks[:, 0:chunk] = early.T
            placed = pltpu.roll(marks[SUB - 16 :], me * chunk, 1)
            at = start + (i + 1) * reach
            small[b, at : at + reach] = placed[16 - reach :]
    for s in range(devices):
        to = lax.rem(me + s, devices)
        outs[s][0:chunk] = grads[:, block_at(to, length)]
        outs[s][chunk:] = small[to].astype(bf16)


def small_sum_kernel(devices, groups, stacked, taps, *refs):
    pays, (sums, later, tiles) = refs[:devices], refs[devices:]
    me = lax.axis_index("ctx")
    width = pays[0].shape[1]
    body = width // devices
    count = stacked * taps
    start = 2 * groups + 2 * count
    reach = taps - 1
    for s in range(devices):
        tiles[lax.rem(me - s + devices, devices)] = pays[s][body:].astype(f32)
    total = tiles[0]
    for c in range(1, devices):
        total += tiles[c]
    lines = [tiles[c, 0:groups] + tiles[c, groups : 2 * groups] for c in range(devices)]
    taps_sum = total[2 * groups : 2 * groups + count] + total[2 * groups + count : start]
    for n, value in enumerate((jnp.concatenate(lines, axis=0), taps_sum)):
        if value.shape[0] < 16:
            rest = jnp.zeros((16 - value.shape[0], width), f32)
            value = jnp.concatenate([value, rest], axis=0)
        for h, half in enumerate(split_bf16(value)):
            sums[:, (2 * h + n) * width : (2 * h + n + 1) * width] = half
    last = pays[devices - 1][body:].astype(f32)
    later[...] = jnp.zeros_like(later)
    later[0, 16 - reach : 16] = last[start : start + reach]
    for i in range(1, stacked):
        later[i, 16 - reach : 16] = total[start + i * reach : start + (i + 1) * reach]


def grad_out_kernel(devices, taps, query_part, pair_w, later, *refs):
    pays, (out, gated) = refs[:devices], refs[devices:]
    me = lax.axis_index("ctx")
    stacked, rows, width = out.shape
    chunk = width // devices
    for s in range(devices):
        at = block_at(lax.rem(me - s + devices, devices), chunk)
        gated[at] = pays[s][0:chunk].astype(f32)
    for i in range(stacked):
        if i == 0:
            turned = query_part[...]
        else:
            j = (i - 1) * taps
            total = pair_w[j] * gated[...]
            for s in range(1, taps):
                total += pltpu.roll(pair_w[j + s] * gated[...], rows - s, 1)
            turned = total.T
        out[i, 0 : rows - 16] = turned[0 : rows - 16].astype(bf16)
        out[i, rows - 16 :] = (turned[rows - 16 :] + later[i]).astype(bf16)


def final_kernel(devices, scale, *refs):
    near, far, refs = refs[:devices], refs[devices : 2 * devices], refs[2 * devices :]
    mine, other, weight_out, short_out, long_out = refs
    me, core = lax.axis_index("ctx"), lax.axis_index("dp")
    rows = near[0].shape[0]
    for side, blocks in ((core, near), (1 - core, far)):
        for s in range(devices):
            at = side * devices + lax.rem(me - s + devices, devices)
            weight_out[block_at(at, rows)] = blocks[s][...].astype(f32)
    width = long_out.shape[1]
    stacked, taps, _ = short_out.shape

    def sums(n):
        pieces = []
        for ref in (mine, other):
            high = ref[:, n * width : (n + 1) * width].astype(f32)
            low = ref[:, (n + 2) * width : (n + 3) * width].astype(f32)
            pieces.append(high + low)
        return (pieces[0] + pieces[1]) * scale

    long_out[...] = sums(0)
    total = sums(1)
    for i in range(stacked):
        short_out[i] = total[i * taps : (i + 1) * taps]


def direct_device(projected, segment_ids, short_filter, long_filter, out_proj, mixed_cotangent):
    devices, parts = lax.axis_size("ctx"), lax.axis_size("tp")
    stacked, _, length, width = projected.shape
    taps = short_filter.shape[1]
    count = long_filter.shape[0]
    groups = count // devices
    chunk = width // devices
    span = length * devices
    total_cols = out_proj.shape[1]
    grad_scale = 1.0 / math.sqrt(projected.shape[1] * lax.axis_size("dp") * span)
    cotangent = mixed_cotangent[0]
    room = 16
    inputs = (projected[:, 0], long_filter, segment_ids)

    outs = on_core(
        functools.partial(pack_kernel, devices, taps - 1),
        [
            (((stacked - 1) * chunk + (2 * room if s == 1 else room), length), bf16)
            for s in range(devices)
        ],
        inputs,
        "pack",
        [
            pltpu.VMEM((stacked - 1, length, width), bf16),
            pltpu.VMEM((16, width), bf16),
            pltpu.VMEM(long_filter.shape, f32),
            pltpu.VMEM(segment_ids.shape, jnp.int32),
            pltpu.VMEM((stacked - 1, width, length), bf16),
            pltpu.VMEM((room, length), f32),
            pltpu.VMEM((room, width), f32),
            pltpu.SemaphoreType.DMA((5,)),
        ],
        whole=True,
    )
    own, *signal = scatter_chunks(outs, "ctx")
    beside = swap(cotangent, "tp", 1)
    columns, own, turned = on_core(
        prepare_kernel,
        [((width, 16), f32), (own.shape, bf16), ((stacked, width, length), bf16)],
        (after(short_filter, beside), own, inputs[0]),
        "prepare",
        [pltpu.VMEM((16, width), f32)],
    )
    signal = [own, *signal]

    conv_flops = 2 * groups * span * span * 64
    outs = on_core(
        functools.partial(conv_kernel, devices, taps),
        [((chunk, length), bf16)] * devices
        + [
            ((stacked - 1, chunk, span), f32),
            (((stacked - 1) * chunk, span), bf16),
            ((8, span), f32),
            ((groups, length, span), bf16),
        ],
        (columns, *signal),
        "conv",
        [
            pltpu.VMEM((room, span), f32),
            pltpu.VMEM((chunk, span), bf16),
            pltpu.VMEM((groups, length, span), bf16),
        ],
        flops=900_000_000,
    )
    longs, kept = outs[:devices], outs[devices:]
    seg = kept[2]
    cots = [cotangent, beside, swap(cotangent, "tp", 2), swap(beside, "tp", 2)]
    outs = on_core(
        functools.partial(grad_y_kernel, devices, parts, taps),
        [((2 * chunk, length), bf16)] * devices + [((width, length), f32)] * 2,
        (out_proj, turned, signal[1], columns, seg, *cots, *longs),
        "grad_y",
        [pltpu.VMEM((8 * taps, span), f32), pltpu.VMEM((width, length), bf16)],
        flops=2 * width * length * total_cols,
    )
    pairs, (grad_y, query_conv) = outs[:devices], outs[devices:]
    pairs = scatter_chunks(pairs, "ctx")

    pair_w, *factors = on_core(
        functools.partial(ready_kernel, devices, taps),
        [
            (((stacked - 1) * taps, width, length), f32),
            ((taps, width, length), f32),
            ((taps - 1, width, length), f32),
            ((groups, SUB, SUB), bf16),
            (((stacked - 1) * taps, chunk, span), f32),
            (((stacked - 1) * (taps - 1), chunk, (devices - 1) * SUB), f32),
        ],
        (turned, signal[1], columns, seg, *kept[:2]),
        "ready",
        [pltpu.VMEM((8 * taps, span), f32)],
    )
    query_conv = after(query_conv, factors[0])

    half = width // 2
    y, long, keep, send = on_core(
        functools.partial(weight_grad_kernel, devices, parts),
        [
            ((width, length), bf16),
            ((width, length), f32),
            ((half, total_cols), f32),
            ((half, total_cols), f32),
        ],
        (query_conv, *cots, *pairs),
        "weight_grad",
        [pltpu.VMEM((width, total_cols), f32)],
        flops=2 * width * length * total_cols,
    )
    other = rotate(send, "dp", 1)
    kept_part, sent_part = on_core(
        mixed_part_kernel,
        [((2 * length, width), f32), ((2 * length, width), bf16)],
        (y, out_proj),
        "mixed_part",
        [pltpu.VMEM((length, total_cols), f32)],
        flops=2 * width * length * total_cols,
    )
    keep = after(keep, kept_part)
    rows = half // devices
    sums = on_core(
        functools.partial(core_sum_kernel, devices),
        [((rows, total_cols), f32)] + [((rows, total_cols), bf16)] * (devices - 1),
        (keep, other),
        "core_sum",
        [pltpu.VMEM((half, total_cols), f32)],
    )
    parts_out = scatter_chunks(sums, "ctx")

    outs = on_core(
        functools.partial(backward_kernel, devices, taps),
        [((chunk + 2 * room, length), bf16)] * devices + [((length, width), f32)],
        (kept[3], columns, grad_y, after(long, sums[1]), *factors, *pairs),
        "backward",
        [
            pltpu.VMEM((chunk, span), bf16),
            pltpu.VMEM((chunk, span), bf16),
            pltpu.VMEM((devices, 2 * room, length), f32),
            pltpu.VMEM((SUB, width), f32),
        ],
        flops=2 * conv_flops,
    )
    back, query_part = outs[:devices], outs[devices]
    back = scatter_chunks(back, "ctx")
    sums, later = on_core(
        functools.partial(small_sum_kernel, devices, groups, stacked, taps),
        [((16, total_cols), bf16), ((stacked, 16, width), f32)],
        back,
        "small_sum",
        [pltpu.VMEM((devices, 2 * room, width), f32)],
        flops=2_000_000_000,
    )
    (grad_projected,) = on_core(
        functools.partial(grad_out_kernel, devices, taps),
        [((stacked, length, width), bf16)],
        (query_part, pair_w, later, *back),
        "grad_out",
        [pltpu.VMEM((width, length), f32)],
    )
    (block,) = on_core(
        functools.partial(block_sum_kernel, grad_scale),
        [((rows, total_cols), bf16)],
        parts_out,
        "block_sum",
    )
    own_part, sent_part = on_core(
        mixed_pair_kernel,
        [((length, width), f32), ((length, width), bf16)],
        (after(kept_part, query_part), swap(sent_part, "tp", 1)),
        "mixed_pair",
    )
    come_part = swap(sent_part, "tp", 2)
    (mixed,) = on_core(
        mixed_sum_kernel, [((length, width), bf16)], (own_part, come_part), "mixed_sum"
    )

    near = spread(block, "ctx")
    other_sums = rotate(sums, "dp", 1)
    near[1] = after(near[1], (grad_projected, come_part, other_sums))
    far = [rotate(piece, "dp", 1) for piece in near]
    grad_out_proj, grad_short, grad_long = on_core(
        functools.partial(final_kernel, devices, grad_scale),
        [((width, total_cols), f32), (short_filter.shape, f32), ((count, length), f32)],
        (*near, *far, sums, other_sums),
        "final",
    )
    return (mixed[None], grad_projected[:, None], grad_short, grad_long, grad_out_proj)


def direct_fits(mesh, projected, short_filter, long_filter, out_proj):
    devices = mesh.shape["ctx"]
    length = projected.shape[2] // devices
    width = projected.shape[3] // mesh.shape["tp"]
    groups = long_filter.shape[0] // mesh.shape["tp"]
    stacked, taps = short_filter.shape[:2]
    return (
        mesh.shape["dp"] == 2
        and mesh.shape["tp"] == 4
        and projected.shape[1] == 2
        and stacked == 3
        and length == width
        and length % SUB == 0
        and groups % devices == 0
        and groups == 16
        and (width // devices) % 16 == 0
        and width // devices <= SUB
        and (width // groups) == 16
        and 2 * groups // devices + 2 <= 16
        and out_proj.shape[1] == 4 * width
        and stacked * (taps - 1) <= 16
        and groups // devices + stacked * taps <= 16
        and 2 * (groups // devices) + 2 * stacked * taps + stacked * (taps - 1) <= 32
    )


def solution(mesh):
    in_specs = (
        P(None, "dp", "ctx", "tp"),
        P("dp", "ctx"),
        P(None, None, "tp"),
        P("tp", "ctx"),
        P("tp", None),
        P("dp", "ctx", "tp"),
    )
    out_specs = (
        P("dp", "ctx", "tp"),
        P(None, "dp", "ctx", "tp"),
        P(None, None, "tp"),
        P("tp", "ctx"),
        P("tp", None),
    )

    def layer(projected, segment_ids, short_filter, long_filter, out_proj, mixed_cotangent):
        fits = direct_fits(mesh, projected, short_filter, long_filter, out_proj)
        return jax.shard_map(
            direct_device if fits else spectral_device,
            mesh=mesh,
            in_specs=in_specs,
            out_specs=out_specs,
            check_vma=False,
        )(projected, segment_ids, short_filter, long_filter, out_proj, mixed_cotangent)

    return layer
```

```python
import functools
import math

import jax
import jax.numpy as jnp
from jax import lax
from jax.experimental import pallas as pl
from jax.experimental.pallas import tpu as pltpu
from jax.sharding import PartitionSpec as P

highest_precision = lax.Precision.HIGHEST


def shifted(value, axis, steps):
    count = lax.axis_size(axis)
    first, last = (max(0, -steps), min(count, count - steps))
    return lax.ppermute(value, axis, [(source, source + steps) for source in range(first, last)])


def angle_table(height, breadth, period, direction):
    product = (
        jnp.arange(height, dtype=jnp.int32)[:, None]
        * jnp.arange(breadth, dtype=jnp.int32)[None, :]
        % period
    )
    angles = direction * 2.0 * math.pi / period * product.astype(jnp.float32)
    return (jnp.cos(angles), jnp.sin(angles))


def row_twiddle(spec_re, spec_im, direction):
    my_index = lax.axis_index("ctx")
    devices = lax.axis_size("ctx")
    row_count = spec_re.shape[1]
    period = 2 * devices * row_count
    freq_pair = 2 * my_index + jnp.arange(2, dtype=jnp.int32)
    product = freq_pair[:, None] * jnp.arange(row_count, dtype=jnp.int32)[None, :] % period
    angles = direction * 2.0 * math.pi / period * product.astype(jnp.float32)
    cosine = jnp.cos(angles)[:, :, None]
    sine_part = jnp.sin(angles)[:, :, None]
    return (spec_re * cosine - spec_im * sine_part, spec_re * sine_part + spec_im * cosine)


def row_transform(spec_re, spec_im, direction):
    row_count = spec_re.shape[1]
    cosine, sine_part = angle_table(row_count, row_count, row_count, direction)

    def along_rows(blocks, matrix):
        return jnp.einsum("kmc,mq->kqc", blocks, matrix, precision=highest_precision)

    return (
        along_rows(spec_re, cosine) - along_rows(spec_im, sine_part),
        along_rows(spec_re, sine_part) + along_rows(spec_im, cosine),
    )


def mixing(matrix, blocks):
    return jnp.einsum("kj,jmc->kmc", matrix, blocks, precision=highest_precision)


def forward_spectrum(real_part):
    devices = lax.axis_size("ctx")
    cosine, sine_part = angle_table(2 * devices, devices, 2 * devices, -1.0)
    spread_re = lax.all_to_all(real_part[None], "ctx", split_axis=1, concat_axis=0, tiled=True)
    column_re = mixing(cosine, spread_re)
    column_im = mixing(sine_part, spread_re)
    near_re, near_im = (
        lax.all_to_all(column_re, "ctx", split_axis=0, concat_axis=1, tiled=True),
        lax.all_to_all(column_im, "ctx", split_axis=0, concat_axis=1, tiled=True),
    )
    twist_re, twist_im = row_twiddle(near_re, near_im, -1.0)
    return row_transform(twist_re, twist_im, -1.0)


def inverse_spectrum(spec_re, spec_im):
    devices = lax.axis_size("ctx")
    row_count = spec_re.shape[1]
    back_re, back_im = row_transform(spec_re, spec_im, 1.0)
    twist_re, twist_im = row_twiddle(back_re / row_count, back_im / row_count, 1.0)
    far_re, far_im = (
        lax.all_to_all(twist_re, "ctx", split_axis=1, concat_axis=0, tiled=True),
        lax.all_to_all(twist_im, "ctx", split_axis=1, concat_axis=0, tiled=True),
    )
    cosine, sine_part = angle_table(devices, 2 * devices, 2 * devices, 1.0)
    out_re = (mixing(cosine, far_re) - mixing(sine_part, far_im)) / (2 * devices)
    rows_re = lax.all_to_all(out_re, "ctx", split_axis=0, concat_axis=1, tiled=True)
    return (rows_re[0], rows_re[0])


def pack_columns(values):
    return (values, values)


def by_filter(val_re, val_im, fil_re, fil_im, conjugate):
    val_shape = val_re.shape
    group_count = fil_re.shape[2]
    v_re = val_re.reshape(val_shape[0], val_shape[1], group_count, -1)
    v_im = val_im.reshape(val_shape[0], val_shape[1], group_count, -1)
    f_re = fil_re[:, :, :, None]
    f_im = fil_im[:, :, :, None]
    if conjugate:
        f_im = -f_im
    out_re = v_re * f_re - v_im * f_im
    out_im = v_re * f_im + v_im * f_re
    return (out_re.reshape(val_shape), out_im.reshape(val_shape))


def short_local(extended, filters, seg_ext):
    reach_taps = filters.shape[1]
    out_rows = extended.shape[1] - reach_taps + 1
    own_seg = seg_ext[reach_taps - 1 :]
    running = jnp.zeros((extended.shape[0], out_rows, extended.shape[2]), jnp.float32)
    for shift_by in range(reach_taps):
        start_row = reach_taps - 1 - shift_by
        same_doc = jnp.where(seg_ext[start_row : start_row + out_rows] == own_seg, 1.0, 0.0)
        running = (
            running
            + filters[:, shift_by][:, None, :]
            * same_doc[None, :, None]
            * extended[:, start_row : start_row + out_rows]
        )
    return running


def spectral_device(projected, segment_ids, short_filter, long_filter, out_proj, mixed_cotangent):
    row_count = projected.shape[2]
    stacked = projected.shape[0]
    width_dev = projected.shape[3]
    short_reach = short_filter.shape[1]
    group_count = long_filter.shape[0]
    grad_scale = 1.0 / math.sqrt(
        projected.shape[1] * lax.axis_size("dp") * row_count * lax.axis_size("ctx")
    )
    segments = segment_ids[0]
    source = projected[:, 0]
    short_rows = short_reach - 1
    cot_full = lax.all_gather(mixed_cotangent[0], "tp", axis=1, tiled=True)
    prev_tail, prev_seg = shifted(
        (source[:, row_count - short_rows :], segments[row_count - short_rows :]), "ctx", 1
    )
    short_seg = jnp.concatenate([prev_seg, segments])
    short_ext = jnp.concatenate([prev_tail, source], axis=1).astype(jnp.float32)

    def short_piece(extended, filters):
        return short_local(extended, filters, short_seg)

    short_out, short_pull = jax.vjp(short_piece, short_ext, short_filter)
    query_conv = short_out[0]
    gated_rows = short_out[1] * short_out[2]
    filter_cols = long_filter.T
    mid_re, mid_im = pack_columns(gated_rows)
    spec_re, spec_im = forward_spectrum(jnp.concatenate([mid_re, filter_cols], axis=1))
    data_cols = spec_re.shape[2] - group_count
    signal_re = spec_re[:, :, :data_cols]
    signal_im = spec_im[:, :, :data_cols]
    filt_re = spec_re[:, :, data_cols:]
    filt_im = spec_im[:, :, data_cols:]
    long_re, long_im = by_filter(signal_re, signal_im, filt_re, filt_im, False)
    out_re, out_im = inverse_spectrum(long_re, long_im)
    y_out = (query_conv * out_re).astype(jnp.bfloat16)
    partial_out = jnp.dot(y_out, out_proj, preferred_element_type=jnp.float32)
    mixed = lax.psum_scatter(partial_out, "tp", scatter_dimension=1, tiled=True).astype(
        jnp.bfloat16
    )
    grad_y = jnp.dot(cot_full, out_proj.T, preferred_element_type=jnp.float32)
    grad_proj_local = jnp.dot(y_out.T, cot_full, preferred_element_type=jnp.float32)
    grad_long_out = grad_y * query_conv
    grad_query = grad_y * out_re
    grad_in_re, grad_in_im = pack_columns(grad_long_out)
    cot_re, cot_im = forward_spectrum(grad_in_re)
    back_re, back_im = by_filter(cot_re, cot_im, filt_re, filt_im, True)
    cross_re = (
        (signal_re * cot_re + signal_im * cot_im).reshape(2, row_count, group_count, -1).sum(axis=3)
    )
    cross_im = (
        (signal_re * cot_im - signal_im * cot_re).reshape(2, row_count, group_count, -1).sum(axis=3)
    )
    inv_re, inv_im = inverse_spectrum(
        jnp.concatenate([back_re, cross_re], axis=2), jnp.concatenate([back_im, cross_im], axis=2)
    )
    grad_gated = inv_re[:, :data_cols]
    grad_long_local = inv_re[:, data_cols:].T
    grad_short_out = jnp.stack([grad_query, grad_gated * short_out[2], grad_gated * short_out[1]])
    grad_short_ext, grad_short_local = short_pull(grad_short_out)
    returned_short = shifted(grad_short_ext[:, :short_rows], "ctx", -1)
    grad_source = grad_short_ext[:, short_rows:] + jnp.concatenate(
        [jnp.zeros((stacked, row_count - short_rows, width_dev), jnp.float32), returned_short],
        axis=1,
    )
    total_proj, total_short = lax.psum((grad_proj_local, grad_short_local), ("ctx", "dp"))
    total_long = lax.psum(grad_long_local, "dp")
    return (
        mixed[None],
        grad_source[:, None].astype(jnp.bfloat16),
        total_short * grad_scale,
        total_long * grad_scale,
        total_proj * grad_scale,
    )


bf16 = jnp.bfloat16
f32 = jnp.float32
SUB = 128


def split_bf16(value):
    high = value.astype(bf16)
    return high, (value - high.astype(f32)).astype(bf16)


def rotate(value, axis, steps):
    count = lax.axis_size(axis)
    return lax.ppermute(value, axis, [(i, (i + steps) % count) for i in range(count)])


def swap(value, axis, bits):
    return lax.ppermute(value, axis, [(i, i ^ bits) for i in range(lax.axis_size(axis))])


def scatter_chunks(chunks, axis):
    return [chunks[0]] + [rotate(chunks[s], axis, s) for s in range(1, len(chunks))]


def after(value, other):
    return lax.optimization_barrier((value, other))[0]


def spread(value, axis):
    return [value] + [rotate(value, axis, s) for s in range(1, lax.axis_size(axis))]


def on_core(kernel, outs, args, name, scratch=(), flops=0, whole=False):
    moved = sum(a.size * a.dtype.itemsize for a in args)
    moved += sum(math.prod(shape) * jnp.dtype(kind).itemsize for shape, kind in outs)
    return pl.pallas_call(
        kernel,
        out_shape=[jax.ShapeDtypeStruct(shape, kind) for shape, kind in outs],
        in_specs=[pl.BlockSpec(memory_space=pltpu.HBM) if whole else pl.BlockSpec()] * len(args),
        scratch_shapes=list(scratch),
        compiler_params=pltpu.CompilerParams(vmem_limit_bytes=(63 if whole else 40) * 1024 * 1024),
        cost_estimate=pl.CostEstimate(flops=flops, bytes_accessed=moved, transcendentals=0),
        name=name,
    )(*args)


def block_at(index, size):
    return pl.ds(pl.multiple_of(index * size, size), size)


def pack_kernel(devices, reach, projected, filter_source, segment_source, *refs):
    outs, refs = refs[:devices], refs[devices:]
    pair, query, filters, segments, turned, small, tail, sems = refs
    _, rows, _ = projected.shape
    sources = (
        (projected.at[1], pair.at[0]),
        (projected.at[2], pair.at[1]),
        (projected.at[0, pl.ds(rows - 16, 16)], query),
        (filter_source, filters),
        (segment_source, segments),
    )
    copies = [
        pltpu.make_async_copy(source, held, sems.at[n])
        for n, (source, held) in enumerate(sources)
    ]
    for copy in copies:
        copy.start()
    me = lax.axis_index("ctx")
    width = pair.shape[2]
    chunk = width // devices
    count = filters.shape[0]
    groups = count // devices
    body = pair.shape[0] * chunk
    small[...] = jnp.zeros_like(small)
    tail[...] = jnp.zeros_like(tail)
    for i in range(pair.shape[0]):
        copies[i].wait()
        turned[i] = pair[i].T
    for copy in copies[2:]:
        copy.wait()
    for i, last in enumerate((query[...], pair[0, rows - 16 :], pair[1, rows - 16 :])):
        tail[i * reach : (i + 1) * reach] = last.astype(f32)[16 - reach :]
    seg = segments[...]
    small[2 * groups : 2 * groups + 1] = (seg >> 8).astype(f32)
    small[2 * groups + 1 : 2 * groups + 2] = (seg & 255).astype(f32)
    for s in range(devices):
        to = lax.rem(me + s, devices)
        for i in range(pair.shape[0]):
            outs[s][i * chunk : (i + 1) * chunk] = turned[i, block_at(to, chunk)]
        lines = pltpu.roll(filters[...], lax.rem(count - to * groups, count), 0)[0:groups]
        high = lines.astype(bf16).astype(f32)
        small[0:groups] = high
        small[groups : 2 * groups] = lines - high
        outs[s][body : body + 16] = small[...].astype(bf16)
    outs[1][body + 16 :] = tail[...].astype(bf16)


def prepare_kernel(short_filter, chunk, projected, columns, chunk_out, turned, flat):
    stacked, taps, _ = short_filter.shape
    flat[...] = jnp.zeros_like(flat)
    for i in range(stacked):
        flat[i * taps : (i + 1) * taps] = short_filter[i]
        turned[i] = projected[i].T
    columns[...] = flat[...].T
    chunk_out[...] = chunk[...]


def tap_masks(seg, taps):
    wide = jnp.broadcast_to(seg, (8, seg.shape[1]))
    place = lax.broadcasted_iota(jnp.int32, wide.shape, 1)
    masks = [None]
    for s in range(1, taps):
        same = (wide == pltpu.roll(wide, s, 1)) & (place >= s)
        masks.append(jnp.where(same, 1.0, 0.0)[0:1])
    return masks


def block_masks(seg, taps, place, me, length):
    masks = tap_masks(seg, taps)
    for s in range(1, taps):
        place[8 * s : 8 * (s + 1)] = jnp.broadcast_to(masks[s], (8, seg.shape[1]))
    return [None] + [place[8 * s : 8 * s + 8, block_at(me, length)][0:1] for s in range(1, taps)]


def local_shifts(turned, previous, taps, i):
    tail = previous[previous.shape[0] - 16 :].astype(f32)
    before = jnp.concatenate([tail, jnp.zeros((SUB - 16, tail.shape[1]), f32)], axis=0)
    before = pltpu.roll(before, SUB - (taps - 1) * (i + 1), 0)
    wide = jnp.concatenate([before.T, turned[i].astype(f32)], axis=1)
    return [wide[:, SUB:]] + [pltpu.roll(wide, s, 1)[:, SUB:] for s in range(1, taps)]


def local_conv(turned, previous, columns, masks, i):
    taps = len(masks)
    shifts = local_shifts(turned, previous, taps, i)
    j = i * taps
    total = columns[:, j : j + 1] * shifts[0]
    for s in range(1, taps):
        total += columns[:, j + s : j + s + 1] * (masks[s] * shifts[s])
    return total


def conv_kernel(devices, taps, columns, *rest):
    pays, rest = rest[:devices], rest[devices:]
    outs, rest = rest[:devices], rest[devices:]
    conv, source, seg_out, toeplitz, small, long, rests = rest
    me = lax.axis_index("ctx")
    stacked, chunk, span = conv.shape
    length = span // devices
    groups = toeplitz.shape[0]
    size = chunk // groups
    body = stacked * chunk
    for s in range(devices):
        at = block_at(lax.rem(me - s + devices, devices), length)
        source[:, at] = pays[s][0:body]
        small[:, at] = pays[s][body : body + 16].astype(f32)
    seg = small[2 * groups : 2 * groups + 1] * 256.0 + small[2 * groups + 1 : 2 * groups + 2]
    seg_out[...] = jnp.broadcast_to(seg, seg_out.shape)
    masks = tap_masks(seg, taps)
    column = columns[block_at(me, chunk)]
    for i in range(stacked):
        x = source[i * chunk : (i + 1) * chunk].astype(f32)
        j = (i + 1) * taps
        total = column[:, j : j + 1] * x
        for s in range(1, taps):
            total += column[:, j + s : j + s + 1] * (masks[s] * pltpu.roll(x, s, 1))
        conv[i] = total
    high, low = split_bf16(conv[0] * conv[1])
    for g in range(groups):
        line = small[g : g + 1] + small[groups + g : groups + g + 1]
        padded = jnp.concatenate([line, jnp.zeros((1, SUB), f32)], axis=1)
        turned = pltpu.roll(
            jnp.broadcast_to(padded, (SUB, span + SUB)), 0, 1, stride=1, stride_axis=0
        )[:, :span]
        for half, into in zip(split_bf16(turned), (toeplitz, rests)):
            for r in range(length // SUB):
                rows = slice(r * SUB, (r + 1) * SUB)
                if r:
                    into[g, rows, : r * SUB] = jnp.zeros((SUB, r * SUB), bf16)
                into[g, rows, r * SUB :] = half[:, : span - r * SUB]
        own = slice(g * size, (g + 1) * size)
        pieces = []
        for j in range(devices):
            at = slice(j * length, (j + 1) * length)
            pieces += [high[own, at], low[own, at]]
        stack = jnp.concatenate(pieces, axis=0)
        totals = [None] * devices
        for lag in range(devices):
            lhs = stack[: 2 * size * (devices - lag)]
            at = slice(lag * length, (lag + 1) * length)
            part = jnp.dot(lhs, toeplitz[g, :, at], preferred_element_type=f32)
            part += jnp.dot(lhs, rests[g, :, at], preferred_element_type=f32)
            for j in range(devices - lag):
                term = part[2 * size * j : 2 * size * j + size]
                term += part[2 * size * j + size : 2 * size * (j + 1)]
                i = j + lag
                totals[i] = term if totals[i] is None else totals[i] + term
        for i in range(devices):
            long[own, i * length : (i + 1) * length] = totals[i].astype(bf16)
    for s in range(devices):
        outs[s][...] = long[:, block_at(lax.rem(me + s, devices), length)]


def grad_y_kernel(devices, parts, taps, weights, turned, previous, columns, seg, *rest):
    cots, rest = rest[:parts], rest[parts:]
    longs, rest = rest[:devices], rest[devices:]
    outs, (grad_y, query_conv, place, full) = rest[:devices], rest[devices:]
    me, mine = lax.axis_index("ctx"), lax.axis_index("tp")
    rows, width = cots[0].shape
    chunk = width // devices
    masks = block_masks(seg[0:1], taps, place, me, rows)
    conv = local_conv(turned, previous, columns, masks, 0)
    query_conv[...] = conv
    total = None
    for s in range(parts):
        cot = cots[s][...]
        lhs = weights[:, block_at(mine ^ s, width)]
        term = lax.dot_general(lhs, cot, (((1,), (1,)), ((), ())), preferred_element_type=f32)
        total = term if total is None else total + term
    grad_y[...] = total
    full[...] = (total * conv).astype(bf16)
    for s in range(devices):
        outs[s][0:chunk] = longs[s][...]
        outs[s][chunk:] = full[block_at(lax.rem(me + s, devices), chunk)]


def weight_grad_kernel(devices, parts, query_conv, *rest):
    cots, rest = rest[:parts], rest[parts:]
    longs, rest = rest[:devices], rest[devices:]
    y_out, long_out, keep, send, full = rest
    me, mine, core = lax.axis_index("ctx"), lax.axis_index("tp"), lax.axis_index("dp")
    rows, width = cots[0].shape
    chunk = width // devices
    half = width // 2
    for s in range(devices):
        at = block_at(lax.rem(me - s + devices, devices), chunk)
        long_out[at] = longs[s][0:chunk].astype(f32)
    y = (query_conv[...] * long_out[...]).astype(bf16)
    y_out[...] = y
    for s in range(parts):
        cot = cots[s][...]
        at = block_at(mine ^ s, width)
        full[:, at] = jnp.dot(y, cot, preferred_element_type=f32)
    keep[...] = full[block_at(core, half)]
    send[...] = full[block_at(1 - core, half)].astype(send.dtype)


def core_sum_kernel(devices, keep, other, *rest):
    outs, (full,) = rest[:devices], rest[devices:]
    me = lax.axis_index("ctx")
    rows = keep.shape[0] // devices
    full[...] = keep[...] + other[...].astype(f32)
    for s in range(devices):
        at = block_at(lax.rem(me + s, devices), rows)
        outs[s][...] = full[at].astype(outs[s].dtype)


def block_sum_kernel(scale, *refs):
    total = refs[0][...]
    for ref in refs[1:-1]:
        total += ref[...].astype(f32)
    refs[-1][...] = (total * scale).astype(bf16)


def mixed_part_kernel(y, weights, kept, sent, full):
    mine = lax.axis_index("tp")
    rows, width = full.shape[0], y.shape[0]
    full[...] = lax.dot_general(
        y[...], weights[...], (((0,), (0,)), ((), ())), preferred_element_type=f32
    )
    for h in range(2):
        kept[h * rows : (h + 1) * rows] = full[:, block_at(mine ^ (2 * h), width)]
        sent[h * rows : (h + 1) * rows] = full[:, block_at(mine ^ (2 * h + 1), width)].astype(bf16)


def mixed_pair_kernel(kept, come, own, sent):
    rows = own.shape[0]
    own[...] = kept[0:rows] + come[0:rows].astype(f32)
    sent[...] = (kept[rows:] + come[rows:].astype(f32)).astype(bf16)


def mixed_sum_kernel(own, come, out):
    out[...] = (own[...] + come[...].astype(f32)).astype(bf16)


def ready_kernel(devices, taps, turned, previous, columns, seg, conv, source, *rest):
    pair_w, query_taps, query_w, flips, sum_w, early_w, place = rest
    me = lax.axis_index("ctx")
    stacked, chunk, span = conv.shape
    _, width, length = turned.shape
    groups = flips.shape[0]
    size = chunk // groups
    subs = span // SUB
    own = block_masks(seg[0:1], taps, place, me, length)
    shifts = local_shifts(turned, previous, taps, 0)
    position = lax.broadcasted_iota(jnp.int32, (width, length), 1)
    query_taps[0] = shifts[0]
    for s in range(1, taps):
        query_taps[s] = own[s] * shifts[s]
        query_w[s - 1] = jnp.broadcast_to(columns[:, s : s + 1] * own[s], (width, length))
    for i in range(stacked):
        other = local_conv(turned, previous, columns, own, stacked - i)
        j = (i + 1) * taps
        pair_w[i * taps] = columns[:, j : j + 1] * other
        for s in range(1, taps):
            weight = columns[:, j + s : j + s + 1] * own[s] * other
            pair_w[i * taps + s] = jnp.where(position >= s, weight, 0.0)
    masks = tap_masks(seg[0:1], taps)
    column = columns[block_at(me, chunk)]
    for i in range(stacked):
        x = source[i * chunk : (i + 1) * chunk].astype(f32)
        other = conv[1 - i]
        j = (i + 1) * taps
        sum_w[i * taps] = other * x
        for s in range(1, taps):
            masked = masks[s] * other
            sum_w[i * taps + s] = masked * pltpu.roll(x, s, 1)
            weight = column[:, j + s : j + s + 1] * masked
            for b in range(devices - 1):
                at = slice((b + 1) * length, (b + 1) * length + SUB)
                early_w[i * (taps - 1) + s - 1, :, b * SUB : (b + 1) * SUB] = weight[:, at]
    gated = (conv[0] * conv[1]).astype(bf16)
    corner = lax.broadcasted_iota(jnp.int32, (SUB, SUB), 0)
    corner += lax.broadcasted_iota(jnp.int32, (SUB, SUB), 1)
    flip = jnp.where(corner == SUB - 1, 1.0, 0.0).astype(bf16)
    for g in range(groups):
        rows = slice(g * size, (g + 1) * size)
        left = jnp.concatenate([gated[rows, j * SUB : (j + 1) * SUB] for j in range(subs)], axis=0)
        flips[g] = lax.dot_general(
            flip, left, (((1,), (1,)), ((), ())), preferred_element_type=f32
        ).astype(bf16)


def backward_kernel(
    devices, taps, toeplitz, columns, grad_y, long, query_taps, query_w, flips, sum_w, early_w, *rest
):
    glos, rest = rest[:devices], rest[devices:]
    outs, (query_out, grad_long_out, grads, small, marks) = rest[:devices], rest[devices:]
    me = lax.axis_index("ctx")
    _, chunk, span = sum_w.shape
    stacked = sum_w.shape[0] // taps
    length = span // devices
    groups = toeplitz.shape[0]
    size = chunk // groups
    width = grad_y.shape[0]
    reach = taps - 1

    grad = grad_y[...] * long[...]
    total = columns[:, 0:1] * grad
    lane = lax.broadcasted_iota(jnp.int32, (width, SUB), 1)
    position = lax.broadcasted_iota(jnp.int32, (width, length), 1)
    sums = jnp.zeros((width, SUB), f32)
    early = jnp.zeros((width, SUB), f32)
    for s in range(taps):
        tap = jnp.sum(grad * query_taps[s], axis=1, keepdims=True)
        sums += jnp.where(lane == groups + s, tap, 0.0)
        if s:
            back = pltpu.roll(query_w[s - 1] * grad, length - s, 1)
            total += jnp.where(position < length - s, back, 0.0)
            early += jnp.where(lane >= SUB - s, back[:, length - SUB :], 0.0)
    query_out[...] = total.T
    common = sums.T[0:16]
    early_query = early.T[SUB - 16 :]

    for s in range(devices):
        at = block_at(lax.rem(me - s + devices, devices), length)
        grad_long_out[:, at] = glos[s][chunk:]
    high = grad_long_out[...]
    gg_parts = []
    subs = span // SUB
    small[...] = jnp.zeros_like(small)
    for g in range(groups):
        own = slice(g * size, (g + 1) * size)
        stack = jnp.concatenate(
            [high[own, i * length : (i + 1) * length] for i in range(devices)], axis=0
        )
        totals = [None] * devices
        for lag in range(devices):
            part = lax.dot_general(
                stack[size * lag :],
                toeplitz[g, :, lag * length : (lag + 1) * length],
                (((1,), (1,)), ((), ())),
                preferred_element_type=f32,
            )
            for j in range(devices - lag):
                term = part[size * j : size * (j + 1)]
                totals[j] = term if totals[j] is None else totals[j] + term
        gg_parts.append(jnp.concatenate(totals, axis=1))
        right = jnp.concatenate([high[own, j * SUB : (j + 1) * SUB] for j in range(subs)], axis=0)
        turned = flips[g]
        lines = []
        for lag in range(subs):
            cross = jnp.dot(
                turned[:, : size * (subs - lag)], right[size * lag :], preferred_element_type=f32
            )
            wide = jnp.concatenate([cross, jnp.zeros((SUB, SUB), f32)], axis=1)
            wide = pltpu.roll(wide, 1, 1, stride=1, stride_axis=0)
            lines.append(jnp.sum(wide, axis=0, keepdims=True))
        per = length // SUB
        for lag in range(subs):
            line = lines[lag][:, SUB:]
            if lag + 1 < subs:
                line += lines[lag + 1][:, :SUB]
            b, within = divmod(lag, per)
            small[b, g : g + 1, within * SUB : (within + 1) * SUB] = line
    grad_gated = jnp.concatenate(gg_parts, axis=0)
    grads[...] = grad_gated.astype(bf16)
    lane = lax.broadcasted_iota(jnp.int32, (chunk, SUB), 1)
    sums = jnp.zeros((chunk, SUB), f32)
    for n in range(stacked * taps):
        tap = jnp.sum(grad_gated * sum_w[n], axis=1, keepdims=True)
        sums += jnp.where(lane == groups + taps + n, tap, 0.0)
    marks[...] = jnp.zeros_like(marks)
    marks[:, 0:chunk] = sums.T
    common += pltpu.roll(marks[0:16], me * chunk, 1)
    count = (stacked + 1) * taps
    start = 2 * groups + 2 * count
    high = common.astype(bf16).astype(f32)
    for b in range(devices):
        lines = small[b, 0:groups]
        top = lines.astype(bf16).astype(f32)
        small[b, 0:groups] = top
        small[b, groups : 2 * groups] = lines - top
        small[b, 2 * groups : 2 * groups + count] = high[groups : groups + count]
        small[b, 2 * groups + count : start] = (common - high)[groups : groups + count]
        small[b, start : start + reach] = early_query[16 - reach :]
        if b == devices - 1:
            continue
        first = grad_gated[:, (b + 1) * length : (b + 1) * length + SUB]
        for i in range(stacked):
            early = jnp.zeros((chunk, SUB), f32)
            for s in range(1, taps):
                weight = early_w[i * reach + s - 1, :, b * SUB : (b + 1) * SUB]
                back = pltpu.roll(weight * first, SUB - s, 1)
                early += jnp.where(lane >= SUB - s, back, 0.0)
            marks[:, 0:chunk] = early.T
            placed = pltpu.roll(marks[SUB - 16 :], me * chunk, 1)
            at = start + (i + 1) * reach
            small[b, at : at + reach] = placed[16 - reach :]
    for s in range(devices):
        to = lax.rem(me + s, devices)
        outs[s][0:chunk] = grads[:, block_at(to, length)]
        outs[s][chunk:] = small[to].astype(bf16)


def small_sum_kernel(devices, groups, stacked, taps, *refs):
    pays, (sums, later, tiles) = refs[:devices], refs[devices:]
    me = lax.axis_index("ctx")
    width = pays[0].shape[1]
    body = width // devices
    count = stacked * taps
    start = 2 * groups + 2 * count
    reach = taps - 1
    for s in range(devices):
        tiles[lax.rem(me - s + devices, devices)] = pays[s][body:].astype(f32)
    total = tiles[0]
    for c in range(1, devices):
        total += tiles[c]
    lines = [tiles[c, 0:groups] + tiles[c, groups : 2 * groups] for c in range(devices)]
    taps_sum = total[2 * groups : 2 * groups + count] + total[2 * groups + count : start]
    for n, value in enumerate((jnp.concatenate(lines, axis=0), taps_sum)):
        if value.shape[0] < 16:
            rest = jnp.zeros((16 - value.shape[0], width), f32)
            value = jnp.concatenate([value, rest], axis=0)
        for h, half in enumerate(split_bf16(value)):
            sums[:, (2 * h + n) * width : (2 * h + n + 1) * width] = half
    last = pays[devices - 1][body:].astype(f32)
    later[...] = jnp.zeros_like(later)
    later[0, 16 - reach : 16] = last[start : start + reach]
    for i in range(1, stacked):
        later[i, 16 - reach : 16] = total[start + i * reach : start + (i + 1) * reach]


def grad_out_kernel(devices, taps, query_part, pair_w, later, *refs):
    pays, (out, gated) = refs[:devices], refs[devices:]
    me = lax.axis_index("ctx")
    stacked, rows, width = out.shape
    chunk = width // devices
    for s in range(devices):
        at = block_at(lax.rem(me - s + devices, devices), chunk)
        gated[at] = pays[s][0:chunk].astype(f32)
    for i in range(stacked):
        if i == 0:
            turned = query_part[...]
        else:
            j = (i - 1) * taps
            total = pair_w[j] * gated[...]
            for s in range(1, taps):
                total += pltpu.roll(pair_w[j + s] * gated[...], rows - s, 1)
            turned = total.T
        out[i, 0 : rows - 16] = turned[0 : rows - 16].astype(bf16)
        out[i, rows - 16 :] = (turned[rows - 16 :] + later[i]).astype(bf16)


def final_kernel(devices, scale, *refs):
    near, far, refs = refs[:devices], refs[devices : 2 * devices], refs[2 * devices :]
    mine, other, weight_out, short_out, long_out = refs
    me, core = lax.axis_index("ctx"), lax.axis_index("dp")
    rows = near[0].shape[0]
    for side, blocks in ((core, near), (1 - core, far)):
        for s in range(devices):
            at = side * devices + lax.rem(me - s + devices, devices)
            weight_out[block_at(at, rows)] = blocks[s][...].astype(f32)
    width = long_out.shape[1]
    stacked, taps, _ = short_out.shape

    def sums(n):
        pieces = []
        for ref in (mine, other):
            high = ref[:, n * width : (n + 1) * width].astype(f32)
            low = ref[:, (n + 2) * width : (n + 3) * width].astype(f32)
            pieces.append(high + low)
        return (pieces[0] + pieces[1]) * scale

    long_out[...] = sums(0)
    total = sums(1)
    for i in range(stacked):
        short_out[i] = total[i * taps : (i + 1) * taps]


def direct_device(projected, segment_ids, short_filter, long_filter, out_proj, mixed_cotangent):
    devices, parts = lax.axis_size("ctx"), lax.axis_size("tp")
    stacked, _, length, width = projected.shape
    taps = short_filter.shape[1]
    count = long_filter.shape[0]
    groups = count // devices
    chunk = width // devices
    span = length * devices
    total_cols = out_proj.shape[1]
    grad_scale = 1.0 / math.sqrt(projected.shape[1] * lax.axis_size("dp") * span)
    cotangent = mixed_cotangent[0]
    room = 16
    inputs = (projected[:, 0], long_filter, segment_ids)

    outs = on_core(
        functools.partial(pack_kernel, devices, taps - 1),
        [
            (((stacked - 1) * chunk + (2 * room if s == 1 else room), length), bf16)
            for s in range(devices)
        ],
        inputs,
        "pack",
        [
            pltpu.VMEM((stacked - 1, length, width), bf16),
            pltpu.VMEM((16, width), bf16),
            pltpu.VMEM(long_filter.shape, f32),
            pltpu.VMEM(segment_ids.shape, jnp.int32),
            pltpu.VMEM((stacked - 1, width, length), bf16),
            pltpu.VMEM((room, length), f32),
            pltpu.VMEM((room, width), f32),
            pltpu.SemaphoreType.DMA((5,)),
        ],
        whole=True,
    )
    own, *signal = scatter_chunks(outs, "ctx")
    beside = swap(cotangent, "tp", 1)
    columns, own, turned = on_core(
        prepare_kernel,
        [((width, 16), f32), (own.shape, bf16), ((stacked, width, length), bf16)],
        (after(short_filter, beside), own, inputs[0]),
        "prepare",
        [pltpu.VMEM((16, width), f32)],
    )
    signal = [own, *signal]

    conv_flops = 2 * groups * span * span * 64
    outs = on_core(
        functools.partial(conv_kernel, devices, taps),
        [((chunk, length), bf16)] * devices
        + [
            ((stacked - 1, chunk, span), f32),
            (((stacked - 1) * chunk, span), bf16),
            ((8, span), f32),
            ((groups, length, span), bf16),
        ],
        (columns, *signal),
        "conv",
        [
            pltpu.VMEM((room, span), f32),
            pltpu.VMEM((chunk, span), bf16),
            pltpu.VMEM((groups, length, span), bf16),
        ],
        flops=900_000_000,
    )
    longs, kept = outs[:devices], outs[devices:]
    seg = kept[2]
    cots = [cotangent, beside, swap(cotangent, "tp", 2), swap(beside, "tp", 2)]
    outs = on_core(
        functools.partial(grad_y_kernel, devices, parts, taps),
        [((2 * chunk, length), bf16)] * devices + [((width, length), f32)] * 2,
        (out_proj, turned, signal[1], columns, seg, *cots, *longs),
        "grad_y",
        [pltpu.VMEM((8 * taps, span), f32), pltpu.VMEM((width, length), bf16)],
        flops=2 * width * length * total_cols,
    )
    pairs, (grad_y, query_conv) = outs[:devices], outs[devices:]
    pairs = scatter_chunks(pairs, "ctx")

    pair_w, *factors = on_core(
        functools.partial(ready_kernel, devices, taps),
        [
            (((stacked - 1) * taps, width, length), f32),
            ((taps, width, length), f32),
            ((taps - 1, width, length), f32),
            ((groups, SUB, SUB), bf16),
            (((stacked - 1) * taps, chunk, span), f32),
            (((stacked - 1) * (taps - 1), chunk, (devices - 1) * SUB), f32),
        ],
        (turned, signal[1], columns, seg, *kept[:2]),
        "ready",
        [pltpu.VMEM((8 * taps, span), f32)],
    )
    query_conv = after(query_conv, factors[0])

    half = width // 2
    y, long, keep, send = on_core(
        functools.partial(weight_grad_kernel, devices, parts),
        [
            ((width, length), bf16),
            ((width, length), f32),
            ((half, total_cols), f32),
            ((half, total_cols), bf16),
        ],
        (query_conv, *cots, *pairs),
        "weight_grad",
        [pltpu.VMEM((width, total_cols), f32)],
        flops=2 * width * length * total_cols,
    )
    other = rotate(send, "dp", 1)
    kept_part, sent_part = on_core(
        mixed_part_kernel,
        [((2 * length, width), f32), ((2 * length, width), bf16)],
        (y, out_proj),
        "mixed_part",
        [pltpu.VMEM((length, total_cols), f32)],
        flops=2 * width * length * total_cols,
    )
    keep = after(keep, kept_part)
    rows = half // devices
    sums = on_core(
        functools.partial(core_sum_kernel, devices),
        [((rows, total_cols), f32)] + [((rows, total_cols), bf16)] * (devices - 1),
        (keep, other),
        "core_sum",
        [pltpu.VMEM((half, total_cols), f32)],
    )
    parts_out = scatter_chunks(sums, "ctx")

    outs = on_core(
        functools.partial(backward_kernel, devices, taps),
        [((chunk + 2 * room, length), bf16)] * devices + [((length, width), f32)],
        (kept[3], columns, grad_y, after(long, sums[1]), *factors, *pairs),
        "backward",
        [
            pltpu.VMEM((chunk, span), bf16),
            pltpu.VMEM((chunk, span), bf16),
            pltpu.VMEM((devices, 2 * room, length), f32),
            pltpu.VMEM((SUB, width), f32),
        ],
        flops=2 * conv_flops,
    )
    back, query_part = outs[:devices], outs[devices]
    back = scatter_chunks(back, "ctx")
    sums, later = on_core(
        functools.partial(small_sum_kernel, devices, groups, stacked, taps),
        [((16, total_cols), bf16), ((stacked, 16, width), f32)],
        back,
        "small_sum",
        [pltpu.VMEM((devices, 2 * room, width), f32)],
        flops=2_000_000_000,
    )
    (grad_projected,) = on_core(
        functools.partial(grad_out_kernel, devices, taps),
        [((stacked, length, width), bf16)],
        (query_part, pair_w, later, *back),
        "grad_out",
        [pltpu.VMEM((width, length), f32)],
    )
    (block,) = on_core(
        functools.partial(block_sum_kernel, grad_scale),
        [((rows, total_cols), bf16)],
        parts_out,
        "block_sum",
    )
    own_part, sent_part = on_core(
        mixed_pair_kernel,
        [((length, width), f32), ((length, width), bf16)],
        (after(kept_part, query_part), swap(sent_part, "tp", 1)),
        "mixed_pair",
    )
    come_part = swap(sent_part, "tp", 2)
    (mixed,) = on_core(
        mixed_sum_kernel, [((length, width), bf16)], (own_part, come_part), "mixed_sum"
    )

    near = spread(block, "ctx")
    other_sums = rotate(sums, "dp", 1)
    near[1] = after(near[1], (grad_projected, come_part, other_sums))
    far = [rotate(piece, "dp", 1) for piece in near]
    grad_out_proj, grad_short, grad_long = on_core(
        functools.partial(final_kernel, devices, grad_scale),
        [((width, total_cols), f32), (short_filter.shape, f32), ((count, length), f32)],
        (*near, *far, sums, other_sums),
        "final",
    )
    return (mixed[None], grad_projected[:, None], grad_short, grad_long, grad_out_proj)


def direct_fits(mesh, projected, short_filter, long_filter, out_proj):
    devices = mesh.shape["ctx"]
    length = projected.shape[2] // devices
    width = projected.shape[3] // mesh.shape["tp"]
    groups = long_filter.shape[0] // mesh.shape["tp"]
    stacked, taps = short_filter.shape[:2]
    return (
        mesh.shape["dp"] == 2
        and mesh.shape["tp"] == 4
        and projected.shape[1] == 2
        and stacked == 3
        and length == width
        and length % SUB == 0
        and groups % devices == 0
        and groups == 16
        and (width // devices) % 16 == 0
        and width // devices <= SUB
        and (width // groups) == 16
        and 2 * groups // devices + 2 <= 16
        and out_proj.shape[1] == 4 * width
        and stacked * (taps - 1) <= 16
        and groups // devices + stacked * taps <= 16
        and 2 * (groups // devices) + 2 * stacked * taps + stacked * (taps - 1) <= 32
    )


def solution(mesh):
    in_specs = (
        P(None, "dp", "ctx", "tp"),
        P("dp", "ctx"),
        P(None, None, "tp"),
        P("tp", "ctx"),
        P("tp", None),
        P("dp", "ctx", "tp"),
    )
    out_specs = (
        P("dp", "ctx", "tp"),
        P(None, "dp", "ctx", "tp"),
        P(None, None, "tp"),
        P("tp", "ctx"),
        P("tp", None),
    )

    def layer(projected, segment_ids, short_filter, long_filter, out_proj, mixed_cotangent):
        fits = direct_fits(mesh, projected, short_filter, long_filter, out_proj)
        return jax.shard_map(
            direct_device if fits else spectral_device,
            mesh=mesh,
            in_specs=in_specs,
            out_specs=out_specs,
            check_vma=False,
        )(projected, segment_ids, short_filter, long_filter, out_proj, mixed_cotangent)

    return layer
```

```python
import functools
import math

import jax
import jax.numpy as jnp
from jax import lax
from jax.experimental import pallas as pl
from jax.experimental.pallas import tpu as pltpu
from jax.sharding import PartitionSpec as P

highest_precision = lax.Precision.HIGHEST


def shifted(value, axis, steps):
    count = lax.axis_size(axis)
    first, last = (max(0, -steps), min(count, count - steps))
    return lax.ppermute(value, axis, [(source, source + steps) for source in range(first, last)])


def angle_table(height, breadth, period, direction):
    product = (
        jnp.arange(height, dtype=jnp.int32)[:, None]
        * jnp.arange(breadth, dtype=jnp.int32)[None, :]
        % period
    )
    angles = direction * 2.0 * math.pi / period * product.astype(jnp.float32)
    return (jnp.cos(angles), jnp.sin(angles))


def row_twiddle(spec_re, spec_im, direction):
    my_index = lax.axis_index("ctx")
    devices = lax.axis_size("ctx")
    row_count = spec_re.shape[1]
    period = 2 * devices * row_count
    freq_pair = 2 * my_index + jnp.arange(2, dtype=jnp.int32)
    product = freq_pair[:, None] * jnp.arange(row_count, dtype=jnp.int32)[None, :] % period
    angles = direction * 2.0 * math.pi / period * product.astype(jnp.float32)
    cosine = jnp.cos(angles)[:, :, None]
    sine_part = jnp.sin(angles)[:, :, None]
    return (spec_re * cosine - spec_im * sine_part, spec_re * sine_part + spec_im * cosine)


def row_transform(spec_re, spec_im, direction):
    row_count = spec_re.shape[1]
    cosine, sine_part = angle_table(row_count, row_count, row_count, direction)

    def along_rows(blocks, matrix):
        return jnp.einsum("kmc,mq->kqc", blocks, matrix, precision=highest_precision)

    return (
        along_rows(spec_re, cosine) - along_rows(spec_im, sine_part),
        along_rows(spec_re, sine_part) + along_rows(spec_im, cosine),
    )


def mixing(matrix, blocks):
    return jnp.einsum("kj,jmc->kmc", matrix, blocks, precision=highest_precision)


def forward_spectrum(real_part):
    devices = lax.axis_size("ctx")
    cosine, sine_part = angle_table(2 * devices, devices, 2 * devices, -1.0)
    spread_re = lax.all_to_all(real_part[None], "ctx", split_axis=1, concat_axis=0, tiled=True)
    column_re = mixing(cosine, spread_re)
    column_im = mixing(sine_part, spread_re)
    near_re, near_im = (
        lax.all_to_all(column_re, "ctx", split_axis=0, concat_axis=1, tiled=True),
        lax.all_to_all(column_im, "ctx", split_axis=0, concat_axis=1, tiled=True),
    )
    twist_re, twist_im = row_twiddle(near_re, near_im, -1.0)
    return row_transform(twist_re, twist_im, -1.0)


def inverse_spectrum(spec_re, spec_im):
    devices = lax.axis_size("ctx")
    row_count = spec_re.shape[1]
    back_re, back_im = row_transform(spec_re, spec_im, 1.0)
    twist_re, twist_im = row_twiddle(back_re / row_count, back_im / row_count, 1.0)
    far_re, far_im = (
        lax.all_to_all(twist_re, "ctx", split_axis=1, concat_axis=0, tiled=True),
        lax.all_to_all(twist_im, "ctx", split_axis=1, concat_axis=0, tiled=True),
    )
    cosine, sine_part = angle_table(devices, 2 * devices, 2 * devices, 1.0)
    out_re = (mixing(cosine, far_re) - mixing(sine_part, far_im)) / (2 * devices)
    rows_re = lax.all_to_all(out_re, "ctx", split_axis=0, concat_axis=1, tiled=True)
    return (rows_re[0], rows_re[0])


def pack_columns(values):
    return (values, values)


def by_filter(val_re, val_im, fil_re, fil_im, conjugate):
    val_shape = val_re.shape
    group_count = fil_re.shape[2]
    v_re = val_re.reshape(val_shape[0], val_shape[1], group_count, -1)
    v_im = val_im.reshape(val_shape[0], val_shape[1], group_count, -1)
    f_re = fil_re[:, :, :, None]
    f_im = fil_im[:, :, :, None]
    if conjugate:
        f_im = -f_im
    out_re = v_re * f_re - v_im * f_im
    out_im = v_re * f_im + v_im * f_re
    return (out_re.reshape(val_shape), out_im.reshape(val_shape))


def short_local(extended, filters, seg_ext):
    reach_taps = filters.shape[1]
    out_rows = extended.shape[1] - reach_taps + 1
    own_seg = seg_ext[reach_taps - 1 :]
    running = jnp.zeros((extended.shape[0], out_rows, extended.shape[2]), jnp.float32)
    for shift_by in range(reach_taps):
        start_row = reach_taps - 1 - shift_by
        same_doc = jnp.where(seg_ext[start_row : start_row + out_rows] == own_seg, 1.0, 0.0)
        running = (
            running
            + filters[:, shift_by][:, None, :]
            * same_doc[None, :, None]
            * extended[:, start_row : start_row + out_rows]
        )
    return running


def spectral_device(projected, segment_ids, short_filter, long_filter, out_proj, mixed_cotangent):
    row_count = projected.shape[2]
    stacked = projected.shape[0]
    width_dev = projected.shape[3]
    short_reach = short_filter.shape[1]
    group_count = long_filter.shape[0]
    grad_scale = 1.0 / math.sqrt(
        projected.shape[1] * lax.axis_size("dp") * row_count * lax.axis_size("ctx")
    )
    segments = segment_ids[0]
    source = projected[:, 0]
    short_rows = short_reach - 1
    cot_full = lax.all_gather(mixed_cotangent[0], "tp", axis=1, tiled=True)
    prev_tail, prev_seg = shifted(
        (source[:, row_count - short_rows :], segments[row_count - short_rows :]), "ctx", 1
    )
    short_seg = jnp.concatenate([prev_seg, segments])
    short_ext = jnp.concatenate([prev_tail, source], axis=1).astype(jnp.float32)

    def short_piece(extended, filters):
        return short_local(extended, filters, short_seg)

    short_out, short_pull = jax.vjp(short_piece, short_ext, short_filter)
    query_conv = short_out[0]
    gated_rows = short_out[1] * short_out[2]
    filter_cols = long_filter.T
    mid_re, mid_im = pack_columns(gated_rows)
    spec_re, spec_im = forward_spectrum(jnp.concatenate([mid_re, filter_cols], axis=1))
    data_cols = spec_re.shape[2] - group_count
    signal_re = spec_re[:, :, :data_cols]
    signal_im = spec_im[:, :, :data_cols]
    filt_re = spec_re[:, :, data_cols:]
    filt_im = spec_im[:, :, data_cols:]
    long_re, long_im = by_filter(signal_re, signal_im, filt_re, filt_im, False)
    out_re, out_im = inverse_spectrum(long_re, long_im)
    y_out = (query_conv * out_re).astype(jnp.bfloat16)
    partial_out = jnp.dot(y_out, out_proj, preferred_element_type=jnp.float32)
    mixed = lax.psum_scatter(partial_out, "tp", scatter_dimension=1, tiled=True).astype(
        jnp.bfloat16
    )
    grad_y = jnp.dot(cot_full, out_proj.T, preferred_element_type=jnp.float32)
    grad_proj_local = jnp.dot(y_out.T, cot_full, preferred_element_type=jnp.float32)
    grad_long_out = grad_y * query_conv
    grad_query = grad_y * out_re
    grad_in_re, grad_in_im = pack_columns(grad_long_out)
    cot_re, cot_im = forward_spectrum(grad_in_re)
    back_re, back_im = by_filter(cot_re, cot_im, filt_re, filt_im, True)
    cross_re = (
        (signal_re * cot_re + signal_im * cot_im).reshape(2, row_count, group_count, -1).sum(axis=3)
    )
    cross_im = (
        (signal_re * cot_im - signal_im * cot_re).reshape(2, row_count, group_count, -1).sum(axis=3)
    )
    inv_re, inv_im = inverse_spectrum(
        jnp.concatenate([back_re, cross_re], axis=2), jnp.concatenate([back_im, cross_im], axis=2)
    )
    grad_gated = inv_re[:, :data_cols]
    grad_long_local = inv_re[:, data_cols:].T
    grad_short_out = jnp.stack([grad_query, grad_gated * short_out[2], grad_gated * short_out[1]])
    grad_short_ext, grad_short_local = short_pull(grad_short_out)
    returned_short = shifted(grad_short_ext[:, :short_rows], "ctx", -1)
    grad_source = grad_short_ext[:, short_rows:] + jnp.concatenate(
        [jnp.zeros((stacked, row_count - short_rows, width_dev), jnp.float32), returned_short],
        axis=1,
    )
    total_proj, total_short = lax.psum((grad_proj_local, grad_short_local), ("ctx", "dp"))
    total_long = lax.psum(grad_long_local, "dp")
    return (
        mixed[None],
        grad_source[:, None].astype(jnp.bfloat16),
        total_short * grad_scale,
        total_long * grad_scale,
        total_proj * grad_scale,
    )


bf16 = jnp.bfloat16
f32 = jnp.float32
SUB = 128


def split_bf16(value):
    high = value.astype(bf16)
    return high, (value - high.astype(f32)).astype(bf16)


def rotate(value, axis, steps):
    count = lax.axis_size(axis)
    return lax.ppermute(value, axis, [(i, (i + steps) % count) for i in range(count)])


def swap(value, axis, bits):
    return lax.ppermute(value, axis, [(i, i ^ bits) for i in range(lax.axis_size(axis))])


def scatter_chunks(chunks, axis):
    return [chunks[0]] + [rotate(chunks[s], axis, s) for s in range(1, len(chunks))]


def after(value, other):
    return lax.optimization_barrier((value, other))[0]


def spread(value, axis):
    return [value] + [rotate(value, axis, s) for s in range(1, lax.axis_size(axis))]


def on_core(kernel, outs, args, name, scratch=(), flops=0, whole=False):
    moved = sum(a.size * a.dtype.itemsize for a in args)
    moved += sum(math.prod(shape) * jnp.dtype(kind).itemsize for shape, kind in outs)
    return pl.pallas_call(
        kernel,
        out_shape=[jax.ShapeDtypeStruct(shape, kind) for shape, kind in outs],
        in_specs=[pl.BlockSpec(memory_space=pltpu.HBM) if whole else pl.BlockSpec()] * len(args),
        scratch_shapes=list(scratch),
        compiler_params=pltpu.CompilerParams(vmem_limit_bytes=(63 if whole else 40) * 1024 * 1024),
        cost_estimate=pl.CostEstimate(flops=flops, bytes_accessed=moved, transcendentals=0),
        name=name,
    )(*args)


def block_at(index, size):
    return pl.ds(pl.multiple_of(index * size, size), size)


def pack_kernel(devices, reach, projected, filter_source, segment_source, *refs):
    outs, refs = refs[:devices], refs[devices:]
    pair, query, filters, segments, turned, small, tail, sems = refs
    _, rows, _ = projected.shape
    sources = (
        (projected.at[1], pair.at[0]),
        (projected.at[2], pair.at[1]),
        (projected.at[0, pl.ds(rows - 16, 16)], query),
        (filter_source, filters),
        (segment_source, segments),
    )
    copies = [
        pltpu.make_async_copy(source, held, sems.at[n])
        for n, (source, held) in enumerate(sources)
    ]
    for copy in copies:
        copy.start()
    me = lax.axis_index("ctx")
    width = pair.shape[2]
    chunk = width // devices
    count = filters.shape[0]
    groups = count // devices
    body = pair.shape[0] * chunk
    small[...] = jnp.zeros_like(small)
    tail[...] = jnp.zeros_like(tail)
    for i in range(pair.shape[0]):
        copies[i].wait()
        turned[i] = pair[i].T
    for copy in copies[2:]:
        copy.wait()
    for i, last in enumerate((query[...], pair[0, rows - 16 :], pair[1, rows - 16 :])):
        tail[i * reach : (i + 1) * reach] = last.astype(f32)[16 - reach :]
    seg = segments[...]
    small[2 * groups : 2 * groups + 1] = (seg >> 8).astype(f32)
    small[2 * groups + 1 : 2 * groups + 2] = (seg & 255).astype(f32)
    for s in range(devices):
        to = lax.rem(me + s, devices)
        for i in range(pair.shape[0]):
            outs[s][i * chunk : (i + 1) * chunk] = turned[i, block_at(to, chunk)]
        lines = pltpu.roll(filters[...], lax.rem(count - to * groups, count), 0)[0:groups]
        high = lines.astype(bf16).astype(f32)
        small[0:groups] = high
        small[groups : 2 * groups] = lines - high
        outs[s][body : body + 16] = small[...].astype(bf16)
    outs[1][body + 16 :] = tail[...].astype(bf16)


def prepare_kernel(short_filter, chunk, projected, columns, chunk_out, turned, flat):
    stacked, taps, _ = short_filter.shape
    flat[...] = jnp.zeros_like(flat)
    for i in range(stacked):
        flat[i * taps : (i + 1) * taps] = short_filter[i]
        turned[i] = projected[i].T
    columns[...] = flat[...].T
    chunk_out[...] = chunk[...]


def tap_masks(seg, taps):
    wide = jnp.broadcast_to(seg, (8, seg.shape[1]))
    place = lax.broadcasted_iota(jnp.int32, wide.shape, 1)
    masks = [None]
    for s in range(1, taps):
        same = (wide == pltpu.roll(wide, s, 1)) & (place >= s)
        masks.append(jnp.where(same, 1.0, 0.0)[0:1])
    return masks


def block_masks(seg, taps, place, me, length):
    masks = tap_masks(seg, taps)
    for s in range(1, taps):
        place[8 * s : 8 * (s + 1)] = jnp.broadcast_to(masks[s], (8, seg.shape[1]))
    return [None] + [place[8 * s : 8 * s + 8, block_at(me, length)][0:1] for s in range(1, taps)]


def local_shifts(turned, previous, taps, i):
    tail = previous[previous.shape[0] - 16 :].astype(f32)
    before = jnp.concatenate([tail, jnp.zeros((SUB - 16, tail.shape[1]), f32)], axis=0)
    before = pltpu.roll(before, SUB - (taps - 1) * (i + 1), 0)
    wide = jnp.concatenate([before.T, turned[i].astype(f32)], axis=1)
    return [wide[:, SUB:]] + [pltpu.roll(wide, s, 1)[:, SUB:] for s in range(1, taps)]


def local_conv(turned, previous, columns, masks, i):
    taps = len(masks)
    shifts = local_shifts(turned, previous, taps, i)
    j = i * taps
    total = columns[:, j : j + 1] * shifts[0]
    for s in range(1, taps):
        total += columns[:, j + s : j + s + 1] * (masks[s] * shifts[s])
    return total


def conv_kernel(devices, taps, columns, *rest):
    pays, rest = rest[:devices], rest[devices:]
    outs, rest = rest[:devices], rest[devices:]
    conv, source, seg_out, toeplitz, small, long, rests = rest
    me = lax.axis_index("ctx")
    stacked, chunk, span = conv.shape
    length = span // devices
    groups = toeplitz.shape[0]
    size = chunk // groups
    body = stacked * chunk
    for s in range(devices):
        at = block_at(lax.rem(me - s + devices, devices), length)
        source[:, at] = pays[s][0:body]
        small[:, at] = pays[s][body : body + 16].astype(f32)
    seg = small[2 * groups : 2 * groups + 1] * 256.0 + small[2 * groups + 1 : 2 * groups + 2]
    seg_out[...] = jnp.broadcast_to(seg, seg_out.shape)
    masks = tap_masks(seg, taps)
    column = columns[block_at(me, chunk)]
    for i in range(stacked):
        x = source[i * chunk : (i + 1) * chunk].astype(f32)
        j = (i + 1) * taps
        total = column[:, j : j + 1] * x
        for s in range(1, taps):
            total += column[:, j + s : j + s + 1] * (masks[s] * pltpu.roll(x, s, 1))
        conv[i] = total
    high, low = split_bf16(conv[0] * conv[1])
    for g in range(groups):
        line = small[g : g + 1] + small[groups + g : groups + g + 1]
        padded = jnp.concatenate([line, jnp.zeros((1, SUB), f32)], axis=1)
        turned = pltpu.roll(
            jnp.broadcast_to(padded, (SUB, span + SUB)), 0, 1, stride=1, stride_axis=0
        )[:, :span]
        for half, into in zip(split_bf16(turned), (toeplitz, rests)):
            for r in range(length // SUB):
                rows = slice(r * SUB, (r + 1) * SUB)
                if r:
                    into[g, rows, : r * SUB] = jnp.zeros((SUB, r * SUB), bf16)
                into[g, rows, r * SUB :] = half[:, : span - r * SUB]
        own = slice(g * size, (g + 1) * size)
        pieces = []
        for j in range(devices):
            at = slice(j * length, (j + 1) * length)
            pieces += [high[own, at], low[own, at]]
        stack = jnp.concatenate(pieces, axis=0)
        totals = [None] * devices
        for lag in range(devices):
            lhs = stack[: 2 * size * (devices - lag)]
            at = slice(lag * length, (lag + 1) * length)
            part = jnp.dot(lhs, toeplitz[g, :, at], preferred_element_type=f32)
            part += jnp.dot(lhs, rests[g, :, at], preferred_element_type=f32)
            for j in range(devices - lag):
                term = part[2 * size * j : 2 * size * j + size]
                term += part[2 * size * j + size : 2 * size * (j + 1)]
                i = j + lag
                totals[i] = term if totals[i] is None else totals[i] + term
        for i in range(devices):
            long[own, i * length : (i + 1) * length] = totals[i].astype(bf16)
    for s in range(devices):
        outs[s][...] = long[:, block_at(lax.rem(me + s, devices), length)]


def grad_y_kernel(devices, parts, taps, weights, turned, previous, columns, seg, *rest):
    cots, rest = rest[:parts], rest[parts:]
    longs, rest = rest[:devices], rest[devices:]
    outs, (grad_y, query_conv, place, full) = rest[:devices], rest[devices:]
    me, mine = lax.axis_index("ctx"), lax.axis_index("tp")
    rows, width = cots[0].shape
    chunk = width // devices
    masks = block_masks(seg[0:1], taps, place, me, rows)
    conv = local_conv(turned, previous, columns, masks, 0)
    query_conv[...] = conv
    total = None
    for s in range(parts):
        cot = cots[s][...]
        lhs = weights[:, block_at(mine ^ s, width)]
        term = lax.dot_general(lhs, cot, (((1,), (1,)), ((), ())), preferred_element_type=f32)
        total = term if total is None else total + term
    grad_y[...] = total
    full[...] = (total * conv).astype(bf16)
    for s in range(devices):
        outs[s][0:chunk] = longs[s][...]
        outs[s][chunk:] = full[block_at(lax.rem(me + s, devices), chunk)]


def weight_grad_kernel(devices, parts, query_conv, *rest):
    cots, rest = rest[:parts], rest[parts:]
    longs, rest = rest[:devices], rest[devices:]
    y_out, long_out, keep, send, full = rest
    me, mine, core = lax.axis_index("ctx"), lax.axis_index("tp"), lax.axis_index("dp")
    rows, width = cots[0].shape
    chunk = width // devices
    half = width // 2
    for s in range(devices):
        at = block_at(lax.rem(me - s + devices, devices), chunk)
        long_out[at] = longs[s][0:chunk].astype(f32)
    y = (query_conv[...] * long_out[...]).astype(bf16)
    y_out[...] = y
    for s in range(parts):
        cot = cots[s][...]
        at = block_at(mine ^ s, width)
        full[:, at] = jnp.dot(y, cot, preferred_element_type=f32)
    keep[...] = full[block_at(core, half)]
    send[...] = full[block_at(1 - core, half)].astype(send.dtype)


def core_sum_kernel(devices, keep, other, *rest):
    outs, (full,) = rest[:devices], rest[devices:]
    me = lax.axis_index("ctx")
    rows = keep.shape[0] // devices
    full[...] = keep[...] + other[...].astype(f32)
    for s in range(devices):
        at = block_at(lax.rem(me + s, devices), rows)
        outs[s][...] = full[at].astype(outs[s].dtype)


def block_sum_kernel(scale, *refs):
    total = refs[0][...]
    for ref in refs[1:-1]:
        total += ref[...].astype(f32)
    refs[-1][...] = (total * scale).astype(bf16)


def mixed_part_kernel(y, weights, kept, sent, full):
    mine = lax.axis_index("tp")
    rows, width = full.shape[0], y.shape[0]
    full[...] = lax.dot_general(
        y[...], weights[...], (((0,), (0,)), ((), ())), preferred_element_type=f32
    )
    for h in range(2):
        kept[h * rows : (h + 1) * rows] = full[:, block_at(mine ^ (2 * h), width)]
        sent[h * rows : (h + 1) * rows] = full[:, block_at(mine ^ (2 * h + 1), width)].astype(bf16)


def mixed_pair_kernel(kept, come, own, sent):
    rows = own.shape[0]
    own[...] = kept[0:rows] + come[0:rows].astype(f32)
    sent[...] = (kept[rows:] + come[rows:].astype(f32)).astype(bf16)


def mixed_sum_kernel(own, come, out):
    out[...] = (own[...] + come[...].astype(f32)).astype(bf16)


def ready_kernel(devices, taps, turned, previous, columns, seg, conv, source, *rest):
    pair_w, query_taps, query_w, flips, sum_w, early_w, place = rest
    me = lax.axis_index("ctx")
    stacked, chunk, span = conv.shape
    _, width, length = turned.shape
    groups = flips.shape[0]
    size = chunk // groups
    subs = span // SUB
    own = block_masks(seg[0:1], taps, place, me, length)
    shifts = local_shifts(turned, previous, taps, 0)
    position = lax.broadcasted_iota(jnp.int32, (width, length), 1)
    query_taps[0] = shifts[0]
    for s in range(1, taps):
        query_taps[s] = own[s] * shifts[s]
        query_w[s - 1] = jnp.broadcast_to(columns[:, s : s + 1] * own[s], (width, length))
    for i in range(stacked):
        other = local_conv(turned, previous, columns, own, stacked - i)
        j = (i + 1) * taps
        pair_w[i * taps] = columns[:, j : j + 1] * other
        for s in range(1, taps):
            weight = columns[:, j + s : j + s + 1] * own[s] * other
            pair_w[i * taps + s] = jnp.where(position >= s, weight, 0.0)
    masks = tap_masks(seg[0:1], taps)
    column = columns[block_at(me, chunk)]
    for i in range(stacked):
        x = source[i * chunk : (i + 1) * chunk].astype(f32)
        other = conv[1 - i]
        j = (i + 1) * taps
        sum_w[i * taps] = other * x
        for s in range(1, taps):
            masked = masks[s] * other
            sum_w[i * taps + s] = masked * pltpu.roll(x, s, 1)
            weight = column[:, j + s : j + s + 1] * masked
            for b in range(devices - 1):
                at = slice((b + 1) * length, (b + 1) * length + SUB)
                early_w[i * (taps - 1) + s - 1, :, b * SUB : (b + 1) * SUB] = weight[:, at]
    gated = (conv[0] * conv[1]).astype(bf16)
    corner = lax.broadcasted_iota(jnp.int32, (SUB, SUB), 0)
    corner += lax.broadcasted_iota(jnp.int32, (SUB, SUB), 1)
    flip = jnp.where(corner == SUB - 1, 1.0, 0.0).astype(bf16)
    for g in range(groups):
        rows = slice(g * size, (g + 1) * size)
        left = jnp.concatenate([gated[rows, j * SUB : (j + 1) * SUB] for j in range(subs)], axis=0)
        flips[g] = lax.dot_general(
            flip, left, (((1,), (1,)), ((), ())), preferred_element_type=f32
        ).astype(bf16)


def backward_kernel(
    devices, taps, toeplitz, columns, grad_y, long, query_taps, query_w, flips, sum_w, early_w, *rest
):
    glos, rest = rest[:devices], rest[devices:]
    outs, (query_out, grad_long_out, grads, small, marks) = rest[:devices], rest[devices:]
    me = lax.axis_index("ctx")
    _, chunk, span = sum_w.shape
    stacked = sum_w.shape[0] // taps
    length = span // devices
    groups = toeplitz.shape[0]
    size = chunk // groups
    width = grad_y.shape[0]
    reach = taps - 1

    grad = grad_y[...] * long[...]
    total = columns[:, 0:1] * grad
    lane = lax.broadcasted_iota(jnp.int32, (width, SUB), 1)
    position = lax.broadcasted_iota(jnp.int32, (width, length), 1)
    sums = jnp.zeros((width, SUB), f32)
    early = jnp.zeros((width, SUB), f32)
    for s in range(taps):
        tap = jnp.sum(grad * query_taps[s], axis=1, keepdims=True)
        sums += jnp.where(lane == groups + s, tap, 0.0)
        if s:
            back = pltpu.roll(query_w[s - 1] * grad, length - s, 1)
            total += jnp.where(position < length - s, back, 0.0)
            early += jnp.where(lane >= SUB - s, back[:, length - SUB :], 0.0)
    query_out[...] = total.T
    common = sums.T[0:16]
    early_query = early.T[SUB - 16 :]

    for s in range(devices):
        at = block_at(lax.rem(me - s + devices, devices), length)
        grad_long_out[:, at] = glos[s][chunk:]
    high = grad_long_out[...]
    gg_parts = []
    subs = span // SUB
    small[...] = jnp.zeros_like(small)
    for g in range(groups):
        own = slice(g * size, (g + 1) * size)
        stack = jnp.concatenate(
            [high[own, i * length : (i + 1) * length] for i in range(devices)], axis=0
        )
        totals = [None] * devices
        for lag in range(devices):
            part = lax.dot_general(
                stack[size * lag :],
                toeplitz[g, :, lag * length : (lag + 1) * length],
                (((1,), (1,)), ((), ())),
                preferred_element_type=f32,
            )
            for j in range(devices - lag):
                term = part[size * j : size * (j + 1)]
                totals[j] = term if totals[j] is None else totals[j] + term
        gg_parts.append(jnp.concatenate(totals, axis=1))
        right = jnp.concatenate([high[own, j * SUB : (j + 1) * SUB] for j in range(subs)], axis=0)
        turned = flips[g]
        lines = []
        for lag in range(subs):
            cross = jnp.dot(
                turned[:, : size * (subs - lag)], right[size * lag :], preferred_element_type=f32
            )
            wide = jnp.concatenate([cross, jnp.zeros((SUB, SUB), f32)], axis=1)
            wide = pltpu.roll(wide, 1, 1, stride=1, stride_axis=0)
            lines.append(jnp.sum(wide, axis=0, keepdims=True))
        per = length // SUB
        for lag in range(subs):
            line = lines[lag][:, SUB:]
            if lag + 1 < subs:
                line += lines[lag + 1][:, :SUB]
            b, within = divmod(lag, per)
            small[b, g : g + 1, within * SUB : (within + 1) * SUB] = line
    grad_gated = jnp.concatenate(gg_parts, axis=0)
    grads[...] = grad_gated.astype(bf16)
    lane = lax.broadcasted_iota(jnp.int32, (chunk, SUB), 1)
    sums = jnp.zeros((chunk, SUB), f32)
    for n in range(stacked * taps):
        tap = jnp.sum(grad_gated * sum_w[n], axis=1, keepdims=True)
        sums += jnp.where(lane == groups + taps + n, tap, 0.0)
    marks[...] = jnp.zeros_like(marks)
    marks[:, 0:chunk] = sums.T
    common += pltpu.roll(marks[0:16], me * chunk, 1)
    count = (stacked + 1) * taps
    start = 2 * groups + 2 * count
    high = common.astype(bf16).astype(f32)
    for b in range(devices):
        lines = small[b, 0:groups]
        top = lines.astype(bf16).astype(f32)
        small[b, 0:groups] = top
        small[b, groups : 2 * groups] = lines - top
        small[b, 2 * groups : 2 * groups + count] = high[groups : groups + count]
        small[b, 2 * groups + count : start] = (common - high)[groups : groups + count]
        small[b, start : start + reach] = early_query[16 - reach :]
        if b == devices - 1:
            continue
        first = grad_gated[:, (b + 1) * length : (b + 1) * length + SUB]
        for i in range(stacked):
            early = jnp.zeros((chunk, SUB), f32)
            for s in range(1, taps):
                weight = early_w[i * reach + s - 1, :, b * SUB : (b + 1) * SUB]
                back = pltpu.roll(weight * first, SUB - s, 1)
                early += jnp.where(lane >= SUB - s, back, 0.0)
            marks[:, 0:chunk] = early.T
            placed = pltpu.roll(marks[SUB - 16 :], me * chunk, 1)
            at = start + (i + 1) * reach
            small[b, at : at + reach] = placed[16 - reach :]
    for s in range(devices):
        to = lax.rem(me + s, devices)
        outs[s][0:chunk] = grads[:, block_at(to, length)]
        outs[s][chunk:] = small[to].astype(bf16)


def small_sum_kernel(devices, groups, stacked, taps, *refs):
    pays, (sums, later, tiles) = refs[:devices], refs[devices:]
    me = lax.axis_index("ctx")
    width = pays[0].shape[1]
    body = width // devices
    count = stacked * taps
    start = 2 * groups + 2 * count
    reach = taps - 1
    for s in range(devices):
        tiles[lax.rem(me - s + devices, devices)] = pays[s][body:].astype(f32)
    total = tiles[0]
    for c in range(1, devices):
        total += tiles[c]
    lines = [tiles[c, 0:groups] + tiles[c, groups : 2 * groups] for c in range(devices)]
    taps_sum = total[2 * groups : 2 * groups + count] + total[2 * groups + count : start]
    for n, value in enumerate((jnp.concatenate(lines, axis=0), taps_sum)):
        if value.shape[0] < 16:
            rest = jnp.zeros((16 - value.shape[0], width), f32)
            value = jnp.concatenate([value, rest], axis=0)
        for h, half in enumerate(split_bf16(value)):
            sums[:, (2 * h + n) * width : (2 * h + n + 1) * width] = half
    last = pays[devices - 1][body:].astype(f32)
    later[...] = jnp.zeros_like(later)
    later[0, 16 - reach : 16] = last[start : start + reach]
    for i in range(1, stacked):
        later[i, 16 - reach : 16] = total[start + i * reach : start + (i + 1) * reach]


def grad_out_kernel(devices, taps, query_part, pair_w, later, *refs):
    pays, (out, gated) = refs[:devices], refs[devices:]
    me = lax.axis_index("ctx")
    stacked, rows, width = out.shape
    chunk = width // devices
    for s in range(devices):
        at = block_at(lax.rem(me - s + devices, devices), chunk)
        gated[at] = pays[s][0:chunk].astype(f32)
    for i in range(stacked):
        if i == 0:
            turned = query_part[...]
        else:
            j = (i - 1) * taps
            total = pair_w[j] * gated[...]
            for s in range(1, taps):
                total += pltpu.roll(pair_w[j + s] * gated[...], rows - s, 1)
            turned = total.T
        out[i, 0 : rows - 16] = turned[0 : rows - 16].astype(bf16)
        out[i, rows - 16 :] = (turned[rows - 16 :] + later[i]).astype(bf16)


def final_kernel(devices, scale, *refs):
    near, far, refs = refs[:devices], refs[devices : 2 * devices], refs[2 * devices :]
    mine, other, weight_out, short_out, long_out = refs
    me, core = lax.axis_index("ctx"), lax.axis_index("dp")
    rows = near[0].shape[0]
    for side, blocks in ((core, near), (1 - core, far)):
        for s in range(devices):
            at = side * devices + lax.rem(me - s + devices, devices)
            weight_out[block_at(at, rows)] = blocks[s][...].astype(f32)
    width = long_out.shape[1]
    stacked, taps, _ = short_out.shape

    def sums(n):
        pieces = []
        for ref in (mine, other):
            high = ref[:, n * width : (n + 1) * width].astype(f32)
            low = ref[:, (n + 2) * width : (n + 3) * width].astype(f32)
            pieces.append(high + low)
        return (pieces[0] + pieces[1]) * scale

    long_out[...] = sums(0)
    total = sums(1)
    for i in range(stacked):
        short_out[i] = total[i * taps : (i + 1) * taps]


def direct_device(projected, segment_ids, short_filter, long_filter, out_proj, mixed_cotangent):
    devices, parts = lax.axis_size("ctx"), lax.axis_size("tp")
    stacked, _, length, width = projected.shape
    taps = short_filter.shape[1]
    count = long_filter.shape[0]
    groups = count // devices
    chunk = width // devices
    span = length * devices
    total_cols = out_proj.shape[1]
    grad_scale = 1.0 / math.sqrt(projected.shape[1] * lax.axis_size("dp") * span)
    cotangent = mixed_cotangent[0]
    room = 16
    inputs = (projected[:, 0], long_filter, segment_ids)

    outs = on_core(
        functools.partial(pack_kernel, devices, taps - 1),
        [
            (((stacked - 1) * chunk + (2 * room if s == 1 else room), length), bf16)
            for s in range(devices)
        ],
        inputs,
        "pack",
        [
            pltpu.VMEM((stacked - 1, length, width), bf16),
            pltpu.VMEM((16, width), bf16),
            pltpu.VMEM(long_filter.shape, f32),
            pltpu.VMEM(segment_ids.shape, jnp.int32),
            pltpu.VMEM((stacked - 1, width, length), bf16),
            pltpu.VMEM((room, length), f32),
            pltpu.VMEM((room, width), f32),
            pltpu.SemaphoreType.DMA((5,)),
        ],
        whole=True,
    )
    own, *signal = scatter_chunks(outs, "ctx")
    beside = swap(cotangent, "tp", 1)
    columns, own, turned = on_core(
        prepare_kernel,
        [((width, 16), f32), (own.shape, bf16), ((stacked, width, length), bf16)],
        (after(short_filter, beside), own, inputs[0]),
        "prepare",
        [pltpu.VMEM((16, width), f32)],
    )
    signal = [own, *signal]

    conv_flops = 2 * groups * span * span * 64
    outs = on_core(
        functools.partial(conv_kernel, devices, taps),
        [((chunk, length), bf16)] * devices
        + [
            ((stacked - 1, chunk, span), f32),
            (((stacked - 1) * chunk, span), bf16),
            ((8, span), f32),
            ((groups, length, span), bf16),
        ],
        (columns, *signal),
        "conv",
        [
            pltpu.VMEM((room, span), f32),
            pltpu.VMEM((chunk, span), bf16),
            pltpu.VMEM((groups, length, span), bf16),
        ],
        flops=900_000_000,
    )
    longs, kept = outs[:devices], outs[devices:]
    seg = kept[2]
    cots = [cotangent, beside, swap(cotangent, "tp", 2), swap(beside, "tp", 2)]
    outs = on_core(
        functools.partial(grad_y_kernel, devices, parts, taps),
        [((2 * chunk, length), bf16)] * devices + [((width, length), f32)] * 2,
        (out_proj, turned, signal[1], columns, seg, *cots, *longs),
        "grad_y",
        [pltpu.VMEM((8 * taps, span), f32), pltpu.VMEM((width, length), bf16)],
        flops=2 * width * length * total_cols,
    )
    pairs, (grad_y, query_conv) = outs[:devices], outs[devices:]
    pairs = scatter_chunks(pairs, "ctx")

    pair_w, *factors = on_core(
        functools.partial(ready_kernel, devices, taps),
        [
            (((stacked - 1) * taps, width, length), f32),
            ((taps, width, length), f32),
            ((taps - 1, width, length), f32),
            ((groups, SUB, SUB), bf16),
            (((stacked - 1) * taps, chunk, span), f32),
            (((stacked - 1) * (taps - 1), chunk, (devices - 1) * SUB), f32),
        ],
        (turned, signal[1], columns, seg, *kept[:2]),
        "ready",
        [pltpu.VMEM((8 * taps, span), f32)],
    )
    query_conv = after(query_conv, factors[0])

    half = width // 2
    y, long, keep, send = on_core(
        functools.partial(weight_grad_kernel, devices, parts),
        [
            ((width, length), bf16),
            ((width, length), f32),
            ((half, total_cols), f32),
            ((half, total_cols), bf16),
        ],
        (query_conv, *cots, *pairs),
        "weight_grad",
        [pltpu.VMEM((width, total_cols), f32)],
        flops=2 * width * length * total_cols,
    )
    other = rotate(send, "dp", 1)
    kept_part, sent_part = on_core(
        mixed_part_kernel,
        [((2 * length, width), f32), ((2 * length, width), bf16)],
        (y, out_proj),
        "mixed_part",
        [pltpu.VMEM((length, total_cols), f32)],
        flops=2 * width * length * total_cols,
    )
    keep = after(keep, kept_part)
    rows = half // devices
    sums = on_core(
        functools.partial(core_sum_kernel, devices),
        [((rows, total_cols), f32)] + [((rows, total_cols), bf16)] * (devices - 1),
        (keep, other),
        "core_sum",
        [pltpu.VMEM((half, total_cols), f32)],
    )
    first_sums = sums[1]
    parts_out = scatter_chunks(sums, "ctx")

    outs = on_core(
        functools.partial(backward_kernel, devices, taps),
        [((chunk + 2 * room, length), bf16)] * devices + [((length, width), f32)],
        (kept[3], columns, grad_y, after(long, sums[1]), *factors, *pairs),
        "backward",
        [
            pltpu.VMEM((chunk, span), bf16),
            pltpu.VMEM((chunk, span), bf16),
            pltpu.VMEM((devices, 2 * room, length), f32),
            pltpu.VMEM((SUB, width), f32),
        ],
        flops=2 * conv_flops,
    )
    back, query_part = outs[:devices], outs[devices]
    back = scatter_chunks(back, "ctx")
    sums, later = on_core(
        functools.partial(small_sum_kernel, devices, groups, stacked, taps),
        [((16, total_cols), bf16), ((stacked, 16, width), f32)],
        back,
        "small_sum",
        [pltpu.VMEM((devices, 2 * room, width), f32)],
        flops=2_000_000_000,
    )
    (grad_projected,) = on_core(
        functools.partial(grad_out_kernel, devices, taps),
        [((stacked, length, width), bf16)],
        (query_part, pair_w, later, *back),
        "grad_out",
        [pltpu.VMEM((width, length), f32)],
    )
    (block,) = on_core(
        functools.partial(block_sum_kernel, grad_scale),
        [((rows, total_cols), bf16)],
        parts_out,
        "block_sum",
        flops=2_000_000_000,
    )
    own_part, sent_part = on_core(
        mixed_pair_kernel,
        [((length, width), f32), ((length, width), bf16)],
        (after(kept_part, query_part), swap(after(sent_part, first_sums), "tp", 1)),
        "mixed_pair",
    )
    come_part = swap(sent_part, "tp", 2)
    (mixed,) = on_core(
        mixed_sum_kernel, [((length, width), bf16)], (own_part, come_part), "mixed_sum"
    )

    near = spread(block, "ctx")
    other_sums = rotate(sums, "dp", 1)
    near[1] = after(near[1], (grad_projected, come_part, other_sums))
    far = [rotate(piece, "dp", 1) for piece in near]
    grad_out_proj, grad_short, grad_long = on_core(
        functools.partial(final_kernel, devices, grad_scale),
        [((width, total_cols), f32), (short_filter.shape, f32), ((count, length), f32)],
        (*near, *far, sums, other_sums),
        "final",
    )
    return (mixed[None], grad_projected[:, None], grad_short, grad_long, grad_out_proj)


def direct_fits(mesh, projected, short_filter, long_filter, out_proj):
    devices = mesh.shape["ctx"]
    length = projected.shape[2] // devices
    width = projected.shape[3] // mesh.shape["tp"]
    groups = long_filter.shape[0] // mesh.shape["tp"]
    stacked, taps = short_filter.shape[:2]
    return (
        mesh.shape["dp"] == 2
        and mesh.shape["tp"] == 4
        and projected.shape[1] == 2
        and stacked == 3
        and length == width
        and length % SUB == 0
        and groups % devices == 0
        and groups == 16
        and (width // devices) % 16 == 0
        and width // devices <= SUB
        and (width // groups) == 16
        and 2 * groups // devices + 2 <= 16
        and out_proj.shape[1] == 4 * width
        and stacked * (taps - 1) <= 16
        and groups // devices + stacked * taps <= 16
        and 2 * (groups // devices) + 2 * stacked * taps + stacked * (taps - 1) <= 32
    )


def solution(mesh):
    in_specs = (
        P(None, "dp", "ctx", "tp"),
        P("dp", "ctx"),
        P(None, None, "tp"),
        P("tp", "ctx"),
        P("tp", None),
        P("dp", "ctx", "tp"),
    )
    out_specs = (
        P("dp", "ctx", "tp"),
        P(None, "dp", "ctx", "tp"),
        P(None, None, "tp"),
        P("tp", "ctx"),
        P("tp", None),
    )

    def layer(projected, segment_ids, short_filter, long_filter, out_proj, mixed_cotangent):
        fits = direct_fits(mesh, projected, short_filter, long_filter, out_proj)
        return jax.shard_map(
            direct_device if fits else spectral_device,
            mesh=mesh,
            in_specs=in_specs,
            out_specs=out_specs,
            check_vma=False,
        )(projected, segment_ids, short_filter, long_filter, out_proj, mixed_cotangent)

    return layer
```
